32 devices in a mesh: member: 4 (over y, core), space: 8 (over z, x).
Axes of the slice: x: 2, y: 2, z: 4, core: 2. Of those that a mesh axis runs over, the one named last changes fastest.
Arguments:
- states: bfloat16 [4, 73, 392, 720], P('member', None, 'space'), may hold values from -6 to 6
- observed: bfloat16 [73, 392, 720], P(None, 'space'), may hold values from -6 to 6
- band_rows: int32 [8], replicated, may hold values from 1 to 49, 361 in all
- encoder_weight: bfloat16 [73, 128], replicated, may hold values from -0.75 to 0.75
- mixing_weight: bfloat16 [128, 128], replicated, may hold values from -0.5 to 0.5
- degree_gain: float32 [368, 128], replicated, may hold values from 0.25 to 2
- decoder_weight: bfloat16 [128, 73], replicated, may hold values from -0.5 to 0.5
Outputs:
- prediction: bfloat16 [4, 73, 392, 720], P('member', None, 'space')
- state_grad: bfloat16 [4, 73, 392, 720], P('member', None, 'space')
The draws below stay inside these ranges and needn't reach their ends.
Inputs may be any that keep to these rules, and one draw needn't show every extreme that they name: Band d holds the next band_rows[d] latitudes, from the north pole southward, in the first rows of the d-th block of 49 rows; the remaining rows of a block are padding, ignored in states and observed. The bands' rows sum to 361, and some band has exactly 49 rows.
All inputs are finite; a program needn't handle non-finite values.
Results may differ from the reference program's by a relative error of at most 0.014.
Values may be sent and summed in bfloat16 or wider, within the bound.
No kernel may reach another device: no remote copies, remote signals or barrier semaphores. Data moves between devices by JAX's collectives and lax.ppermute only.
A program may use at most 256 MiB of HBM per device.

```python
import math
import jax
import jax.numpy as jnp
import numpy as np
from jax import lax

NLAT = 361
NLON = 720
LMAX = 360
CH = 128
FIELDS = 73
MEMBERS = 4
BAND = 49
ROWS = 392
MPAD = 368
DEG = 368
N_SPACE = 8


def block_scale(stream_key, extent, shards, least, largest):
    gain = 1.0
    for dim, shards_of in shards:
        draws = jax.random.uniform(jax.random.fold_in(jax.random.fold_in(stream_key, 6), dim), (shards_of,), jnp.float32, least / len(shards), largest / len(shards))
        gain = gain * jnp.repeat(jnp.exp(draws), extent[dim] // shards_of).reshape((-1,) + (1,) * (len(extent) - 1 - dim))
    return gain


def profile(count, total, most, lean):
    portions = [(1 << 20) // math.isqrt(standing ** lean) + 1 for standing in range(2, count + 1)]
    spare, holding = total - most - (count - 1), [1] * (count - 1)
    while spare > 0:
        movable = [i for i in range(count - 1) if holding[i] < most]
        pool, budget = sum([portions[i] for i in movable]), spare
        for i in movable:
            extra = min(most - holding[i], max(1, budget * portions[i] // pool), spare)
            holding[i] = holding[i] + extra
            spare = spare - extra
    return np.array([most] + holding)


def uneven_parts(own_key, count, total, most, skew):
    if count == 2:
        one = jax.random.randint(own_key, (), max(1, total - most), min(most, total - 1) + 1)
        return jnp.stack([one, total - one])
    lengths = jnp.asarray(profile(count, total, most, skew), jnp.int32)
    twos = (count - 1) // 2
    source_of, taker = lengths[1:1 + 2 * twos:2], lengths[2:2 + 2 * twos:2]
    slack = jnp.minimum(source_of - 1, most - taker)
    shifted = jax.random.randint(jax.random.fold_in(own_key, 1), (twos,), 0, 1 << 20) % (slack + 1)
    lengths = lengths.at[1:1 + 2 * twos:2].set(source_of - shifted).at[2:2 + 2 * twos:2].set(taker + shifted)
    return lengths[jax.random.permutation(jax.random.fold_in(own_key, 2), count)]


def centred(stream_key, extent, scale, most, cuts=(), held_as=jnp.bfloat16):
    values = jax.random.normal(stream_key, extent, jnp.float32) * scale
    if len(cuts) > 0:
        values = block_scale(stream_key, extent, cuts, -0.22, 0.18) * values
    return jnp.clip(values, min=-most, max=most).astype(held_as)


def setup_inputs(seed: int = 0) -> dict:
    keys = jax.random.split(jax.random.key(seed), 8)
    states = centred(keys[0], (MEMBERS, FIELDS, ROWS, NLON), 1.0, 6.0, ((0, 4), (2, 8)))
    observed = centred(keys[1], (FIELDS, ROWS, NLON), 1.0, 6.0, ((1, 8),))
    band_rows = uneven_parts(keys[2], N_SPACE, NLAT, BAND, 1).astype(jnp.int32)
    encoder_weight = centred(keys[3], (FIELDS, CH), FIELDS ** -0.5, 0.75)
    mixing_weight = centred(keys[4], (CH, CH), CH ** -0.5, 0.5)
    degree_gain = jnp.clip(jnp.exp(jax.random.uniform(keys[5], (DEG, CH), jnp.float32, math.log(0.25), math.log(2.0))), 0.25, 2.0)
    decoder_weight = centred(keys[6], (CH, FIELDS), CH ** -0.5, 0.5)
    return dict(states=states, observed=observed, band_rows=band_rows, encoder_weight=encoder_weight, mixing_weight=mixing_weight, degree_gain=degree_gain, decoder_weight=decoder_weight)


EPSILON = 1e-05

def row_geometry(band_rows, band_len, lat_count):
    band_count = band_rows.shape[0]
    row_index = jnp.arange(band_count * band_len, dtype=jnp.int32)
    row_owner = row_index // band_len
    offset = row_index - row_owner * band_len
    starts = jnp.cumsum(band_rows) - band_rows
    owner_hot = (row_owner[:, None] == jnp.arange(band_count, dtype=jnp.int32)[None, :]).astype(jnp.int32)
    first_lat = lax.optimization_barrier(jnp.sum(owner_hot * starts[None, :], axis=1))
    length = lax.optimization_barrier(jnp.sum(owner_hot * band_rows[None, :], axis=1))
    live_rows = offset < length
    latitude = jnp.minimum(first_lat + offset, lat_count - 1)
    colatitude = latitude.astype(jnp.float32) * (math.pi / (lat_count - 1))
    return (live_rows, jnp.cos(colatitude), jnp.sin(colatitude))

def diagonal_logs(order_count):
    kvalues = jnp.arange(order_count, dtype=jnp.float32)
    increments = jnp.where(kvalues >= 1.0, 0.5 * jnp.log((2.0 * kvalues + 1.0) / jnp.maximum(2.0 * kvalues, 1.0)), 0.0)
    return 0.5 * math.log(0.5) + jnp.cumsum(increments)

def legendre(orders, log_diag, cosines, sines, top_degree, degrees):
    order_f = orders.astype(jnp.float32)[:, None]
    log_start = log_diag[:, None] + order_f * jnp.log(jnp.maximum(sines, 1e-30))[None, :]
    empty_rows = jnp.zeros((orders.shape[0], cosines.shape[0]), jnp.float32)
    cosine_row = cosines[None, :]

    def recur_block(state_in, block_start):
        first, second, log_scale = state_in
        stacked = []
        for position in range(16):
            degree = block_start + position
            degree_f = degree.astype(jnp.float32)
            past_onset = degree > orders[:, None]
            at_onset = degree == orders[:, None]
            factor_up = jnp.sqrt((4.0 * degree_f * degree_f - 1.0) / jnp.maximum(degree_f * degree_f - order_f * order_f, 1.0))
            factor_back = jnp.sqrt(jnp.maximum((degree_f - 1.0) * (degree_f - 1.0) - order_f * order_f, 0.0) / jnp.maximum(4.0 * (degree_f - 1.0) * (degree_f - 1.0) - 1.0, 1.0))
            current = jnp.where(past_onset, factor_up * (cosine_row * first - factor_back * second), jnp.where(at_onset, 1.0, 0.0))
            magnitude = jnp.maximum(jnp.abs(current), jnp.abs(first))
            factor = jnp.where(magnitude > 1.0, magnitude, 1.0)
            current = current / factor
            previous = first / factor
            log_scale = log_scale + jnp.log(factor)
            keep_mask = (past_onset | at_onset) & (degree <= top_degree)
            stacked.append(jnp.where(keep_mask, current * jnp.exp(log_scale), 0.0))
            second = previous
            first = current
        return ((first, second, log_scale), jnp.stack(stacked))
    block_starts = jnp.arange(degrees // 16, dtype=jnp.int32) * 16
    final_state, legendre_table = lax.scan(recur_block, (empty_rows, empty_rows, log_start), block_starts)
    return legendre_table.reshape(degrees, orders.shape[0], cosines.shape[0])

def transforms(lon_count, order_count, top_degree):
    lon_index = jnp.arange(lon_count, dtype=jnp.int32)
    order_index = jnp.arange(order_count, dtype=jnp.int32)
    angle_table = (order_index[:, None] * lon_index[None, :] % lon_count).astype(jnp.float32) * (2.0 * math.pi / lon_count)
    live_order = (order_index <= top_degree)[:, None]
    cosines = jnp.where(live_order, jnp.cos(angle_table), 0.0)
    sines = jnp.where(live_order, jnp.sin(angle_table), 0.0)
    weight = jnp.where((order_index == 0) | (2 * order_index == lon_count), 1.0, 2.0)[:, None]
    forward = jnp.transpose(jnp.stack([cosines, -sines]), (2, 0, 1)) / lon_count
    inverse = jnp.stack([weight * cosines, -weight * sines])
    return (forward.astype(jnp.bfloat16), inverse.astype(jnp.bfloat16))

def gelu_slope(values):
    return 0.5 * (1.0 + lax.erf(values * (1.0 / math.sqrt(2.0)))) + values * jnp.exp(-0.5 * values * values) * (1.0 / math.sqrt(2.0 * math.pi))

def score_grad(own_fields, everyone, observed, area_weight):
    own_f = own_fields.astype(jnp.float32)
    truth_gap = own_f - observed.astype(jnp.float32)
    truth_dist = jnp.sqrt(lax.optimization_barrier(jnp.sum(truth_gap * truth_gap, axis=0, keepdims=True)) + EPSILON)

    def accumulate(running, other_member):
        member_gap = own_f - other_member.astype(jnp.float32)
        member_dist = jnp.sqrt(lax.optimization_barrier(jnp.sum(member_gap * member_gap, axis=0, keepdims=True)) + EPSILON)
        return (running + member_gap / member_dist, None)
    pair_sum, unused = lax.scan(accumulate, jnp.zeros(own_f.shape, jnp.float32), everyone)
    result = area_weight[None, :, None] * (truth_gap / truth_dist - pair_sum / everyone.shape[0])
    return result.astype(jnp.bfloat16)

def reference(states, observed, band_rows, encoder_weight, mixing_weight, degree_gain, decoder_weight):
    live_rows, cosines, sines = row_geometry(band_rows, BAND, NLAT)
    live_f = live_rows.astype(jnp.float32)
    orders = jnp.arange(MPAD, dtype=jnp.int32)
    legendre_table = legendre(orders, diagonal_logs(MPAD), cosines, sines, LMAX, DEG)
    quad_weight = live_f * sines * (math.pi / (NLAT - 1))
    legendre_forward = (legendre_table * quad_weight[None, None, :]).astype(jnp.bfloat16).astype(jnp.float32)
    legendre_inverse = (legendre_table * live_f[None, None, :]).astype(jnp.bfloat16).astype(jnp.float32)
    fwd_table, inv_table = transforms(NLON, MPAD, LMAX)
    fwd_table = fwd_table.astype(jnp.float32)
    inv_table = inv_table.astype(jnp.float32)
    area_weight = 8.0 * sines * live_f
    enc_f = encoder_weight.astype(jnp.float32)
    mix_f = mixing_weight.astype(jnp.float32)
    dec_f = decoder_weight.astype(jnp.float32)

    def run_forward(member):
        hidden = (jnp.einsum('frl,fc->rlc', member.astype(jnp.float32), enc_f) * live_f[:, None, None]).astype(jnp.bfloat16)
        longitude_modes = jnp.einsum('rlc,lkm->kmrc', hidden.astype(jnp.float32), fwd_table).astype(jnp.bfloat16)
        harmonic_weights = jnp.einsum('ghqn,uhq->guhn', longitude_modes.astype(jnp.float32), legendre_forward).astype(jnp.bfloat16)
        masked_spectrum = (jnp.einsum('klmc,cd->klmd', harmonic_weights.astype(jnp.float32), mix_f) * degree_gain[None, :, None, :]).astype(jnp.bfloat16)
        rebuilt_field = jnp.einsum('pjcx,jco->pcox', masked_spectrum.astype(jnp.float32), legendre_inverse).astype(jnp.bfloat16)
        grid_field = jnp.einsum('kmrc,kml->rlc', rebuilt_field.astype(jnp.float32), inv_table)
        block_out = ((jax.nn.gelu(grid_field, approximate=False) + hidden.astype(jnp.float32)) * live_f[:, None, None]).astype(jnp.bfloat16)
        predicted = (member.astype(jnp.float32) + jnp.einsum('rlc,cf->frl', block_out.astype(jnp.float32), dec_f)) * live_f[None, :, None]
        return (grid_field, predicted.astype(jnp.bfloat16))
    prediction = lax.map(lambda member: run_forward(member)[1], states)
    score_all = lax.map(lambda own_fields: score_grad(own_fields, prediction, observed, area_weight), prediction)

    def run_backward(inputs):
        member, grad_pred = inputs
        grid_field = run_forward(member)[0]
        grad_f = grad_pred.astype(jnp.float32)
        grad_block = jnp.einsum('frl,cf->rlc', grad_f, dec_f)
        grad_field = (grad_block * gelu_slope(grid_field)).astype(jnp.bfloat16)
        rebuilt_gradient = jnp.einsum('rlc,kml->kmrc', grad_field.astype(jnp.float32), inv_table).astype(jnp.bfloat16)
        masked_gradient = jnp.einsum('ghqn,uhq->guhn', rebuilt_gradient.astype(jnp.float32), legendre_inverse)
        grad_scaled = (masked_gradient * degree_gain[None, :, None, :]).astype(jnp.bfloat16)
        harmonic_gradient = jnp.einsum('klmd,cd->klmc', grad_scaled.astype(jnp.float32), mix_f).astype(jnp.bfloat16)
        longitude_gradient = jnp.einsum('sbzv,bze->szev', harmonic_gradient.astype(jnp.float32), legendre_forward).astype(jnp.bfloat16)
        grad_spectral = jnp.einsum('kmrc,lkm->rlc', longitude_gradient.astype(jnp.float32), fwd_table)
        grad_hidden = ((grad_block + grad_spectral) * live_f[:, None, None]).astype(jnp.bfloat16)
        result = (grad_f + jnp.einsum('rlc,fc->frl', grad_hidden.astype(jnp.float32), enc_f)) * live_f[None, :, None]
        return result.astype(jnp.bfloat16)
    state_grad = lax.map(run_backward, (states, score_all))
    return (prediction, state_grad)
```

```python
import functools
import math

import jax
import jax.numpy as jnp
import ml_dtypes
import numpy as np
from jax import lax
from jax.experimental import pallas as pl
from jax.experimental.pallas import tpu as pltpu
from jax.sharding import PartitionSpec as P

NLAT = 361
LMAX = 360
EPSILON = 1e-05
GROUP = 192
SPLIT = 64
REST = 16
LANES = 128
VMEM = 60 * 1024 * 1024
BF = jnp.bfloat16
F32 = jnp.float32


def ceil_to(value, step):
    return -(-value // step) * step


class Plan:
    def __init__(self, space, band, fields, lon, channels, degrees):
        self.n, self.rows, self.fields, self.lon = space, band, fields, lon
        self.channels, self.degrees = channels, degrees
        self.all_rows = space * band
        self.fpad = SPLIT + REST
        self.live_t = -(-GROUP // space)
        self.tp = ceil_to(self.live_t, 8)
        self.tb = self.tp // 8
        self.rest_groups = -(-self.tb // 4)
        self.rows1 = ceil_to(self.tp + 8 * self.rest_groups, 16)
        self.rows2 = 2 * self.tp
        self.groups = -(-(LMAX + 1) // (space * self.live_t))
        self.rb = max(k for k in range(1, 9) if band % k == 0)
        blocks = band // self.rb
        parts = min(3, blocks)
        counts = [blocks // parts + (1 if p >= parts - blocks % parts else 0) for p in range(parts)]
        self.chunks = []
        start = 0
        for count in counts:
            self.chunks.append((start * self.rb, count * self.rb))
            start += count

    def orders(self, group):
        device = np.arange(self.n)[:, None]
        position = np.arange(self.tp)[None, :]
        order = group * self.n * self.live_t + device * self.live_t + position
        return np.where((position < self.live_t) & (order <= LMAX), order, 1 << 14)


def dft_rows(plan, group, inverse):
    order = plan.orders(group)
    live = (order <= LMAX)[..., None]
    turn = (np.where(order <= LMAX, order, 0)[..., None] * np.arange(plan.lon)) % plan.lon
    angle = turn * (2.0 * math.pi / plan.lon)
    if inverse:
        scale = np.where((order == 0) | (2 * order == plan.lon), 1.0, 2.0)[..., None]
    else:
        scale = 1.0 / plan.lon
    rows = np.stack([np.cos(angle) * scale, -np.sin(angle) * scale]) * live
    return rows.astype(ml_dtypes.bfloat16)


def params(**more):
    return pltpu.CompilerParams(vmem_limit_bytes=VMEM, **more)


def whole(shape):
    return pl.BlockSpec(shape, lambda *_: (0,) * len(shape))


def table_kernel(m_ref, start_ref, cos_ref, quad_ref, live_ref, fwd_ref, inv_ref, one, two, logs, stage):
    block = pl.program_id(1)
    lanes = fwd_ref.shape[2]
    order = m_ref[...]

    @pl.when(block == 0)
    def _():
        one[...] = jnp.zeros_like(one)
        two[...] = jnp.zeros_like(two)
        logs[...] = start_ref[...]

    ups, backs, pasts, onsets, keeps = [], [], [], [], []
    for p in range(16):
        degree = block * 16 + p
        deg = degree.astype(F32)
        ups.append(
            jnp.sqrt((4.0 * deg * deg - 1.0) / jnp.maximum(deg * deg - order * order, 1.0))
        )
        less = (deg - 1.0) * (deg - 1.0)
        backs.append(
            jnp.sqrt(
                jnp.maximum(less - order * order, 0.0) / jnp.maximum(4.0 * less - 1.0, 1.0)
            )
        )
        pasts.append(order < deg)
        onsets.append(jnp.where(order == deg, 1.0, 0.0))
        keeps.append((order <= deg) & (degree <= LMAX))
    for c in range(one.shape[1] // LANES):
        at = slice(c * LANES, (c + 1) * LANES)
        first, second, log_scale = one[:, at], two[:, at], logs[:, at]
        cosine = cos_ref[:, at]
        scale = jnp.exp(log_scale)
        for p in range(16):
            current = jnp.where(
                pasts[p], ups[p] * (cosine * first - backs[p] * second), onsets[p]
            )
            stage[c, pl.ds(p, 8, stride=16), :] = jnp.where(keeps[p], current * scale, 0.0)
            second = first
            first = current
        size = jnp.maximum(jnp.abs(first), jnp.abs(second))
        factor = jnp.where(size > 1.0, size, 1.0)
        one[:, at] = first / factor
        two[:, at] = second / factor
        logs[:, at] = log_scale + jnp.log(factor)
        width = min(LANES, lanes - c * LANES)
        out = slice(c * LANES, c * LANES + width)
        for i in range(8):
            values = stage[c, i * 16 : (i + 1) * 16, :]
            fwd_ref[i, :, out] = (values * quad_ref[:, at]).astype(BF)[:, :width]
            inv_ref[i, :, out] = (values * live_ref[:, at]).astype(BF)[:, :width]


def legendre_tables(plan, orders, log_start, cosines, quad, live):
    rows = cosines.shape[0]
    wide = ceil_to(rows, LANES)
    tp = orders.shape[0]

    def spread(row):
        return jnp.pad(row, (0, wide - rows))[None]

    order_f = jnp.broadcast_to(orders.astype(F32)[:, None], (tp, LANES))
    shape = jax.ShapeDtypeStruct((tp, plan.degrees, rows), BF)
    row_spec = pl.BlockSpec((1, wide), lambda i, j: (0, 0))
    out_spec = pl.BlockSpec((8, 16, rows), lambda i, j: (i, j, 0))
    return pl.pallas_call(
        table_kernel,
        grid=(tp // 8, plan.degrees // 16),
        in_specs=[
            pl.BlockSpec((8, LANES), lambda i, j: (i, 0)),
            pl.BlockSpec((8, wide), lambda i, j: (i, 0)),
            row_spec,
            row_spec,
            row_spec,
        ],
        out_specs=[out_spec, out_spec],
        out_shape=[shape, shape],
        scratch_shapes=[
            pltpu.VMEM((8, wide), F32),
            pltpu.VMEM((8, wide), F32),
            pltpu.VMEM((8, wide), F32),
            pltpu.VMEM((wide // LANES, 128, LANES), F32),
        ],
        compiler_params=params(),
        name="legendre_tables",
    )(order_f, jnp.pad(log_start, ((0, 0), (0, wide - rows))), spread(cosines), spread(quad), spread(live))


def analyse_kernel(plan, x_ref, dft_ref, *outs):
    lane = lax.broadcasted_iota(jnp.int32, (1, LANES), 1)
    part = lane // REST
    n, tp = plan.n, plan.tp
    for r in range(plan.rb):
        x = x_ref[r]
        head, tail = x[:SPLIT], x[SPLIT:]
        right = jnp.concatenate([head, head] + [tail] * (LANES // REST), axis=0)
        for g, out in enumerate(outs):
            cosine, sine = [
                lax.dot_general(
                    dft_ref[g, k], right, (((1,), (1,)), ((), ())), preferred_element_type=F32
                )
                for k in range(2)
            ]
            main = jnp.where(lane < SPLIT, cosine[:, :LANES], sine[:, :LANES])
            for o in range(n):
                pieces = [main[o * tp : (o + 1) * tp]]
                for group in range(plan.rest_groups):
                    rest = jnp.zeros((8, LANES), F32)
                    for i in range(min(4, plan.tb - group * 4)):
                        first = o * tp + (group * 4 + i) * 8
                        rest = jnp.where(part == 2 * i, cosine[first : first + 8, LANES:], rest)
                        rest = jnp.where(part == 2 * i + 1, sine[first : first + 8, LANES:], rest)
                    pieces.append(rest)
                spare = plan.rows1 - tp - 8 * plan.rest_groups
                if spare:
                    pieces.append(jnp.zeros((spare, LANES), F32))
                out[o, r] = jnp.concatenate(pieces, axis=0).astype(BF)


def analyse(plan, x, dft):
    shape = (plan.n, plan.rows, plan.rows1, LANES)
    out_spec = pl.BlockSpec((plan.n, plan.rb, plan.rows1, LANES), lambda i: (0, i, 0, 0))
    return pl.pallas_call(
        functools.partial(analyse_kernel, plan),
        grid=(plan.rows // plan.rb,),
        in_specs=[
            pl.BlockSpec((plan.rb, plan.fpad, plan.lon), lambda i: (i, 0, 0)),
            whole(dft.shape),
        ],
        out_specs=[out_spec] * plan.groups,
        out_shape=[jax.ShapeDtypeStruct(shape, BF)] * plan.groups,
        compiler_params=params(),
        name="analyse",
    )(x, dft)


def unpack(plan, refs, store, height):
    start = 0
    for ref in refs:
        count = ref.shape[1]
        for o in range(plan.n):
            base = o * plan.rows + start

            def step(r, unused, o=o, base=base, ref=ref):
                at = pl.multiple_of((base + r) * height, 8)
                store[pl.ds(at, height), :] = ref[o, r].astype(F32)
                return unused

            lax.fori_loop(0, count, step, 0)
        start += count


def repack(plan, refs, store, height):
    start = 0
    for ref in refs:
        count = ref.shape[1]
        for o in range(plan.n):
            base = o * plan.rows + start

            def step(r, unused, o=o, base=base, ref=ref):
                at = pl.multiple_of((base + r) * height, 8)
                ref[o, r] = store[pl.ds(at, height), :].astype(BF)
                return unused

            lax.fori_loop(0, count, step, 0)
        start += count


def rest_row(plan, t):
    block = t // 8
    return plan.tp + 8 * (block // 4) + t % 8


def spectrum_forward_kernel(plan, recv, fwd, inv, mix, gain, *refs):
    outs, zin, yout = refs[:-2], refs[-2], refs[-1]
    t = pl.program_id(0)

    @pl.when(t == 0)
    def _():
        unpack(plan, [recv], zin, plan.rows1)
        if plan.live_t < plan.tp:
            yout[...] = jnp.zeros_like(yout)

    z = jnp.concatenate(
        [
            zin[pl.ds(t, plan.all_rows, stride=plan.rows1), :],
            zin[pl.ds(rest_row(plan, t), plan.all_rows, stride=plan.rows1), :],
        ],
        axis=1,
    ).astype(BF)
    coeffs = jnp.dot(fwd[0], z, preferred_element_type=F32).astype(BF)
    filtered = (jnp.dot(coeffs, mix[0], preferred_element_type=F32) * gain[...]).astype(BF)
    y = lax.dot_general(
        inv[0], filtered, (((0,), (0,)), ((), ())), preferred_element_type=F32
    )
    for k in range(2):
        yout[pl.ds(k * plan.tp + t, plan.all_rows, stride=plan.rows2), :] = y[
            :, k * LANES : (k + 1) * LANES
        ]

    @pl.when(t == plan.live_t - 1)
    def _():
        repack(plan, outs, yout, plan.rows2)


def spectrum_backward_kernel(plan, count, *refs):
    recvs = refs[:count]
    fwd, inv, mix, gain = refs[count : count + 4]
    out, zin, yout = refs[count + 4 :]
    t = pl.program_id(0)

    @pl.when(t == 0)
    def _():
        unpack(plan, recvs, zin, plan.rows2)
        yout[...] = jnp.zeros_like(yout)

    z = jnp.concatenate(
        [
            zin[pl.ds(k * plan.tp + t, plan.all_rows, stride=plan.rows2), :]
            for k in range(2)
        ],
        axis=1,
    ).astype(BF)
    grad = (jnp.dot(inv[0], z, preferred_element_type=F32) * gain[...]).astype(BF)
    back = jnp.dot(grad, mix[0], preferred_element_type=F32).astype(BF)
    y = lax.dot_general(fwd[0], back, (((0,), (0,)), ((), ())), preferred_element_type=F32)
    yout[pl.ds(t, plan.all_rows, stride=plan.rows1), :] = y[:, :LANES]
    where = pl.ds(rest_row(plan, t), plan.all_rows, stride=plan.rows1)
    yout[where, :] = yout[where, :] + y[:, LANES:]

    @pl.when(t == plan.live_t - 1)
    def _():
        repack(plan, [out], yout, plan.rows1)


def spectrum_specs(plan, mix, gain):
    table = pl.BlockSpec((1, plan.degrees, plan.all_rows), lambda t: (t, 0, 0))
    return [table, table, pl.BlockSpec((1,) + mix.shape[1:], lambda t: (t // 8, 0, 0)), whole(gain.shape)]


def spectrum_forward(plan, recv, fwd, inv, mix, gain):
    shapes = [(plan.n, count, plan.rows2, LANES) for _, count in plan.chunks]
    return pl.pallas_call(
        functools.partial(spectrum_forward_kernel, plan),
        grid=(plan.live_t,),
        in_specs=[whole(recv.shape)] + spectrum_specs(plan, mix, gain),
        out_specs=[whole(s) for s in shapes],
        out_shape=[jax.ShapeDtypeStruct(s, BF) for s in shapes],
        scratch_shapes=[
            pltpu.VMEM((plan.all_rows * plan.rows1, LANES), F32),
            pltpu.VMEM((plan.all_rows * plan.rows2, LANES), F32),
        ],
        compiler_params=params(),
        name="spectrum_forward",
    )(recv, fwd, inv, mix, gain)


def spectrum_backward(plan, recvs, fwd, inv, mix, gain):
    shape = (plan.n, plan.rows, plan.rows1, LANES)
    return pl.pallas_call(
        functools.partial(spectrum_backward_kernel, plan, len(recvs)),
        grid=(plan.live_t,),
        in_specs=[whole(r.shape) for r in recvs] + spectrum_specs(plan, mix, gain),
        out_specs=whole(shape),
        out_shape=jax.ShapeDtypeStruct(shape, BF),
        scratch_shapes=[
            pltpu.VMEM((plan.all_rows * plan.rows2, LANES), F32),
            pltpu.VMEM((plan.all_rows * plan.rows1, LANES), F32),
        ],
        compiler_params=params(),
        name="spectrum_backward",
    )(*recvs, fwd, inv, mix, gain)


def predict_kernel(plan, first, live_ref, x_ref, idft_ref, enc_ref, dec_ref, *refs):
    recvs = refs[: plan.groups]
    pred_ref, slope_ref, left, field = refs[plan.groups :]
    c = plan.channels
    for r in range(plan.rb):
        for g, recv in enumerate(recvs):
            piece = recv[:, r].reshape(plan.n * plan.rows2, LANES)
            wide = plan.n * plan.rows2
            left[r * c : (r + 1) * c, g * wide : (g + 1) * wide] = piece.T
    field[...] = jnp.dot(left[...], idft_ref[...], preferred_element_type=F32)
    base = first + pl.program_id(0) * plan.rb

    def step(r, unused):
        live = live_ref[base + r]
        x = x_ref[r]
        u = field[pl.ds(pl.multiple_of(r * c, 8), c), :]
        hidden = (jnp.dot(enc_ref[...], x, preferred_element_type=F32) * live).astype(BF)
        phi = 0.5 + 0.5 * lax.erf(u * (1.0 / math.sqrt(2.0)))
        slope = phi + u * jnp.exp(-0.5 * u * u) * (1.0 / math.sqrt(2.0 * math.pi))
        slope_ref[r] = slope.astype(BF)
        block = ((u * phi + hidden.astype(F32)) * live).astype(BF)
        decoded = jnp.dot(dec_ref[...], block, preferred_element_type=F32)
        pred_ref[r] = ((x.astype(F32) + decoded) * live).astype(BF)
        return unused

    lax.fori_loop(0, plan.rb, step, 0)


def predict(plan, chunk, live, x, idft, enc_t, dec_t, recvs):
    first, count = chunk
    skip = first // plan.rb
    shape = (count, plan.fpad, plan.lon)
    slope_shape = (count, plan.channels, plan.lon)
    recv_spec = pl.BlockSpec((plan.n, plan.rb, plan.rows2, LANES), lambda i: (0, i, 0, 0))
    return pl.pallas_call(
        functools.partial(predict_kernel, plan, first),
        grid=(count // plan.rb,),
        in_specs=[
            pl.BlockSpec(memory_space=pltpu.SMEM),
            pl.BlockSpec((plan.rb,) + shape[1:], lambda i: (i + skip, 0, 0)),
            whole(idft.shape),
            whole(enc_t.shape),
            whole(dec_t.shape),
        ]
        + [recv_spec] * plan.groups,
        out_specs=[
            pl.BlockSpec((plan.rb,) + shape[1:], lambda i: (i, 0, 0)),
            pl.BlockSpec((plan.rb,) + slope_shape[1:], lambda i: (i, 0, 0)),
        ],
        out_shape=[jax.ShapeDtypeStruct(shape, BF), jax.ShapeDtypeStruct(slope_shape, BF)],
        scratch_shapes=[
            pltpu.VMEM((plan.rb * plan.channels, idft.shape[0]), BF),
            pltpu.VMEM((plan.rb * plan.channels, plan.lon), F32),
        ],
        compiler_params=params(),
        name="predict",
    )(live, x, idft, enc_t, dec_t, *recvs)


def score_kernel(plan, first, members, area_ref, own_ref, all_ref, obs_ref, slope_ref, idft_ref, dec_ref, *refs):
    grad_ref, outs, right = refs[0], refs[1 : 1 + plan.groups], refs[1 + plan.groups]
    c = plan.channels
    base = first + pl.program_id(0) * plan.rb

    def step(r, unused):
        area = area_ref[base + r]
        own = own_ref[r].astype(F32)
        gap = own - obs_ref[r].astype(F32)
        total = gap * lax.rsqrt(jnp.sum(gap * gap, axis=0, keepdims=True) + EPSILON)
        for e in range(members):
            gap = own - all_ref[e, r].astype(F32)
            near = lax.rsqrt(jnp.sum(gap * gap, axis=0, keepdims=True) + EPSILON)
            total = total - gap * (near * (1.0 / members))
        grad = (total * area).astype(BF)
        grad_ref[r] = grad
        block = jnp.dot(dec_ref[...], grad, preferred_element_type=F32)
        right[pl.ds(pl.multiple_of(r * c, 16), c), :] = (
            block * slope_ref[r].astype(F32)
        ).astype(BF)
        return unused

    lax.fori_loop(0, plan.rb, step, 0)
    wide = plan.n * plan.rows2
    for g, out in enumerate(outs):
        modes = lax.dot_general(
            idft_ref[g * wide : (g + 1) * wide, :],
            right[...],
            (((1,), (1,)), ((), ())),
            preferred_element_type=F32,
        ).astype(BF)
        for r in range(plan.rb):
            for o in range(plan.n):
                out[o, r] = modes[o * plan.rows2 : (o + 1) * plan.rows2, r * c : (r + 1) * c]


def score(plan, chunk, area, own, everyone, observed, slope, idft, dec):
    first, count = chunk
    skip = first // plan.rb
    members = everyone.shape[0]
    cell = (plan.rb, plan.fpad, plan.lon)
    out_shape = (plan.n, count, plan.rows2, LANES)
    here = pl.BlockSpec(cell, lambda i: (i, 0, 0))
    return pl.pallas_call(
        functools.partial(score_kernel, plan, first, members),
        grid=(count // plan.rb,),
        in_specs=[
            pl.BlockSpec(memory_space=pltpu.SMEM),
            here,
            pl.BlockSpec((members,) + cell, lambda i: (0, i, 0, 0)),
            pl.BlockSpec(cell, lambda i: (i + skip, 0, 0)),
            pl.BlockSpec((plan.rb, plan.channels, plan.lon), lambda i: (i, 0, 0)),
            whole(idft.shape),
            whole(dec.shape),
        ],
        out_specs=[here]
        + [pl.BlockSpec((plan.n, plan.rb, plan.rows2, LANES), lambda i: (0, i, 0, 0))] * plan.groups,
        out_shape=[jax.ShapeDtypeStruct((count,) + cell[1:], BF)]
        + [jax.ShapeDtypeStruct(out_shape, BF)] * plan.groups,
        scratch_shapes=[pltpu.VMEM((plan.rb * plan.channels, plan.lon), BF)],
        compiler_params=params(),
        name="score",
    )(area, own, everyone, observed, slope, idft, dec)


def finish_kernel(plan, live_ref, grad_ref, main_ref, rest_ref, through_ref, *refs):
    recvs, out_ref, left, small, field, field_small = refs[: plan.groups], *refs[plan.groups :]
    n, tp, tb = plan.n, plan.tp, plan.tb
    wide = n * tp
    for r in range(plan.rb):
        for g, recv in enumerate(recvs):
            piece = recv[:, r].astype(F32)
            main = piece[:, :tp].reshape(wide, LANES).T
            for k in range(2):
                at = (g * 2 + k) * wide
                left[r * SPLIT : (r + 1) * SPLIT, at : at + wide] = main[
                    k * SPLIT : (k + 1) * SPLIT
                ].astype(BF)
            for group in range(plan.rest_groups):
                first = tp + 8 * group
                rest = piece[:, first : first + 8].reshape(n * 8, LANES).T.astype(BF)
                for i in range(min(4, tb - 4 * group)):
                    for k in range(2):
                        at = ((g * tb + group * 4 + i) * 2 + k) * n * 8
                        part = 2 * i + k
                        small[r * REST : (r + 1) * REST, at : at + n * 8] = rest[
                            part * REST : (part + 1) * REST
                        ]
    field[...] = jnp.dot(left[...], main_ref[...], preferred_element_type=F32)
    field_small[...] = jnp.dot(small[...], rest_ref[...], preferred_element_type=F32)
    base = pl.program_id(0) * plan.rb

    def step(r, unused):
        live = live_ref[base + r]
        grad = grad_ref[r]
        through = jnp.dot(through_ref[...], grad, preferred_element_type=F32)
        spectral = jnp.concatenate(
            [
                field[pl.ds(pl.multiple_of(r * SPLIT, 8), SPLIT), :],
                field_small[pl.ds(pl.multiple_of(r * REST, 8), REST), :],
            ],
            axis=0,
        )
        out_ref[r] = ((grad.astype(F32) + through + spectral) * live).astype(BF)
        return unused

    lax.fori_loop(0, plan.rb, step, 0)


def finish(plan, live, grad, main, rest, through, recvs):
    cell = (plan.rb, plan.fpad, plan.lon)
    here = pl.BlockSpec(cell, lambda i: (i, 0, 0))
    recv_spec = pl.BlockSpec((plan.n, plan.rb, plan.rows1, LANES), lambda i: (0, i, 0, 0))
    return pl.pallas_call(
        functools.partial(finish_kernel, plan),
        grid=(plan.rows // plan.rb,),
        in_specs=[
            pl.BlockSpec(memory_space=pltpu.SMEM),
            here,
            whole(main.shape),
            whole(rest.shape),
            whole(through.shape),
        ]
        + [recv_spec] * plan.groups,
        out_specs=here,
        out_shape=jax.ShapeDtypeStruct((plan.rows, plan.fpad, plan.lon), BF),
        scratch_shapes=[
            pltpu.VMEM((plan.rb * SPLIT, main.shape[0]), BF),
            pltpu.VMEM((plan.rb * REST, rest.shape[0]), BF),
            pltpu.VMEM((plan.rb * SPLIT, plan.lon), F32),
            pltpu.VMEM((plan.rb * REST, plan.lon), F32),
        ],
        compiler_params=params(),
        name="finish",
    )(live, grad, main, rest, through, *recvs)


def row_geometry(band_rows, band_len, lat_count):
    band_count = band_rows.shape[0]
    row_index = jnp.arange(band_count * band_len, dtype=jnp.int32)
    row_owner = row_index // band_len
    offset = row_index - row_owner * band_len
    starts = jnp.cumsum(band_rows) - band_rows
    owner_hot = (row_owner[:, None] == jnp.arange(band_count, dtype=jnp.int32)[None, :]).astype(
        jnp.int32
    )
    first_lat = jnp.sum(owner_hot * starts[None, :], axis=1)
    length = jnp.sum(owner_hot * band_rows[None, :], axis=1)
    live_rows = offset < length
    latitude = jnp.minimum(first_lat + offset, lat_count - 1)
    colatitude = latitude.astype(F32) * (math.pi / (lat_count - 1))
    return (live_rows.astype(F32), jnp.cos(colatitude), jnp.sin(colatitude))


def log_diagonal(order):
    index = np.arange(1, LMAX + 1, dtype=np.float64)
    sums = np.concatenate([[0.0], np.cumsum(0.5 * np.log((2 * index + 1) / (2 * index)))])
    return (0.5 * math.log(0.5) + sums[np.minimum(order, LMAX)]).astype(np.float32)


def field_weights(plan, weight):
    c = plan.channels
    head, tail = weight[:SPLIT], jnp.pad(weight[SPLIT:], ((0, plan.fpad - plan.fields), (0, 0)))
    blocks = []
    for b in range(min(plan.tb, 4)):
        out = jnp.zeros((2 * LANES, 2 * c), F32)
        for k in range(2):
            out = out.at[k * SPLIT : (k + 1) * SPLIT, k * c : (k + 1) * c].set(head)
            first = LANES + (2 * b + k) * REST
            out = out.at[first : first + REST, k * c : (k + 1) * c].set(tail)
        blocks.append(out)
    return jnp.stack([blocks[b % 4] for b in range(plan.tb)]).astype(BF)


def on_device(
    states, observed, band_rows, encoder_weight, mixing_weight, degree_gain, decoder_weight
):
    space = lax.axis_size("space")
    me = lax.axis_index("space")
    fields, band, lon = observed.shape
    channels = encoder_weight.shape[1]
    plan = Plan(space, band, fields, lon, channels, degree_gain.shape[0])
    live, cosines, sines = row_geometry(band_rows, band, NLAT)
    quad = live * sines * (math.pi / (NLAT - 1))
    log_sines = jnp.log(jnp.maximum(sines, 1e-30))
    live_own = lax.dynamic_slice_in_dim(live, me * band, band)
    area = 8.0 * lax.dynamic_slice_in_dim(sines, me * band, band) * live_own

    pad = plan.fpad - fields
    rows = jnp.pad(jnp.transpose(states[0], (1, 0, 2)), ((0, 0), (0, pad), (0, 0)))
    truth = jnp.pad(jnp.transpose(observed, (1, 0, 2)), ((0, 0), (0, pad), (0, 0)))

    enc_f = encoder_weight.astype(F32)
    exact = lax.Precision.HIGHEST
    through_mix = jnp.dot(enc_f, mixing_weight.astype(F32), precision=exact)
    mix = field_weights(plan, through_mix)
    mix_back = jnp.transpose(mix, (0, 2, 1))
    gain = jnp.concatenate([degree_gain, degree_gain], axis=1)
    enc_t = jnp.pad(encoder_weight.T, ((0, 0), (0, pad)))
    dec_t = jnp.pad(decoder_weight.T, ((0, pad), (0, 0)))
    dec = jnp.pad(decoder_weight, ((0, 0), (0, pad)))
    through = jnp.pad(
        jnp.dot(enc_f, decoder_weight.astype(F32), precision=exact), ((0, pad), (0, pad))
    ).astype(BF)

    forward = [dft_rows(plan, g, False) for g in range(plan.groups)]
    inverse = [dft_rows(plan, g, True) for g in range(plan.groups)]
    n, tp, tb = plan.n, plan.tp, plan.tb
    dft = jnp.asarray(np.stack([f.reshape(2, n * tp, lon) for f in forward]))
    idft = jnp.asarray(
        np.concatenate([f.transpose(1, 0, 2, 3).reshape(n * 2 * tp, lon) for f in inverse])
    )
    dft_main = jnp.asarray(np.concatenate([f.reshape(2 * n * tp, lon) for f in forward]))
    dft_rest = jnp.asarray(
        np.concatenate(
            [
                f.reshape(2, n, tb, 8, lon).transpose(2, 0, 1, 3, 4).reshape(tb * 2 * n * 8, lon)
                for f in forward
            ]
        )
    )

    sent = analyse(plan, rows, dft)

    def exchange(block):
        return lax.all_to_all(block, "space", split_axis=0, concat_axis=0, tiled=True)

    tables = []
    for g in range(plan.groups):
        order_table = plan.orders(g)
        orders = lax.dynamic_index_in_dim(jnp.asarray(order_table, jnp.int32), me, keepdims=False)
        diagonal = lax.dynamic_index_in_dim(
            jnp.asarray(log_diagonal(order_table)), me, keepdims=False
        )
        start = diagonal[:, None] + orders.astype(F32)[:, None] * log_sines[None, :]
        tables.append(legendre_tables(plan, orders, start, cosines, quad, live))

    synth = []
    for g in range(plan.groups):
        spectrum = spectrum_forward(plan, exchange(sent[g]), *tables[g], mix, gain)
        synth.append([exchange(part) for part in spectrum])

    predictions, grads, returned = [], [], []
    for i, chunk in enumerate(plan.chunks):
        pred, slope = predict(
            plan, chunk, live_own, rows, idft, enc_t, dec_t, [synth[g][i] for g in range(plan.groups)]
        )
        everyone = lax.all_gather(pred[None], "member", axis=0, tiled=True)
        out = score(plan, chunk, area, pred, everyone, truth, slope, idft, dec)
        predictions.append(pred)
        grads.append(out[0])
        returned.append([exchange(part) for part in out[1:]])

    last = []
    for g in range(plan.groups):
        part = spectrum_backward(
            plan, [returned[i][g] for i in range(len(plan.chunks))], *tables[g], mix_back, gain
        )
        last.append(exchange(part))
    state_grad = finish(
        plan, live_own, jnp.concatenate(grads), dft_main, dft_rest, through, last
    )

    def outward(block):
        return jnp.transpose(block[:, :fields], (1, 0, 2))[None]

    return (outward(jnp.concatenate(predictions)), outward(state_grad))


def solution(mesh):
    in_specs = (P("member", None, "space", None), P(None, "space", None), P(), P(), P(), P(), P())
    out_specs = (P("member", None, "space", None), P("member", None, "space", None))
    return jax.shard_map(
        on_device, mesh=mesh, in_specs=in_specs, out_specs=out_specs, check_vma=False
    )
```

```python
import functools
import math

import jax
import jax.numpy as jnp
import ml_dtypes
import numpy as np
from jax import lax
from jax.experimental import pallas as pl
from jax.experimental.pallas import tpu as pltpu
from jax.sharding import PartitionSpec as P

NLAT = 361
LMAX = 360
EPSILON = 1e-05
GROUP = 192
SPLIT = 64
REST = 16
LANES = 128
NONE = 1 << 14
VMEM = 60 * 1024 * 1024
BF = jnp.bfloat16
F32 = jnp.float32


def ceil_to(value, step):
    return -(-value // step) * step


class Plan:
    def __init__(self, space, band, fields, lon, channels, degrees):
        self.n, self.rows, self.fields, self.lon = space, band, fields, lon
        self.channels, self.degrees = channels, degrees
        self.all_rows = space * band
        self.fpad = SPLIT + REST
        self.live_t = -(-GROUP // space)
        self.tp = ceil_to(self.live_t, 8)
        self.tb = self.tp // 8
        self.rest_groups = -(-self.tb // 4)
        self.rows1 = ceil_to(self.tp + 8 * self.rest_groups, 16)
        self.rows2 = 2 * self.tp
        self.low = space * self.live_t
        self.high = LMAX + 1 - self.low
        self.pairs = ceil_to(-(-self.high // 2), 8)
        self.quads = self.pairs // 4
        self.quad_pad = ceil_to(self.quads, 8)
        self.span = ceil_to(self.high + 1, 16)
        self.half = ceil_to(band, 16)
        self.half_lanes = LANES // 2
        self.rb = max(k for k in range(1, 9) if band % k == 0)
        blocks = band // self.rb
        parts = min(3, blocks)
        counts = [blocks // parts + (1 if p >= parts - blocks % parts else 0) for p in range(parts)]
        self.chunks = []
        start = 0
        for count in counts:
            self.chunks.append((start * self.rb, count * self.rb))
            start += count

    def low_orders(self):
        device = np.arange(self.n)[:, None]
        position = np.arange(self.tp)[None, :]
        return np.where(position < self.live_t, device * self.live_t + position, NONE)

    def high_orders(self):
        pair = np.arange(self.pairs)
        first = np.where(2 * pair < self.high, self.low + pair, NONE)
        second = np.where(2 * pair < self.high - 1, LMAX - pair, NONE)
        return np.stack([first, second])


def dft_rows(plan, order, inverse):
    live = (order <= LMAX)[..., None]
    turn = (np.where(order <= LMAX, order, 0)[..., None] * np.arange(plan.lon)) % plan.lon
    angle = turn * (2.0 * math.pi / plan.lon)
    if inverse:
        scale = np.where((order == 0) | (2 * order == plan.lon), 1.0, 2.0)[..., None]
    else:
        scale = 1.0 / plan.lon
    rows = np.stack([np.cos(angle) * scale, -np.sin(angle) * scale]) * live
    return rows.astype(ml_dtypes.bfloat16)


def params(**more):
    return pltpu.CompilerParams(vmem_limit_bytes=VMEM, **more)


def whole(shape):
    return pl.BlockSpec(shape, lambda *_: (0,) * len(shape))


def table_kernel(m_ref, shift_ref, start_ref, cos_ref, quad_ref, live_ref, fwd_ref, inv_ref, one, two, logs, stage):
    block = pl.program_id(1)
    lanes = fwd_ref.shape[2]
    order, shift = m_ref[...], shift_ref[...]

    @pl.when(block == 0)
    def _():
        one[...] = jnp.zeros_like(one)
        two[...] = jnp.zeros_like(two)
        logs[...] = start_ref[...]

    ups, backs, pasts, onsets, keeps = [], [], [], [], []
    for p in range(16):
        deg = shift + (block * 16 + p).astype(F32)
        ups.append(
            jnp.sqrt((4.0 * deg * deg - 1.0) / jnp.maximum(deg * deg - order * order, 1.0))
        )
        less = (deg - 1.0) * (deg - 1.0)
        backs.append(
            jnp.sqrt(
                jnp.maximum(less - order * order, 0.0) / jnp.maximum(4.0 * less - 1.0, 1.0)
            )
        )
        pasts.append(order < deg)
        onsets.append(jnp.where(order == deg, 1.0, 0.0))
        keeps.append((order <= deg) & (deg <= LMAX))
    for c in range(one.shape[1] // LANES):
        at = slice(c * LANES, (c + 1) * LANES)
        first, second, log_scale = one[:, at], two[:, at], logs[:, at]
        cosine = cos_ref[:, at]
        scale = jnp.exp(log_scale)
        for p in range(16):
            current = jnp.where(
                pasts[p], ups[p] * (cosine * first - backs[p] * second), onsets[p]
            )
            stage[c, pl.ds(p, 8, stride=16), :] = jnp.where(keeps[p], current * scale, 0.0)
            second = first
            first = current
        size = jnp.maximum(jnp.abs(first), jnp.abs(second))
        factor = jnp.where(size > 1.0, size, 1.0)
        one[:, at] = first / factor
        two[:, at] = second / factor
        logs[:, at] = log_scale + jnp.log(factor)
        width = min(LANES, lanes - c * LANES)
        out = slice(c * LANES, c * LANES + width)
        for i in range(8):
            values = stage[c, i * 16 : (i + 1) * 16, :]
            fwd_ref[i, :, out] = (values * quad_ref[:, at]).astype(BF)[:, :width]
            inv_ref[i, :, out] = (values * live_ref[:, at]).astype(BF)[:, :width]


def legendre_tables(orders, shift, log_start, cosines, quad, live, degrees):
    rows = cosines.shape[0]
    wide = ceil_to(rows, LANES)
    tp = orders.shape[0]

    def spread(row):
        return jnp.pad(row, (0, wide - rows))[None]

    shape = jax.ShapeDtypeStruct((tp, degrees, rows), BF)
    row_spec = pl.BlockSpec((1, wide), lambda i, j: (0, 0))
    lane_spec = pl.BlockSpec((8, LANES), lambda i, j: (i, 0))
    out_spec = pl.BlockSpec((8, 16, rows), lambda i, j: (i, j, 0))
    return pl.pallas_call(
        table_kernel,
        grid=(tp // 8, degrees // 16),
        in_specs=[
            lane_spec,
            lane_spec,
            pl.BlockSpec((8, wide), lambda i, j: (i, 0)),
            row_spec,
            row_spec,
            row_spec,
        ],
        out_specs=[out_spec, out_spec],
        out_shape=[shape, shape],
        scratch_shapes=[
            pltpu.VMEM((8, wide), F32),
            pltpu.VMEM((8, wide), F32),
            pltpu.VMEM((8, wide), F32),
            pltpu.VMEM((wide // LANES, 128, LANES), F32),
        ],
        compiler_params=params(),
        name="legendre_tables",
    )(
        orders.astype(F32),
        shift.astype(F32),
        jnp.pad(log_start, ((0, 0), (0, wide - rows))),
        spread(cosines),
        spread(quad),
        spread(live),
    )


def analyse_kernel(plan, x_ref, low_ref, high_ref, out, out_high):
    lane = lax.broadcasted_iota(jnp.int32, (1, LANES), 1)
    part = lane // REST
    n, tp = plan.n, plan.tp
    for r in range(plan.rb):
        x = x_ref[r]
        head, tail = x[:SPLIT], x[SPLIT:]
        right = jnp.concatenate([head, head] + [tail] * (LANES // REST), axis=0)

        def modes(dft_ref):
            return [
                lax.dot_general(
                    dft_ref[k], right, (((1,), (1,)), ((), ())), preferred_element_type=F32
                )
                for k in range(2)
            ]

        cosine, sine = modes(low_ref)
        main = jnp.where(lane < SPLIT, cosine[:, :LANES], sine[:, :LANES])
        for o in range(n):
            pieces = [main[o * tp : (o + 1) * tp]]
            for group in range(plan.rest_groups):
                rest = jnp.zeros((8, LANES), F32)
                for i in range(min(4, plan.tb - group * 4)):
                    first = o * tp + (group * 4 + i) * 8
                    rest = jnp.where(part == 2 * i, cosine[first : first + 8, LANES:], rest)
                    rest = jnp.where(part == 2 * i + 1, sine[first : first + 8, LANES:], rest)
                pieces.append(rest)
            spare = plan.rows1 - tp - 8 * plan.rest_groups
            if spare:
                pieces.append(jnp.zeros((spare, LANES), F32))
            out[o, r] = jnp.concatenate(pieces, axis=0).astype(BF)
        cosine, sine = modes(high_ref)
        main = jnp.where(lane < SPLIT, cosine[:, :LANES], sine[:, :LANES])
        rest = jnp.where(part % 2 == 0, cosine[:, LANES:], sine[:, LANES:])
        out_high[r] = jnp.concatenate([main, rest], axis=1).astype(BF)


def analyse(plan, x, low, high):
    shape = (plan.n, plan.rows, plan.rows1, LANES)
    high_shape = (plan.rows, 2 * plan.pairs, 2 * LANES)
    return pl.pallas_call(
        functools.partial(analyse_kernel, plan),
        grid=(plan.rows // plan.rb,),
        in_specs=[
            pl.BlockSpec((plan.rb, plan.fpad, plan.lon), lambda i: (i, 0, 0)),
            whole(low.shape),
            whole(high.shape),
        ],
        out_specs=[
            pl.BlockSpec((plan.n, plan.rb, plan.rows1, LANES), lambda i: (0, i, 0, 0)),
            pl.BlockSpec((plan.rb,) + high_shape[1:], lambda i: (i, 0, 0)),
        ],
        out_shape=[jax.ShapeDtypeStruct(shape, BF), jax.ShapeDtypeStruct(high_shape, BF)],
        compiler_params=params(),
        name="analyse",
    )(x, low, high)


def unpack(plan, refs, store, height):
    start = 0
    for ref in refs:
        count = ref.shape[1]
        for o in range(plan.n):
            base = o * plan.rows + start

            def step(r, unused, o=o, base=base, ref=ref):
                at = pl.multiple_of((base + r) * height, 8)
                store[pl.ds(at, height), :] = ref[o, r].astype(F32)
                return unused

            lax.fori_loop(0, count, step, 0)
        start += count


def repack(plan, refs, store, height):
    start = 0
    for ref in refs:
        count = ref.shape[1]
        for o in range(plan.n):
            base = o * plan.rows + start

            def step(r, unused, o=o, base=base, ref=ref):
                at = pl.multiple_of((base + r) * height, 8)
                ref[o, r] = store[pl.ds(at, height), :].astype(BF)
                return unused

            lax.fori_loop(0, count, step, 0)
        start += count


def rest_row(plan, t):
    block = t // 8
    return plan.tp + 8 * (block // 4) + t % 8


def spectrum_forward_kernel(plan, recv, fwd, inv, mix, gain, *refs):
    outs, zin, yout = refs[:-2], refs[-2], refs[-1]
    t = pl.program_id(0)

    @pl.when(t == 0)
    def _():
        unpack(plan, [recv], zin, plan.rows1)
        if plan.live_t < plan.tp:
            yout[...] = jnp.zeros_like(yout)

    z = jnp.concatenate(
        [
            zin[pl.ds(t, plan.all_rows, stride=plan.rows1), :],
            zin[pl.ds(rest_row(plan, t), plan.all_rows, stride=plan.rows1), :],
        ],
        axis=1,
    ).astype(BF)
    coeffs = jnp.dot(fwd[0], z, preferred_element_type=F32).astype(BF)
    filtered = (jnp.dot(coeffs, mix[0], preferred_element_type=F32) * gain[...]).astype(BF)
    y = lax.dot_general(
        inv[0], filtered, (((0,), (0,)), ((), ())), preferred_element_type=F32
    )
    for k in range(2):
        yout[pl.ds(k * plan.tp + t, plan.all_rows, stride=plan.rows2), :] = y[
            :, k * LANES : (k + 1) * LANES
        ]

    @pl.when(t == plan.live_t - 1)
    def _():
        repack(plan, outs, yout, plan.rows2)


def spectrum_backward_kernel(plan, count, *refs):
    recvs = refs[:count]
    fwd, inv, mix, gain = refs[count : count + 4]
    out, zin, yout = refs[count + 4 :]
    t = pl.program_id(0)

    @pl.when(t == 0)
    def _():
        unpack(plan, recvs, zin, plan.rows2)
        yout[...] = jnp.zeros_like(yout)

    z = jnp.concatenate(
        [
            zin[pl.ds(k * plan.tp + t, plan.all_rows, stride=plan.rows2), :]
            for k in range(2)
        ],
        axis=1,
    ).astype(BF)
    grad = (jnp.dot(inv[0], z, preferred_element_type=F32) * gain[...]).astype(BF)
    back = jnp.dot(grad, mix[0], preferred_element_type=F32).astype(BF)
    y = lax.dot_general(fwd[0], back, (((0,), (0,)), ((), ())), preferred_element_type=F32)
    yout[pl.ds(t, plan.all_rows, stride=plan.rows1), :] = y[:, :LANES]
    where = pl.ds(rest_row(plan, t), plan.all_rows, stride=plan.rows1)
    yout[where, :] = yout[where, :] + y[:, LANES:]

    @pl.when(t == plan.live_t - 1)
    def _():
        repack(plan, [out], yout, plan.rows1)


def spectrum_specs(plan, mix, gain):
    table = pl.BlockSpec((1, plan.degrees, plan.all_rows), lambda t: (t, 0, 0))
    return [table, table, pl.BlockSpec((1,) + mix.shape[1:], lambda t: ((t // 8) % 4, 0, 0)), whole(gain.shape)]


def spectrum_forward(plan, recv, fwd, inv, mix, gain):
    shapes = [(plan.n, count, plan.rows2, LANES) for _, count in plan.chunks]
    return pl.pallas_call(
        functools.partial(spectrum_forward_kernel, plan),
        grid=(plan.live_t,),
        in_specs=[whole(recv.shape)] + spectrum_specs(plan, mix, gain),
        out_specs=[whole(s) for s in shapes],
        out_shape=[jax.ShapeDtypeStruct(s, BF) for s in shapes],
        scratch_shapes=[
            pltpu.VMEM((plan.all_rows * plan.rows1, LANES), F32),
            pltpu.VMEM((plan.all_rows * plan.rows2, LANES), F32),
        ],
        compiler_params=params(),
        name="spectrum_forward",
    )(recv, fwd, inv, mix, gain)


def spectrum_backward(plan, recvs, fwd, inv, mix, gain):
    shape = (plan.n, plan.rows, plan.rows1, LANES)
    return pl.pallas_call(
        functools.partial(spectrum_backward_kernel, plan, len(recvs)),
        grid=(plan.live_t,),
        in_specs=[whole(r.shape) for r in recvs] + spectrum_specs(plan, mix, gain),
        out_specs=whole(shape),
        out_shape=jax.ShapeDtypeStruct(shape, BF),
        scratch_shapes=[
            pltpu.VMEM((plan.all_rows * plan.rows2, LANES), F32),
            pltpu.VMEM((plan.all_rows * plan.rows1, LANES), F32),
        ],
        compiler_params=params(),
        name="spectrum_backward",
    )(*recvs, fwd, inv, mix, gain)


def pair_gain(plan, pair, gain):
    row = lax.broadcasted_iota(jnp.int32, (plan.span, 1), 0)
    first, second = plan.low + pair, plan.low - 1
    first_at = pl.multiple_of(first // 8 * 8, 8)
    one = jnp.where(
        row < plan.high - pair,
        gain[first % 8, pl.ds(first_at, plan.span), :],
        gain[second % 8, pl.ds(second // 8 * 8, plan.span), :],
    )
    return jnp.concatenate([one, one], axis=1)


def load_rows(plan, refs, store, height, wide):
    start = 0
    for ref in refs:

        def step(r, unused, start=start, ref=ref):
            at = pl.multiple_of((start + r) * height, 8)
            for w in range(wide):
                store[w, pl.ds(at, height), :] = ref[r, :, w * LANES : (w + 1) * LANES].astype(F32)
            return unused

        lax.fori_loop(0, ref.shape[0], step, 0)
        start += ref.shape[0]

    def clear(r, unused):
        at = pl.multiple_of(r * height, 8)
        for w in range(wide):
            store[w, pl.ds(at, height), :] = jnp.zeros((height, LANES), F32)
        return unused

    lax.fori_loop(start, plan.half_lanes, clear, 0)


def high_partial_kernel(plan, zonal, fwd, out, zin):
    quad = pl.program_id(0)
    block = lax.broadcasted_iota(jnp.int32, (1, LANES), 1) // (2 * REST)

    @pl.when(quad == 0)
    def _():
        load_rows(plan, [zonal], zin, 2 * plan.pairs, 2)

    rest = jnp.zeros((plan.span, LANES), F32)
    for i in range(4):
        pair = quad * 4 + i
        z = jnp.concatenate(
            [
                jnp.concatenate(
                    [
                        zin[w, pl.ds(s * plan.pairs + pair, plan.half_lanes, stride=2 * plan.pairs), :]
                        for s in range(2)
                    ],
                    axis=0,
                )
                for w in range(2)
            ],
            axis=1,
        ).astype(BF)
        coeffs = jnp.dot(fwd[i], z, preferred_element_type=F32)
        out[0, i] = coeffs[:, :LANES].astype(BF)
        rest = rest + jnp.where(block == i, coeffs[:, LANES:], 0.0)
    out[0, 4] = rest.astype(BF)


def high_synthesis_kernel(plan, coeffs, inv, mix, gain, out, yout):
    quad = pl.program_id(0)
    height = 4 * plan.pairs
    for i in range(4):
        pair = quad * 4 + i
        both = jnp.concatenate([coeffs[0, i], coeffs[0, 4]], axis=1)
        filtered = jnp.dot(both, mix[i], preferred_element_type=F32) * pair_gain(plan, pair, gain)
        y = lax.dot_general(
            inv[i], filtered.astype(BF), (((0,), (0,)), ((), ())), preferred_element_type=F32
        )
        for k in range(2):
            for s in range(2):
                yout[pl.ds((2 * k + s) * plan.pairs + pair, plan.half_lanes, stride=height), :] = y[
                    s * plan.half_lanes : (s + 1) * plan.half_lanes, k * LANES : (k + 1) * LANES
                ]

    @pl.when(quad == plan.quads - 1)
    def _():
        def step(r, unused):
            out[r] = yout[pl.ds(pl.multiple_of(r * height, 8), height), :].astype(BF)
            return unused

        lax.fori_loop(0, plan.rows, step, 0)


def high_adjoint_kernel(plan, count, *refs):
    grads, (inv, mix, gain, out, zin) = refs[:count], refs[count:]
    quad = pl.program_id(0)
    height = 4 * plan.pairs

    @pl.when(quad == 0)
    def _():
        load_rows(plan, grads, zin, height, 1)

    rest = jnp.zeros((plan.span, LANES), F32)
    for i in range(4):
        pair = quad * 4 + i
        z = jnp.concatenate(
            [
                jnp.concatenate(
                    [
                        zin[0, pl.ds((2 * k + s) * plan.pairs + pair, plan.half_lanes, stride=height), :]
                        for s in range(2)
                    ],
                    axis=0,
                )
                for k in range(2)
            ],
            axis=1,
        ).astype(BF)
        grad = jnp.dot(inv[i], z, preferred_element_type=F32) * pair_gain(plan, pair, gain)
        back = jnp.dot(grad.astype(BF), mix[i], preferred_element_type=F32)
        out[0, i] = back[:, :LANES].astype(BF)
        rest = rest + back[:, LANES:]
    out[0, 4] = rest.astype(BF)


def high_zonal_kernel(plan, grads, fwd, out, yout):
    quad = pl.program_id(0)
    height = 2 * plan.pairs + 2 * plan.quad_pad
    block = lax.broadcasted_iota(jnp.int32, (1, LANES), 1) // (2 * REST)

    if plan.quad_pad > plan.quads:

        @pl.when(quad == 0)
        def _():
            yout[...] = jnp.zeros_like(yout)

    rest = jnp.zeros((LANES, LANES), F32)
    for i in range(4):
        pair = quad * 4 + i
        both = jnp.concatenate([grads[0, i], grads[0, 4]], axis=1)
        y = lax.dot_general(
            fwd[i], both, (((0,), (0,)), ((), ())), preferred_element_type=F32
        )
        for s in range(2):
            yout[pl.ds(s * plan.pairs + pair, plan.half_lanes, stride=height), :] = y[
                s * plan.half_lanes : (s + 1) * plan.half_lanes, :LANES
            ]
        rest = rest + jnp.where(block == i, y[:, LANES:], 0.0)
    for s in range(2):
        row = 2 * plan.pairs + s * plan.quad_pad + quad
        yout[pl.ds(row, plan.half_lanes, stride=height), :] = rest[
            s * plan.half_lanes : (s + 1) * plan.half_lanes
        ]

    @pl.when(quad == plan.quads - 1)
    def _():
        def step(r, unused):
            out[r] = yout[pl.ds(pl.multiple_of(r * height, 8), height), :].astype(BF)
            return unused

        lax.fori_loop(0, plan.rows, step, 0)


def high_call(plan, kernel, name, whole_in, blocked, fixed, out_shape, out_whole, scratch):
    def quad_spec(array):
        size = array.shape[0] // plan.quads
        rest = array.shape[1:]
        return pl.BlockSpec((size,) + rest, lambda q: (q,) + (0,) * len(rest))

    return pl.pallas_call(
        kernel,
        grid=(plan.quads,),
        in_specs=[whole(a.shape) for a in whole_in]
        + [quad_spec(a) for a in blocked]
        + [whole(a.shape) for a in fixed],
        out_specs=whole(out_shape) if out_whole else quad_spec(jax.ShapeDtypeStruct(out_shape, BF)),
        out_shape=jax.ShapeDtypeStruct(out_shape, BF),
        scratch_shapes=[pltpu.VMEM(scratch, F32)],
        compiler_params=params(),
        name=name,
    )(*whole_in, *blocked, *fixed)


def high_partial(plan, zonal, fwd):
    return high_call(
        plan, functools.partial(high_partial_kernel, plan), "high_partial", [zonal], [fwd], [],
        (plan.quads, 5, plan.span, LANES), False, (2, plan.half_lanes * 2 * plan.pairs, LANES),
    )


def high_synthesis(plan, coeffs, inv, mix, gain):
    return high_call(
        plan, functools.partial(high_synthesis_kernel, plan), "high_synthesis", [], [coeffs, inv],
        [mix, gain], (plan.rows, 4 * plan.pairs, LANES), True,
        (plan.half_lanes * 4 * plan.pairs, LANES),
    )


def high_adjoint(plan, grads, inv, mix, gain):
    return high_call(
        plan, functools.partial(high_adjoint_kernel, plan, len(grads)), "high_adjoint", grads, [inv],
        [mix, gain], (plan.quads, 5, plan.span, LANES), False,
        (1, plan.half_lanes * 4 * plan.pairs, LANES),
    )


def high_zonal(plan, grads, fwd):
    height = 2 * plan.pairs + 2 * plan.quad_pad
    return high_call(
        plan, functools.partial(high_zonal_kernel, plan), "high_zonal", [], [grads, fwd], [],
        (plan.rows, height, LANES), True, (plan.half_lanes * height, LANES),
    )


def predict_kernel(plan, first, live_ref, x_ref, idft_ref, enc_ref, dec_ref, *refs):
    recv, high, pred_ref, slope_ref, left, field = refs
    c = plan.channels
    wide = plan.n * plan.rows2
    for r in range(plan.rb):
        left[r * c : (r + 1) * c, :wide] = recv[:, r].reshape(wide, LANES).T
        left[r * c : (r + 1) * c, wide:] = high[r].T
    field[...] = jnp.dot(left[...], idft_ref[...], preferred_element_type=F32)
    base = first + pl.program_id(0) * plan.rb

    def step(r, unused):
        live = live_ref[base + r]
        x = x_ref[r]
        u = field[pl.ds(pl.multiple_of(r * c, 8), c), :]
        hidden = (jnp.dot(enc_ref[...], x, preferred_element_type=F32) * live).astype(BF)
        phi = 0.5 + 0.5 * lax.erf(u * (1.0 / math.sqrt(2.0)))
        slope = phi + u * jnp.exp(-0.5 * u * u) * (1.0 / math.sqrt(2.0 * math.pi))
        slope_ref[r] = slope.astype(BF)
        block = ((u * phi + hidden.astype(F32)) * live).astype(BF)
        decoded = jnp.dot(dec_ref[...], block, preferred_element_type=F32)
        pred_ref[r] = ((x.astype(F32) + decoded) * live).astype(BF)
        return unused

    lax.fori_loop(0, plan.rb, step, 0)


def predict(plan, chunk, live, x, idft, enc_t, dec_t, recv, high):
    first, count = chunk
    skip = first // plan.rb
    shape = (count, plan.fpad, plan.lon)
    slope_shape = (count, plan.channels, plan.lon)
    return pl.pallas_call(
        functools.partial(predict_kernel, plan, first),
        grid=(count // plan.rb,),
        in_specs=[
            pl.BlockSpec(memory_space=pltpu.SMEM),
            pl.BlockSpec((plan.rb,) + shape[1:], lambda i: (i + skip, 0, 0)),
            whole(idft.shape),
            whole(enc_t.shape),
            whole(dec_t.shape),
            pl.BlockSpec((plan.n, plan.rb, plan.rows2, LANES), lambda i: (0, i, 0, 0)),
            pl.BlockSpec((plan.rb,) + high.shape[1:], lambda i: (i + skip, 0, 0)),
        ],
        out_specs=[
            pl.BlockSpec((plan.rb,) + shape[1:], lambda i: (i, 0, 0)),
            pl.BlockSpec((plan.rb,) + slope_shape[1:], lambda i: (i, 0, 0)),
        ],
        out_shape=[jax.ShapeDtypeStruct(shape, BF), jax.ShapeDtypeStruct(slope_shape, BF)],
        scratch_shapes=[
            pltpu.VMEM((plan.rb * plan.channels, idft.shape[0]), BF),
            pltpu.VMEM((plan.rb * plan.channels, plan.lon), F32),
        ],
        compiler_params=params(),
        name="predict",
    )(live, x, idft, enc_t, dec_t, recv, high)


def score_kernel(plan, first, members, area_ref, own_ref, all_ref, obs_ref, slope_ref, idft_ref, dec_ref, *refs):
    grad_ref, out, out_high, right = refs
    c = plan.channels
    base = first + pl.program_id(0) * plan.rb

    def step(r, unused):
        area = area_ref[base + r]
        own = own_ref[r].astype(F32)
        gap = own - obs_ref[r].astype(F32)
        total = gap * lax.rsqrt(jnp.sum(gap * gap, axis=0, keepdims=True) + EPSILON)
        for e in range(members):
            gap = own - all_ref[e, r].astype(F32)
            near = lax.rsqrt(jnp.sum(gap * gap, axis=0, keepdims=True) + EPSILON)
            total = total - gap * (near * (1.0 / members))
        grad = (total * area).astype(BF)
        grad_ref[r] = grad
        block = jnp.dot(dec_ref[...], grad, preferred_element_type=F32)
        right[pl.ds(pl.multiple_of(r * c, 16), c), :] = (
            block * slope_ref[r].astype(F32)
        ).astype(BF)
        return unused

    lax.fori_loop(0, plan.rb, step, 0)
    wide = plan.n * plan.rows2

    def modes(first, last):
        return lax.dot_general(
            idft_ref[first:last, :],
            right[...],
            (((1,), (1,)), ((), ())),
            preferred_element_type=F32,
        ).astype(BF)

    low, high = modes(0, wide), modes(wide, idft_ref.shape[0])
    for r in range(plan.rb):
        for o in range(plan.n):
            out[o, r] = low[o * plan.rows2 : (o + 1) * plan.rows2, r * c : (r + 1) * c]
        out_high[r] = high[:, r * c : (r + 1) * c]


def score(plan, chunk, area, own, everyone, observed, slope, idft, dec):
    first, count = chunk
    skip = first // plan.rb
    members = everyone.shape[0]
    cell = (plan.rb, plan.fpad, plan.lon)
    out_shape = (plan.n, count, plan.rows2, LANES)
    high = 4 * plan.pairs
    here = pl.BlockSpec(cell, lambda i: (i, 0, 0))
    return pl.pallas_call(
        functools.partial(score_kernel, plan, first, members),
        grid=(count // plan.rb,),
        in_specs=[
            pl.BlockSpec(memory_space=pltpu.SMEM),
            here,
            pl.BlockSpec((members,) + cell, lambda i: (0, i, 0, 0)),
            pl.BlockSpec(cell, lambda i: (i + skip, 0, 0)),
            pl.BlockSpec((plan.rb, plan.channels, plan.lon), lambda i: (i, 0, 0)),
            whole(idft.shape),
            whole(dec.shape),
        ],
        out_specs=[
            here,
            pl.BlockSpec((plan.n, plan.rb, plan.rows2, LANES), lambda i: (0, i, 0, 0)),
            pl.BlockSpec((plan.rb, high, LANES), lambda i: (i, 0, 0)),
        ],
        out_shape=[
            jax.ShapeDtypeStruct((count,) + cell[1:], BF),
            jax.ShapeDtypeStruct(out_shape, BF),
            jax.ShapeDtypeStruct((count, high, LANES), BF),
        ],
        scratch_shapes=[pltpu.VMEM((plan.rb * plan.channels, plan.lon), BF)],
        compiler_params=params(),
        name="score",
    )(area, own, everyone, observed, slope, idft, dec)


def finish_kernel(
    plan, live_ref, grad_ref, main_ref, rest_ref, through_ref, recv, high_ref, out_ref, left, small, field, field_small
):
    n, tp, tb = plan.n, plan.tp, plan.tb
    wide, tall, quads = n * tp, 2 * plan.pairs, 2 * plan.quad_pad
    for r in range(plan.rb):
        piece = recv[:, r].astype(F32)
        high = high_ref[r].astype(F32)
        mains = [(0, piece[:, :tp].reshape(wide, LANES).T), (2 * wide, high[:tall].T)]
        for first, main in mains:
            size = main.shape[1]
            for k in range(2):
                at = first + k * size
                left[r * SPLIT : (r + 1) * SPLIT, at : at + size] = main[
                    k * SPLIT : (k + 1) * SPLIT
                ].astype(BF)
        at = 0
        rests = [
            (piece[:, tp + 8 * group : tp + 8 * (group + 1)].reshape(n * 8, LANES), min(4, tb - 4 * group))
            for group in range(plan.rest_groups)
        ] + [(high[tall:], 4)]
        for rest, blocks in rests:
            turned = rest.T.astype(BF)
            for part in range(2 * blocks):
                small[r * REST : (r + 1) * REST, at : at + turned.shape[1]] = turned[
                    part * REST : (part + 1) * REST
                ]
                at += turned.shape[1]
    field[...] = jnp.dot(left[...], main_ref[...], preferred_element_type=F32)
    field_small[...] = jnp.dot(small[...], rest_ref[...], preferred_element_type=F32)
    base = pl.program_id(0) * plan.rb

    def step(r, unused):
        live = live_ref[base + r]
        grad = grad_ref[r]
        through = jnp.dot(through_ref[...], grad, preferred_element_type=F32)
        spectral = jnp.concatenate(
            [
                field[pl.ds(pl.multiple_of(r * SPLIT, 8), SPLIT), :],
                field_small[pl.ds(pl.multiple_of(r * REST, 8), REST), :],
            ],
            axis=0,
        )
        out_ref[r] = ((grad.astype(F32) + through + spectral) * live).astype(BF)
        return unused

    lax.fori_loop(0, plan.rb, step, 0)


def finish(plan, live, grad, main, rest, through, recv, high):
    cell = (plan.rb, plan.fpad, plan.lon)
    here = pl.BlockSpec(cell, lambda i: (i, 0, 0))
    return pl.pallas_call(
        functools.partial(finish_kernel, plan),
        grid=(plan.rows // plan.rb,),
        in_specs=[
            pl.BlockSpec(memory_space=pltpu.SMEM),
            here,
            whole(main.shape),
            whole(rest.shape),
            whole(through.shape),
            pl.BlockSpec((plan.n, plan.rb, plan.rows1, LANES), lambda i: (0, i, 0, 0)),
            pl.BlockSpec((plan.rb,) + high.shape[1:], lambda i: (i, 0, 0)),
        ],
        out_specs=here,
        out_shape=jax.ShapeDtypeStruct((plan.rows, plan.fpad, plan.lon), BF),
        scratch_shapes=[
            pltpu.VMEM((plan.rb * SPLIT, main.shape[0]), BF),
            pltpu.VMEM((plan.rb * REST, rest.shape[0]), BF),
            pltpu.VMEM((plan.rb * SPLIT, plan.lon), F32),
            pltpu.VMEM((plan.rb * REST, plan.lon), F32),
        ],
        compiler_params=params(),
        name="finish",
    )(live, grad, main, rest, through, recv, high)


def row_geometry(band_rows, band_len, lat_count):
    band_count = band_rows.shape[0]
    row_index = jnp.arange(band_count * band_len, dtype=jnp.int32)
    row_owner = row_index // band_len
    offset = row_index - row_owner * band_len
    starts = jnp.cumsum(band_rows) - band_rows
    owner_hot = (row_owner[:, None] == jnp.arange(band_count, dtype=jnp.int32)[None, :]).astype(
        jnp.int32
    )
    first_lat = jnp.sum(owner_hot * starts[None, :], axis=1)
    length = jnp.sum(owner_hot * band_rows[None, :], axis=1)
    live_rows = offset < length
    latitude = jnp.minimum(first_lat + offset, lat_count - 1)
    colatitude = latitude.astype(F32) * (math.pi / (lat_count - 1))
    return (live_rows.astype(F32), jnp.cos(colatitude), jnp.sin(colatitude))


def log_diagonal(order):
    index = np.arange(1, LMAX + 1, dtype=np.float64)
    sums = np.concatenate([[0.0], np.cumsum(0.5 * np.log((2 * index + 1) / (2 * index)))])
    return (0.5 * math.log(0.5) + sums[np.minimum(order, LMAX)]).astype(np.float32)


def field_weights(plan, weight):
    c = plan.channels
    head, tail = weight[:SPLIT], jnp.pad(weight[SPLIT:], ((0, plan.fpad - plan.fields), (0, 0)))
    blocks = []
    for b in range(4):
        out = jnp.zeros((2 * LANES, 2 * c), F32)
        for k in range(2):
            out = out.at[k * SPLIT : (k + 1) * SPLIT, k * c : (k + 1) * c].set(head)
            first = LANES + (2 * b + k) * REST
            out = out.at[first : first + REST, k * c : (k + 1) * c].set(tail)
        blocks.append(out)
    return jnp.stack(blocks).astype(BF)


def on_device(
    states, observed, band_rows, encoder_weight, mixing_weight, degree_gain, decoder_weight
):
    space = lax.axis_size("space")
    me = lax.axis_index("space")
    fields, band, lon = observed.shape
    channels = encoder_weight.shape[1]
    plan = Plan(space, band, fields, lon, channels, degree_gain.shape[0])
    live, cosines, sines = row_geometry(band_rows, band, NLAT)
    quad = live * sines * (math.pi / (NLAT - 1))
    log_sines = jnp.log(jnp.maximum(sines, 1e-30))
    live_own = lax.dynamic_slice_in_dim(live, me * band, band)
    area = 8.0 * lax.dynamic_slice_in_dim(sines, me * band, band) * live_own

    pad = plan.fpad - fields
    rows = jnp.pad(jnp.transpose(states[0], (1, 0, 2)), ((0, 0), (0, pad), (0, 0)))
    truth = jnp.pad(jnp.transpose(observed, (1, 0, 2)), ((0, 0), (0, pad), (0, 0)))

    enc_f = encoder_weight.astype(F32)
    exact = lax.Precision.HIGHEST
    through_mix = jnp.dot(enc_f, mixing_weight.astype(F32), precision=exact)
    mix = field_weights(plan, through_mix)
    mix_back = jnp.transpose(mix, (0, 2, 1))
    gain = jnp.concatenate([degree_gain, degree_gain], axis=1)
    enc_t = jnp.pad(encoder_weight.T, ((0, 0), (0, pad)))
    dec_t = jnp.pad(decoder_weight.T, ((0, pad), (0, 0)))
    dec = jnp.pad(decoder_weight, ((0, 0), (0, pad)))
    through = jnp.pad(
        jnp.dot(enc_f, decoder_weight.astype(F32), precision=exact), ((0, pad), (0, pad))
    ).astype(BF)

    n, tp, tb = plan.n, plan.tp, plan.tb
    low, high = plan.low_orders(), plan.high_orders()
    low_f, high_f = dft_rows(plan, low, False), dft_rows(plan, high, False)
    low_i, high_i = dft_rows(plan, low, True), dft_rows(plan, high, True)
    dft_low = jnp.asarray(low_f.reshape(2, n * tp, lon))
    dft_high = jnp.asarray(high_f.reshape(2, 2 * plan.pairs, lon))
    idft = jnp.asarray(
        np.concatenate(
            [
                low_i.transpose(1, 0, 2, 3).reshape(n * 2 * tp, lon),
                high_i.reshape(4 * plan.pairs, lon),
            ]
        )
    )
    dft_main = jnp.asarray(
        np.concatenate([low_f.reshape(2 * n * tp, lon), high_f.reshape(4 * plan.pairs, lon)])
    )
    low_rest = low_f.reshape(2, n, tb, 8, lon).transpose(2, 0, 1, 3, 4)
    quads = np.zeros((2, 2, plan.quad_pad, 4, lon), low_f.dtype)
    quads[:, :, : plan.quads] = high_f.reshape(2, 2, plan.quads, 4, lon)
    dft_rest = jnp.asarray(
        np.concatenate(
            [low_rest.reshape(-1, lon), quads.transpose(3, 0, 1, 2, 4).reshape(-1, lon)]
        )
    )

    def exchange(block):
        return lax.all_to_all(block, "space", split_axis=0, concat_axis=0, tiled=True)

    sent, zonal_high = analyse(plan, rows, dft_low, dft_high)
    recv = exchange(sent)

    half = plan.half_lanes

    def side(value):
        value = jnp.pad(value, (0, half - band))
        return jnp.concatenate([value, value])

    def sides(pair_values):
        return jnp.asarray(np.repeat(pair_values.T, half, axis=1))

    own = [
        side(lax.dynamic_slice_in_dim(v, me * band, band)) for v in (cosines, quad, live, log_sines)
    ]
    shift = np.stack([plan.low + np.arange(plan.pairs), np.full(plan.pairs, plan.low - 1)])
    start = sides(log_diagonal(high)) + sides(high.astype(np.float32)) * own[3][None, :]
    high_fwd, high_inv = legendre_tables(
        sides(high), sides(shift), start, own[0], own[1], own[2], plan.span
    )
    high_coeffs = lax.psum(high_partial(plan, zonal_high, high_fwd), "space")

    orders = lax.dynamic_index_in_dim(jnp.asarray(low, jnp.int32), me, keepdims=False)
    diagonal = lax.dynamic_index_in_dim(jnp.asarray(log_diagonal(low)), me, keepdims=False)
    orders_wide = jnp.broadcast_to(orders[:, None], (tp, LANES))
    start = diagonal[:, None] + orders.astype(F32)[:, None] * log_sines[None, :]
    low_fwd, low_inv = legendre_tables(
        orders_wide, jnp.zeros_like(orders_wide), start, cosines, quad, live, plan.degrees
    )

    spectrum = spectrum_forward(plan, recv, low_fwd, low_inv, mix, gain)
    synth = [exchange(part) for part in spectrum]
    reach = ceil_to(plan.low + plan.pairs + plan.span, 8)
    longer = jnp.pad(degree_gain, ((0, reach + 8 - degree_gain.shape[0]), (0, 0)))
    gain_long = jnp.stack([longer[s : s + reach] for s in range(8)])
    synth_high = high_synthesis(plan, high_coeffs, high_inv, mix, gain_long)

    predictions, grads, returned, returned_high = [], [], [], []
    for i, chunk in enumerate(plan.chunks):
        pred, slope = predict(
            plan, chunk, live_own, rows, idft, enc_t, dec_t, synth[i], synth_high
        )
        everyone = lax.all_gather(pred[None], "member", axis=0, tiled=True)
        grad, out, out_high = score(plan, chunk, area, pred, everyone, truth, slope, idft, dec)
        predictions.append(pred)
        grads.append(grad)
        returned.append(exchange(out))
        returned_high.append(out_high)

    high_grads = lax.psum(
        high_adjoint(plan, returned_high, high_inv, mix_back, gain_long), "space"
    )
    last = exchange(spectrum_backward(plan, returned, low_fwd, low_inv, mix_back, gain))
    zonal_grad = high_zonal(plan, high_grads, high_fwd)
    state_grad = finish(
        plan, live_own, jnp.concatenate(grads), dft_main, dft_rest, through, last, zonal_grad
    )

    def outward(block):
        return jnp.transpose(block[:, :fields], (1, 0, 2))[None]

    return (outward(jnp.concatenate(predictions)), outward(state_grad))


def solution(mesh):
    in_specs = (P("member", None, "space", None), P(None, "space", None), P(), P(), P(), P(), P())
    out_specs = (P("member", None, "space", None), P("member", None, "space", None))
    return jax.shard_map(
        on_device, mesh=mesh, in_specs=in_specs, out_specs=out_specs, check_vma=False
    )
```

```python
import functools
import math

import jax
import jax.numpy as jnp
import ml_dtypes
import numpy as np
from jax import lax
from jax.experimental import pallas as pl
from jax.experimental.pallas import tpu as pltpu
from jax.sharding import PartitionSpec as P

NLAT = 361
LMAX = 360
EPSILON = 1e-05
GROUP = 256
SPLIT = 64
REST = 16
LANES = 128
NONE = 1 << 14
VMEM = 60 * 1024 * 1024
BF = jnp.bfloat16
F32 = jnp.float32


def ceil_to(value, step):
    return -(-value // step) * step


class Plan:
    def __init__(self, space, band, fields, lon, channels, degrees):
        self.n, self.rows, self.fields, self.lon = space, band, fields, lon
        self.channels, self.degrees = channels, degrees
        self.all_rows = space * band
        self.fpad = SPLIT + REST
        self.live_t = -(-GROUP // space)
        self.tp = ceil_to(self.live_t, 8)
        self.tb = self.tp // 8
        self.rest_groups = -(-self.tb // 4)
        self.rows1 = self.tp + 8 * self.rest_groups
        self.rows2 = 2 * self.tp
        self.low = space * self.live_t
        self.high = LMAX + 1 - self.low
        self.pairs = ceil_to(-(-self.high // 2), 8)
        self.quads = self.pairs // 4
        self.quad_pad = ceil_to(self.quads, 8)
        self.span = ceil_to(self.high + 1, 16)
        self.half = ceil_to(band, 16)
        self.half_lanes = LANES // 2
        self.rb = max(k for k in range(1, 9) if band % k == 0)
        blocks = band // self.rb
        half = blocks // 2
        counts = [count for count in (half, blocks - 1 - half, 1) if count > 0]
        self.chunks = []
        start = 0
        for count in counts:
            self.chunks.append((start * self.rb, count * self.rb))
            start += count

    def low_orders(self):
        device = np.arange(self.n)[:, None]
        position = np.arange(self.tp)[None, :]
        return np.where(position < self.live_t, device * self.live_t + position, NONE)

    def high_orders(self):
        pair = np.arange(self.pairs)
        first = np.where(2 * pair < self.high, self.low + pair, NONE)
        second = np.where(2 * pair < self.high - 1, LMAX - pair, NONE)
        return np.stack([first, second])


def dft_rows(plan, order, inverse):
    live = (order <= LMAX)[..., None]
    turn = (np.where(order <= LMAX, order, 0)[..., None] * np.arange(plan.lon)) % plan.lon
    angle = turn * (2.0 * math.pi / plan.lon)
    if inverse:
        scale = np.where((order == 0) | (2 * order == plan.lon), 1.0, 2.0)[..., None]
    else:
        scale = 1.0 / plan.lon
    rows = np.stack([np.cos(angle) * scale, -np.sin(angle) * scale]) * live
    return rows.astype(ml_dtypes.bfloat16)


def params(**more):
    return pltpu.CompilerParams(vmem_limit_bytes=VMEM, **more)


def whole(shape):
    return pl.BlockSpec(shape, lambda *_: (0,) * len(shape))


def table_kernel(m_ref, shift_ref, start_ref, cos_ref, quad_ref, live_ref, fwd_ref, inv_ref, one, two, logs, stage):
    block = pl.program_id(1)
    lanes = fwd_ref.shape[2]
    order, shift = m_ref[...], shift_ref[...]

    @pl.when(block == 0)
    def _():
        one[...] = jnp.zeros_like(one)
        two[...] = jnp.zeros_like(two)
        logs[...] = start_ref[...]

    ups, backs, pasts, onsets, keeps = [], [], [], [], []
    for p in range(16):
        deg = shift + (block * 16 + p).astype(F32)
        ups.append(
            jnp.sqrt((4.0 * deg * deg - 1.0) / jnp.maximum(deg * deg - order * order, 1.0))
        )
        less = (deg - 1.0) * (deg - 1.0)
        backs.append(
            jnp.sqrt(
                jnp.maximum(less - order * order, 0.0) / jnp.maximum(4.0 * less - 1.0, 1.0)
            )
        )
        pasts.append(order < deg)
        onsets.append(jnp.where(order == deg, 1.0, 0.0))
        keeps.append((order <= deg) & (deg <= LMAX))
    for c in range(one.shape[1] // LANES):
        at = slice(c * LANES, (c + 1) * LANES)
        first, second, log_scale = one[:, at], two[:, at], logs[:, at]
        cosine = cos_ref[:, at]
        scale = jnp.exp(log_scale)
        for p in range(16):
            current = jnp.where(
                pasts[p], ups[p] * (cosine * first - backs[p] * second), onsets[p]
            )
            stage[c, pl.ds(p, 8, stride=16), :] = jnp.where(keeps[p], current * scale, 0.0)
            second = first
            first = current
        size = jnp.maximum(jnp.abs(first), jnp.abs(second))
        factor = jnp.where(size > 1.0, size, 1.0)
        one[:, at] = first / factor
        two[:, at] = second / factor
        logs[:, at] = log_scale + jnp.log(factor)
        width = min(LANES, lanes - c * LANES)
        out = slice(c * LANES, c * LANES + width)
        for i in range(8):
            values = stage[c, i * 16 : (i + 1) * 16, :]
            fwd_ref[i, :, out] = (values * quad_ref[:, at]).astype(BF)[:, :width]
            inv_ref[i, :, out] = (values * live_ref[:, at]).astype(BF)[:, :width]


def legendre_tables(orders, shift, log_start, cosines, quad, live, degrees):
    rows = cosines.shape[0]
    wide = ceil_to(rows, LANES)
    tp = orders.shape[0]

    def spread(row):
        return jnp.pad(row, (0, wide - rows))[None]

    shape = jax.ShapeDtypeStruct((tp, degrees, rows), BF)
    row_spec = pl.BlockSpec((1, wide), lambda i, j: (0, 0))
    lane_spec = pl.BlockSpec((8, LANES), lambda i, j: (i, 0))
    out_spec = pl.BlockSpec((8, 16, rows), lambda i, j: (i, j, 0))
    return pl.pallas_call(
        table_kernel,
        grid=(tp // 8, degrees // 16),
        in_specs=[
            lane_spec,
            lane_spec,
            pl.BlockSpec((8, wide), lambda i, j: (i, 0)),
            row_spec,
            row_spec,
            row_spec,
        ],
        out_specs=[out_spec, out_spec],
        out_shape=[shape, shape],
        scratch_shapes=[
            pltpu.VMEM((8, wide), F32),
            pltpu.VMEM((8, wide), F32),
            pltpu.VMEM((8, wide), F32),
            pltpu.VMEM((wide // LANES, 128, LANES), F32),
        ],
        compiler_params=params(),
        name="legendre_tables",
    )(
        orders.astype(F32),
        shift.astype(F32),
        jnp.pad(log_start, ((0, 0), (0, wide - rows))),
        spread(cosines),
        spread(quad),
        spread(live),
    )


def analyse_modes(x, dft_ref):
    head, tail = x[:SPLIT], x[SPLIT:]
    right = jnp.concatenate([head, head] + [tail] * (LANES // REST), axis=0)
    return [
        lax.dot_general(
            dft_ref[k], right, (((1,), (1,)), ((), ())), preferred_element_type=F32
        )
        for k in range(2)
    ]


def analyse_low_kernel(plan, x_ref, dft_ref, out):
    lane = lax.broadcasted_iota(jnp.int32, (1, LANES), 1)
    part = lane // REST
    n, tp = plan.n, plan.tp
    for r in range(plan.rb):
        cosine, sine = analyse_modes(x_ref[r], dft_ref)
        main = jnp.where(lane < SPLIT, cosine[:, :LANES], sine[:, :LANES])
        for o in range(n):
            pieces = [main[o * tp : (o + 1) * tp]]
            for group in range(plan.rest_groups):
                rest = jnp.zeros((8, LANES), F32)
                for i in range(min(4, plan.tb - group * 4)):
                    first = o * tp + (group * 4 + i) * 8
                    rest = jnp.where(part == 2 * i, cosine[first : first + 8, LANES:], rest)
                    rest = jnp.where(part == 2 * i + 1, sine[first : first + 8, LANES:], rest)
                pieces.append(rest)
            out[o, r] = jnp.concatenate(pieces, axis=0).astype(BF)


def analyse_high_kernel(plan, x_ref, dft_ref, out):
    lane = lax.broadcasted_iota(jnp.int32, (1, LANES), 1)
    even = lane // REST % 2 == 0
    for r in range(plan.rb):
        cosine, sine = analyse_modes(x_ref[r], dft_ref)
        main = jnp.where(lane < SPLIT, cosine[:, :LANES], sine[:, :LANES])
        rest = jnp.where(even, cosine[:, LANES:], sine[:, LANES:])
        out[r] = jnp.concatenate([main, rest], axis=1).astype(BF)


def analyse(plan, kernel, name, x, dft, shape, axis):
    block = shape[:axis] + (plan.rb,) + shape[axis + 1 :]
    return pl.pallas_call(
        functools.partial(kernel, plan),
        grid=(plan.rows // plan.rb,),
        in_specs=[
            pl.BlockSpec((plan.rb, plan.fpad, plan.lon), lambda i: (i, 0, 0)),
            whole(dft.shape),
        ],
        out_specs=pl.BlockSpec(block, lambda i: tuple(i if a == axis else 0 for a in range(len(shape)))),
        out_shape=jax.ShapeDtypeStruct(shape, BF),
        compiler_params=params(),
        name=name,
    )(x, dft)


def analyse_low(plan, x, dft):
    shape = (plan.n, plan.rows, plan.rows1, LANES)
    return analyse(plan, analyse_low_kernel, "analyse_low", x, dft, shape, 1)


def analyse_high(plan, x, dft):
    shape = (plan.rows, 2 * plan.pairs, 2 * LANES)
    return analyse(plan, analyse_high_kernel, "analyse_high", x, dft, shape, 0)


def unpack(plan, refs, store, height):
    start = 0
    for ref in refs:
        count = ref.shape[1]
        for o in range(plan.n):
            base = o * plan.rows + start

            def step(r, unused, o=o, base=base, ref=ref):
                at = pl.multiple_of((base + r) * height, 8)
                store[pl.ds(at, height), :] = ref[o, r].astype(F32)
                return unused

            lax.fori_loop(0, count, step, 0)
        start += count


def repack(plan, refs, store, height):
    start = 0
    for ref in refs:
        count = ref.shape[1]
        for o in range(plan.n):
            base = o * plan.rows + start

            def step(r, unused, o=o, base=base, ref=ref):
                at = pl.multiple_of((base + r) * height, 8)
                ref[o, r] = store[pl.ds(at, height), :].astype(BF)
                return unused

            lax.fori_loop(0, count, step, 0)
        start += count


def rest_row(plan, t):
    block = t // 8
    return plan.tp + 8 * (block // 4) + t % 8


def spectrum_forward_kernel(plan, recv, fwd, inv, mix, gain, *refs):
    outs, zin, yout = refs[:-2], refs[-2], refs[-1]
    t = pl.program_id(0)

    @pl.when(t == 0)
    def _():
        unpack(plan, [recv], zin, plan.rows1)
        if plan.live_t < plan.tp:
            yout[...] = jnp.zeros_like(yout)

    z = jnp.concatenate(
        [
            zin[pl.ds(t, plan.all_rows, stride=plan.rows1), :],
            zin[pl.ds(rest_row(plan, t), plan.all_rows, stride=plan.rows1), :],
        ],
        axis=1,
    ).astype(BF)
    coeffs = jnp.dot(fwd[0], z, preferred_element_type=F32).astype(BF)
    filtered = (jnp.dot(coeffs, mix[0], preferred_element_type=F32) * gain[...]).astype(BF)
    y = lax.dot_general(
        inv[0], filtered, (((0,), (0,)), ((), ())), preferred_element_type=F32
    )
    for k in range(2):
        yout[pl.ds(k * plan.tp + t, plan.all_rows, stride=plan.rows2), :] = y[
            :, k * LANES : (k + 1) * LANES
        ]

    @pl.when(t == plan.live_t - 1)
    def _():
        repack(plan, outs, yout, plan.rows2)


def spectrum_backward_kernel(plan, count, *refs):
    recvs = refs[:count]
    fwd, inv, mix, gain = refs[count : count + 4]
    out, zin, yout = refs[count + 4 :]
    t = pl.program_id(0)

    @pl.when(t == 0)
    def _():
        unpack(plan, recvs, zin, plan.rows2)
        yout[...] = jnp.zeros_like(yout)

    z = jnp.concatenate(
        [
            zin[pl.ds(k * plan.tp + t, plan.all_rows, stride=plan.rows2), :]
            for k in range(2)
        ],
        axis=1,
    ).astype(BF)
    grad = (jnp.dot(inv[0], z, preferred_element_type=F32) * gain[...]).astype(BF)
    back = jnp.dot(grad, mix[0], preferred_element_type=F32).astype(BF)
    y = lax.dot_general(fwd[0], back, (((0,), (0,)), ((), ())), preferred_element_type=F32)
    yout[pl.ds(t, plan.all_rows, stride=plan.rows1), :] = y[:, :LANES]
    where = pl.ds(rest_row(plan, t), plan.all_rows, stride=plan.rows1)
    yout[where, :] = yout[where, :] + y[:, LANES:]

    @pl.when(t == plan.live_t - 1)
    def _():
        repack(plan, [out], yout, plan.rows1)


def spectrum_specs(plan, mix, gain):
    table = pl.BlockSpec((1, plan.degrees, plan.all_rows), lambda t: (t, 0, 0))
    return [table, table, pl.BlockSpec((1,) + mix.shape[1:], lambda t: ((t // 8) % 4, 0, 0)), whole(gain.shape)]


def spectrum_forward(plan, recv, fwd, inv, mix, gain):
    shapes = [(plan.n, count, plan.rows2, LANES) for _, count in plan.chunks]
    return pl.pallas_call(
        functools.partial(spectrum_forward_kernel, plan),
        grid=(plan.live_t,),
        in_specs=[whole(recv.shape)] + spectrum_specs(plan, mix, gain),
        out_specs=[whole(s) for s in shapes],
        out_shape=[jax.ShapeDtypeStruct(s, BF) for s in shapes],
        scratch_shapes=[
            pltpu.VMEM((plan.all_rows * plan.rows1, LANES), F32),
            pltpu.VMEM((plan.all_rows * plan.rows2, LANES), F32),
        ],
        compiler_params=params(),
        name="spectrum_forward",
    )(recv, fwd, inv, mix, gain)


def spectrum_backward(plan, recvs, fwd, inv, mix, gain):
    shape = (plan.n, plan.rows, plan.rows1, LANES)
    return pl.pallas_call(
        functools.partial(spectrum_backward_kernel, plan, len(recvs)),
        grid=(plan.live_t,),
        in_specs=[whole(r.shape) for r in recvs] + spectrum_specs(plan, mix, gain),
        out_specs=whole(shape),
        out_shape=jax.ShapeDtypeStruct(shape, BF),
        scratch_shapes=[
            pltpu.VMEM((plan.all_rows * plan.rows2, LANES), F32),
            pltpu.VMEM((plan.all_rows * plan.rows1, LANES), F32),
        ],
        compiler_params=params(),
        name="spectrum_backward",
    )(*recvs, fwd, inv, mix, gain)


def pair_gain(plan, pair, gain):
    row = lax.broadcasted_iota(jnp.int32, (plan.span, 1), 0)
    first, second = plan.low + pair, plan.low - 1
    first_at = pl.multiple_of(first // 8 * 8, 8)
    one = jnp.where(
        row < plan.high - pair,
        gain[first % 8, pl.ds(first_at, plan.span), :],
        gain[second % 8, pl.ds(second // 8 * 8, plan.span), :],
    )
    return jnp.concatenate([one, one], axis=1)


def load_rows(plan, refs, store, height, wide):
    start = 0
    for ref in refs:

        def step(r, unused, start=start, ref=ref):
            at = pl.multiple_of((start + r) * height, 8)
            for w in range(wide):
                store[w, pl.ds(at, height), :] = ref[r, :, w * LANES : (w + 1) * LANES].astype(F32)
            return unused

        lax.fori_loop(0, ref.shape[0], step, 0)
        start += ref.shape[0]

    def clear(r, unused):
        at = pl.multiple_of(r * height, 8)
        for w in range(wide):
            store[w, pl.ds(at, height), :] = jnp.zeros((height, LANES), F32)
        return unused

    lax.fori_loop(start, plan.half_lanes, clear, 0)


def high_partial_kernel(plan, zonal, fwd, out, zin):
    quad = pl.program_id(0)
    block = lax.broadcasted_iota(jnp.int32, (1, LANES), 1) // (2 * REST)

    @pl.when(quad == 0)
    def _():
        load_rows(plan, [zonal], zin, 2 * plan.pairs, 2)

    rest = jnp.zeros((plan.span, LANES), F32)
    for i in range(4):
        pair = quad * 4 + i
        z = jnp.concatenate(
            [
                jnp.concatenate(
                    [
                        zin[w, pl.ds(s * plan.pairs + pair, plan.half_lanes, stride=2 * plan.pairs), :]
                        for s in range(2)
                    ],
                    axis=0,
                )
                for w in range(2)
            ],
            axis=1,
        ).astype(BF)
        coeffs = jnp.dot(fwd[i], z, preferred_element_type=F32)
        out[0, i] = coeffs[:, :LANES].astype(BF)
        rest = rest + jnp.where(block == i, coeffs[:, LANES:], 0.0)
    out[0, 4] = rest.astype(BF)


def high_synthesis_kernel(plan, coeffs, inv, mix, gain, out, yout):
    quad = pl.program_id(0)
    height = 4 * plan.pairs
    for i in range(4):
        pair = quad * 4 + i
        both = jnp.concatenate([coeffs[0, i], coeffs[0, 4]], axis=1)
        filtered = jnp.dot(both, mix[i], preferred_element_type=F32) * pair_gain(plan, pair, gain)
        y = lax.dot_general(
            inv[i], filtered.astype(BF), (((0,), (0,)), ((), ())), preferred_element_type=F32
        )
        for k in range(2):
            for s in range(2):
                yout[pl.ds((2 * k + s) * plan.pairs + pair, plan.half_lanes, stride=height), :] = y[
                    s * plan.half_lanes : (s + 1) * plan.half_lanes, k * LANES : (k + 1) * LANES
                ]

    @pl.when(quad == plan.quads - 1)
    def _():
        def step(r, unused):
            out[r] = yout[pl.ds(pl.multiple_of(r * height, 8), height), :].astype(BF)
            return unused

        lax.fori_loop(0, plan.rows, step, 0)


def high_adjoint_kernel(plan, count, *refs):
    grads, (inv, mix, gain, out, zin) = refs[:count], refs[count:]
    quad = pl.program_id(0)
    height = 4 * plan.pairs

    @pl.when(quad == 0)
    def _():
        load_rows(plan, grads, zin, height, 1)

    rest = jnp.zeros((plan.span, LANES), F32)
    for i in range(4):
        pair = quad * 4 + i
        z = jnp.concatenate(
            [
                jnp.concatenate(
                    [
                        zin[0, pl.ds((2 * k + s) * plan.pairs + pair, plan.half_lanes, stride=height), :]
                        for s in range(2)
                    ],
                    axis=0,
                )
                for k in range(2)
            ],
            axis=1,
        ).astype(BF)
        grad = jnp.dot(inv[i], z, preferred_element_type=F32) * pair_gain(plan, pair, gain)
        back = jnp.dot(grad.astype(BF), mix[i], preferred_element_type=F32)
        out[0, i] = back[:, :LANES].astype(BF)
        rest = rest + back[:, LANES:]
    out[0, 4] = rest.astype(BF)


def high_zonal_kernel(plan, grads, fwd, out, yout):
    quad = pl.program_id(0)
    height = 2 * plan.pairs + 2 * plan.quad_pad
    block = lax.broadcasted_iota(jnp.int32, (1, LANES), 1) // (2 * REST)

    if plan.quad_pad > plan.quads:

        @pl.when(quad == 0)
        def _():
            yout[...] = jnp.zeros_like(yout)

    rest = jnp.zeros((LANES, LANES), F32)
    for i in range(4):
        pair = quad * 4 + i
        both = jnp.concatenate([grads[0, i], grads[0, 4]], axis=1)
        y = lax.dot_general(
            fwd[i], both, (((0,), (0,)), ((), ())), preferred_element_type=F32
        )
        for s in range(2):
            yout[pl.ds(s * plan.pairs + pair, plan.half_lanes, stride=height), :] = y[
                s * plan.half_lanes : (s + 1) * plan.half_lanes, :LANES
            ]
        rest = rest + jnp.where(block == i, y[:, LANES:], 0.0)
    for s in range(2):
        row = 2 * plan.pairs + s * plan.quad_pad + quad
        yout[pl.ds(row, plan.half_lanes, stride=height), :] = rest[
            s * plan.half_lanes : (s + 1) * plan.half_lanes
        ]

    @pl.when(quad == plan.quads - 1)
    def _():
        def step(r, unused):
            out[r] = yout[pl.ds(pl.multiple_of(r * height, 8), height), :].astype(BF)
            return unused

        lax.fori_loop(0, plan.rows, step, 0)


def high_call(plan, kernel, name, whole_in, blocked, fixed, out_shape, out_whole, scratch):
    def quad_spec(array):
        size = array.shape[0] // plan.quads
        rest = array.shape[1:]
        return pl.BlockSpec((size,) + rest, lambda q: (q,) + (0,) * len(rest))

    return pl.pallas_call(
        kernel,
        grid=(plan.quads,),
        in_specs=[whole(a.shape) for a in whole_in]
        + [quad_spec(a) for a in blocked]
        + [whole(a.shape) for a in fixed],
        out_specs=whole(out_shape) if out_whole else quad_spec(jax.ShapeDtypeStruct(out_shape, BF)),
        out_shape=jax.ShapeDtypeStruct(out_shape, BF),
        scratch_shapes=[pltpu.VMEM(scratch, F32)],
        compiler_params=params(),
        name=name,
    )(*whole_in, *blocked, *fixed)


def high_partial(plan, zonal, fwd):
    return high_call(
        plan, functools.partial(high_partial_kernel, plan), "high_partial", [zonal], [fwd], [],
        (plan.quads, 5, plan.span, LANES), False, (2, plan.half_lanes * 2 * plan.pairs, LANES),
    )


def high_synthesis(plan, coeffs, inv, mix, gain):
    return high_call(
        plan, functools.partial(high_synthesis_kernel, plan), "high_synthesis", [], [coeffs, inv],
        [mix, gain], (plan.rows, 4 * plan.pairs, LANES), True,
        (plan.half_lanes * 4 * plan.pairs, LANES),
    )


def high_adjoint(plan, grads, inv, mix, gain):
    return high_call(
        plan, functools.partial(high_adjoint_kernel, plan, len(grads)), "high_adjoint", grads, [inv],
        [mix, gain], (plan.quads, 5, plan.span, LANES), False,
        (1, plan.half_lanes * 4 * plan.pairs, LANES),
    )


def high_zonal(plan, grads, fwd):
    height = 2 * plan.pairs + 2 * plan.quad_pad
    return high_call(
        plan, functools.partial(high_zonal_kernel, plan), "high_zonal", [], [grads, fwd], [],
        (plan.rows, height, LANES), True, (plan.half_lanes * height, LANES),
    )


def predict_kernel(plan, first, live_ref, x_ref, idft_ref, enc_ref, dec_ref, *refs):
    recv, high, pred_ref, slope_ref, left, field = refs
    c = plan.channels
    wide = plan.n * plan.rows2
    for r in range(plan.rb):
        left[r * c : (r + 1) * c, :wide] = recv[:, r].reshape(wide, LANES).T
        left[r * c : (r + 1) * c, wide:] = high[r].T
    field[...] = jnp.dot(left[...], idft_ref[...], preferred_element_type=F32)
    base = first + pl.program_id(0) * plan.rb

    def step(r, unused):
        live = live_ref[base + r]
        x = x_ref[r]
        u = field[pl.ds(pl.multiple_of(r * c, 8), c), :]
        hidden = (jnp.dot(enc_ref[...], x, preferred_element_type=F32) * live).astype(BF)
        phi = 0.5 + 0.5 * lax.erf(u * (1.0 / math.sqrt(2.0)))
        slope = phi + u * jnp.exp(-0.5 * u * u) * (1.0 / math.sqrt(2.0 * math.pi))
        slope_ref[r] = slope.astype(BF)
        block = ((u * phi + hidden.astype(F32)) * live).astype(BF)
        decoded = jnp.dot(dec_ref[...], block, preferred_element_type=F32)
        pred_ref[r] = ((x.astype(F32) + decoded) * live).astype(BF)
        return unused

    lax.fori_loop(0, plan.rb, step, 0)


def predict(plan, chunk, live, x, idft, enc_t, dec_t, recv, high):
    first, count = chunk
    skip = first // plan.rb
    shape = (count, plan.fpad, plan.lon)
    slope_shape = (count, plan.channels, plan.lon)
    return pl.pallas_call(
        functools.partial(predict_kernel, plan, first),
        grid=(count // plan.rb,),
        in_specs=[
            pl.BlockSpec(memory_space=pltpu.SMEM),
            pl.BlockSpec((plan.rb,) + shape[1:], lambda i: (i + skip, 0, 0)),
            whole(idft.shape),
            whole(enc_t.shape),
            whole(dec_t.shape),
            pl.BlockSpec((plan.n, plan.rb, plan.rows2, LANES), lambda i: (0, i, 0, 0)),
            pl.BlockSpec((plan.rb,) + high.shape[1:], lambda i: (i + skip, 0, 0)),
        ],
        out_specs=[
            pl.BlockSpec((plan.rb,) + shape[1:], lambda i: (i, 0, 0)),
            pl.BlockSpec((plan.rb,) + slope_shape[1:], lambda i: (i, 0, 0)),
        ],
        out_shape=[jax.ShapeDtypeStruct(shape, BF), jax.ShapeDtypeStruct(slope_shape, BF)],
        scratch_shapes=[
            pltpu.VMEM((plan.rb * plan.channels, idft.shape[0]), BF),
            pltpu.VMEM((plan.rb * plan.channels, plan.lon), F32),
        ],
        compiler_params=params(),
        name="predict",
    )(live, x, idft, enc_t, dec_t, recv, high)


def score_kernel(plan, first, members, area_ref, own_ref, all_ref, obs_ref, slope_ref, idft_ref, dec_ref, *refs):
    grad_ref, out, out_high, right = refs
    c = plan.channels
    base = first + pl.program_id(0) * plan.rb

    def step(r, unused):
        area = area_ref[base + r]
        own = own_ref[r].astype(F32)
        gap = own - obs_ref[r].astype(F32)
        total = gap * lax.rsqrt(jnp.sum(gap * gap, axis=0, keepdims=True) + EPSILON)
        for e in range(members):
            gap = own - all_ref[e, r].astype(F32)
            near = lax.rsqrt(jnp.sum(gap * gap, axis=0, keepdims=True) + EPSILON)
            total = total - gap * (near * (1.0 / members))
        grad = (total * area).astype(BF)
        grad_ref[r] = grad
        block = jnp.dot(dec_ref[...], grad, preferred_element_type=F32)
        right[pl.ds(pl.multiple_of(r * c, 16), c), :] = (
            block * slope_ref[r].astype(F32)
        ).astype(BF)
        return unused

    lax.fori_loop(0, plan.rb, step, 0)
    wide = plan.n * plan.rows2

    def modes(first, last):
        return lax.dot_general(
            idft_ref[first:last, :],
            right[...],
            (((1,), (1,)), ((), ())),
            preferred_element_type=F32,
        ).astype(BF)

    low, high = modes(0, wide), modes(wide, idft_ref.shape[0])
    for r in range(plan.rb):
        for o in range(plan.n):
            out[o, r] = low[o * plan.rows2 : (o + 1) * plan.rows2, r * c : (r + 1) * c]
        out_high[r] = high[:, r * c : (r + 1) * c]


def score(plan, chunk, area, own, everyone, observed, slope, idft, dec):
    first, count = chunk
    skip = first // plan.rb
    members = everyone.shape[0]
    cell = (plan.rb, plan.fpad, plan.lon)
    out_shape = (plan.n, count, plan.rows2, LANES)
    high = 4 * plan.pairs
    here = pl.BlockSpec(cell, lambda i: (i, 0, 0))
    return pl.pallas_call(
        functools.partial(score_kernel, plan, first, members),
        grid=(count // plan.rb,),
        in_specs=[
            pl.BlockSpec(memory_space=pltpu.SMEM),
            here,
            pl.BlockSpec((members,) + cell, lambda i: (0, i, 0, 0)),
            pl.BlockSpec(cell, lambda i: (i + skip, 0, 0)),
            pl.BlockSpec((plan.rb, plan.channels, plan.lon), lambda i: (i, 0, 0)),
            whole(idft.shape),
            whole(dec.shape),
        ],
        out_specs=[
            here,
            pl.BlockSpec((plan.n, plan.rb, plan.rows2, LANES), lambda i: (0, i, 0, 0)),
            pl.BlockSpec((plan.rb, high, LANES), lambda i: (i, 0, 0)),
        ],
        out_shape=[
            jax.ShapeDtypeStruct((count,) + cell[1:], BF),
            jax.ShapeDtypeStruct(out_shape, BF),
            jax.ShapeDtypeStruct((count, high, LANES), BF),
        ],
        scratch_shapes=[pltpu.VMEM((plan.rb * plan.channels, plan.lon), BF)],
        compiler_params=params(),
        name="score",
    )(area, own, everyone, observed, slope, idft, dec)


def finish_kernel(
    plan, live_ref, grad_ref, main_ref, rest_ref, through_ref, recv, high_ref, out_ref, left, small, field, field_small
):
    n, tp, tb = plan.n, plan.tp, plan.tb
    wide, tall, quads = n * tp, 2 * plan.pairs, 2 * plan.quad_pad
    for r in range(plan.rb):
        piece = recv[:, r].astype(F32)
        high = high_ref[r].astype(F32)
        mains = [(0, piece[:, :tp].reshape(wide, LANES).T), (2 * wide, high[:tall].T)]
        for first, main in mains:
            size = main.shape[1]
            for k in range(2):
                at = first + k * size
                left[r * SPLIT : (r + 1) * SPLIT, at : at + size] = main[
                    k * SPLIT : (k + 1) * SPLIT
                ].astype(BF)
        at = 0
        rests = [
            (piece[:, tp + 8 * group : tp + 8 * (group + 1)].reshape(n * 8, LANES), min(4, tb - 4 * group))
            for group in range(plan.rest_groups)
        ] + [(high[tall:], 4)]
        for rest, blocks in rests:
            turned = rest.T.astype(BF)
            for part in range(2 * blocks):
                small[r * REST : (r + 1) * REST, at : at + turned.shape[1]] = turned[
                    part * REST : (part + 1) * REST
                ]
                at += turned.shape[1]
    field[...] = jnp.dot(left[...], main_ref[...], preferred_element_type=F32)
    field_small[...] = jnp.dot(small[...], rest_ref[...], preferred_element_type=F32)
    base = pl.program_id(0) * plan.rb

    def step(r, unused):
        live = live_ref[base + r]
        grad = grad_ref[r]
        through = jnp.dot(through_ref[...], grad, preferred_element_type=F32)
        spectral = jnp.concatenate(
            [
                field[pl.ds(pl.multiple_of(r * SPLIT, 8), SPLIT), :],
                field_small[pl.ds(pl.multiple_of(r * REST, 8), REST), :],
            ],
            axis=0,
        )
        out_ref[r] = ((grad.astype(F32) + through + spectral) * live).astype(BF)
        return unused

    lax.fori_loop(0, plan.rb, step, 0)


def finish(plan, live, grad, main, rest, through, recv, high):
    cell = (plan.rb, plan.fpad, plan.lon)
    here = pl.BlockSpec(cell, lambda i: (i, 0, 0))
    return pl.pallas_call(
        functools.partial(finish_kernel, plan),
        grid=(plan.rows // plan.rb,),
        in_specs=[
            pl.BlockSpec(memory_space=pltpu.SMEM),
            here,
            whole(main.shape),
            whole(rest.shape),
            whole(through.shape),
            pl.BlockSpec((plan.n, plan.rb, plan.rows1, LANES), lambda i: (0, i, 0, 0)),
            pl.BlockSpec((plan.rb,) + high.shape[1:], lambda i: (i, 0, 0)),
        ],
        out_specs=here,
        out_shape=jax.ShapeDtypeStruct((plan.rows, plan.fpad, plan.lon), BF),
        scratch_shapes=[
            pltpu.VMEM((plan.rb * SPLIT, main.shape[0]), BF),
            pltpu.VMEM((plan.rb * REST, rest.shape[0]), BF),
            pltpu.VMEM((plan.rb * SPLIT, plan.lon), F32),
            pltpu.VMEM((plan.rb * REST, plan.lon), F32),
        ],
        compiler_params=params(),
        name="finish",
    )(live, grad, main, rest, through, recv, high)


def row_geometry(band_rows, band_len, lat_count):
    band_count = band_rows.shape[0]
    row_index = jnp.arange(band_count * band_len, dtype=jnp.int32)
    row_owner = row_index // band_len
    offset = row_index - row_owner * band_len
    starts = jnp.cumsum(band_rows) - band_rows
    owner_hot = (row_owner[:, None] == jnp.arange(band_count, dtype=jnp.int32)[None, :]).astype(
        jnp.int32
    )
    first_lat = jnp.sum(owner_hot * starts[None, :], axis=1)
    length = jnp.sum(owner_hot * band_rows[None, :], axis=1)
    live_rows = offset < length
    latitude = jnp.minimum(first_lat + offset, lat_count - 1)
    colatitude = latitude.astype(F32) * (math.pi / (lat_count - 1))
    return (live_rows.astype(F32), jnp.cos(colatitude), jnp.sin(colatitude))


def log_diagonal(order):
    index = np.arange(1, LMAX + 1, dtype=np.float64)
    sums = np.concatenate([[0.0], np.cumsum(0.5 * np.log((2 * index + 1) / (2 * index)))])
    return (0.5 * math.log(0.5) + sums[np.minimum(order, LMAX)]).astype(np.float32)


def field_weights(plan, weight):
    select = np.zeros((4, 2 * LANES, plan.fields), np.float32)
    side = np.zeros((4, 2 * LANES, 2), np.float32)
    for b in range(4):
        for k in range(2):
            for f in range(plan.fields):
                first = k * SPLIT + f if f < SPLIT else LANES + (2 * b + k) * REST + f - SPLIT
                select[b, first, f] = 1.0
                side[b, first, k] = 1.0
    spread = jnp.einsum("blf,fc->blc", select, weight, precision=lax.Precision.HIGHEST)
    both = jnp.concatenate([spread, spread], axis=2)
    return (both * np.repeat(side, plan.channels, axis=2)).astype(BF)


def on_device(
    states, observed, band_rows, encoder_weight, mixing_weight, degree_gain, decoder_weight
):
    space = lax.axis_size("space")
    me = lax.axis_index("space")
    fields, band, lon = observed.shape
    channels = encoder_weight.shape[1]
    plan = Plan(space, band, fields, lon, channels, degree_gain.shape[0])
    live, cosines, sines = row_geometry(band_rows, band, NLAT)
    quad = live * sines * (math.pi / (NLAT - 1))
    log_sines = jnp.log(jnp.maximum(sines, 1e-30))
    live_own = lax.dynamic_slice_in_dim(live, me * band, band)
    area = 8.0 * lax.dynamic_slice_in_dim(sines, me * band, band) * live_own

    pad = plan.fpad - fields
    rows = jnp.pad(jnp.transpose(states[0], (1, 0, 2)), ((0, 0), (0, pad), (0, 0)))
    truth = jnp.pad(jnp.transpose(observed, (1, 0, 2)), ((0, 0), (0, pad), (0, 0)))

    enc_f = encoder_weight.astype(F32)
    exact = lax.Precision.HIGHEST
    through_mix = jnp.dot(enc_f, mixing_weight.astype(F32), precision=exact)
    mix = field_weights(plan, through_mix)
    mix_back = jnp.transpose(mix, (0, 2, 1))
    gain = jnp.concatenate([degree_gain, degree_gain], axis=1)
    enc_t = jnp.pad(encoder_weight.T, ((0, 0), (0, pad)))
    dec_t = jnp.pad(decoder_weight.T, ((0, pad), (0, 0)))
    dec = jnp.pad(decoder_weight, ((0, 0), (0, pad)))
    through = jnp.pad(
        jnp.dot(enc_f, decoder_weight.astype(F32), precision=exact), ((0, pad), (0, pad))
    ).astype(BF)

    n, tp, tb = plan.n, plan.tp, plan.tb
    low, high = plan.low_orders(), plan.high_orders()
    low_f, high_f = dft_rows(plan, low, False), dft_rows(plan, high, False)
    low_i, high_i = dft_rows(plan, low, True), dft_rows(plan, high, True)
    dft_low = jnp.asarray(low_f.reshape(2, n * tp, lon))
    dft_high = jnp.asarray(high_f.reshape(2, 2 * plan.pairs, lon))
    idft = jnp.asarray(
        np.concatenate(
            [
                low_i.transpose(1, 0, 2, 3).reshape(n * 2 * tp, lon),
                high_i.reshape(4 * plan.pairs, lon),
            ]
        )
    )
    dft_main = jnp.asarray(
        np.concatenate([low_f.reshape(2 * n * tp, lon), high_f.reshape(4 * plan.pairs, lon)])
    )
    low_rest = low_f.reshape(2, n, tb, 8, lon).transpose(2, 0, 1, 3, 4)
    quads = np.zeros((2, 2, plan.quad_pad, 4, lon), low_f.dtype)
    quads[:, :, : plan.quads] = high_f.reshape(2, 2, plan.quads, 4, lon)
    dft_rest = jnp.asarray(
        np.concatenate(
            [low_rest.reshape(-1, lon), quads.transpose(3, 0, 1, 2, 4).reshape(-1, lon)]
        )
    )

    def exchange(block):
        return lax.all_to_all(block, "space", split_axis=0, concat_axis=0, tiled=True)

    recv = exchange(analyse_low(plan, rows, dft_low))
    zonal_high = analyse_high(plan, rows, dft_high)

    half = plan.half_lanes

    def side(value):
        value = jnp.pad(value, (0, half - band))
        return jnp.concatenate([value, value])

    def sides(pair_values):
        return jnp.asarray(np.repeat(pair_values.T, half, axis=1))

    own = [
        side(lax.dynamic_slice_in_dim(v, me * band, band)) for v in (cosines, quad, live, log_sines)
    ]
    shift = np.stack([plan.low + np.arange(plan.pairs), np.full(plan.pairs, plan.low - 1)])
    start = sides(log_diagonal(high)) + sides(high.astype(np.float32)) * own[3][None, :]
    high_fwd, high_inv = legendre_tables(
        sides(high), sides(shift), start, own[0], own[1], own[2], plan.span
    )
    high_coeffs = lax.psum(high_partial(plan, zonal_high, high_fwd), "space")

    orders = lax.dynamic_index_in_dim(jnp.asarray(low, jnp.int32), me, keepdims=False)
    diagonal = lax.dynamic_index_in_dim(jnp.asarray(log_diagonal(low)), me, keepdims=False)
    orders_wide = jnp.broadcast_to(orders[:, None], (tp, LANES))
    start = diagonal[:, None] + orders.astype(F32)[:, None] * log_sines[None, :]
    low_fwd, low_inv = legendre_tables(
        orders_wide, jnp.zeros_like(orders_wide), start, cosines, quad, live, plan.degrees
    )

    spectrum = spectrum_forward(plan, recv, low_fwd, low_inv, mix, gain)
    synth = [exchange(part) for part in spectrum]
    reach = ceil_to(plan.low + plan.pairs + plan.span, 8)
    longer = jnp.pad(degree_gain, ((0, reach + 8 - degree_gain.shape[0]), (0, 0)))
    gain_long = jnp.stack([longer[s : s + reach] for s in range(8)])
    synth_high = high_synthesis(plan, high_coeffs, high_inv, mix, gain_long)

    predictions, grads, returned, returned_high = [], [], [], []
    for i, chunk in enumerate(plan.chunks):
        pred, slope = predict(
            plan, chunk, live_own, rows, idft, enc_t, dec_t, synth[i], synth_high
        )
        everyone = lax.all_gather(pred[None], "member", axis=0, tiled=True)
        grad, out, out_high = score(plan, chunk, area, pred, everyone, truth, slope, idft, dec)
        predictions.append(pred)
        grads.append(grad)
        returned_high.append(out_high)
        if i == len(plan.chunks) - 1:
            high_grads = high_adjoint(plan, returned_high, high_inv, mix_back, gain_long)
            out, high_grads = lax.optimization_barrier((out, high_grads))
            high_grads = lax.psum(high_grads, "space")
        returned.append(exchange(out))

    last = exchange(spectrum_backward(plan, returned, low_fwd, low_inv, mix_back, gain))
    zonal_grad = high_zonal(plan, high_grads, high_fwd)
    state_grad = finish(
        plan, live_own, jnp.concatenate(grads), dft_main, dft_rest, through, last, zonal_grad
    )

    def outward(block):
        return jnp.transpose(block[:, :fields], (1, 0, 2))[None]

    return (outward(jnp.concatenate(predictions)), outward(state_grad))


def solution(mesh):
    in_specs = (P("member", None, "space", None), P(None, "space", None), P(), P(), P(), P(), P())
    out_specs = (P("member", None, "space", None), P("member", None, "space", None))
    return jax.shard_map(
        on_device, mesh=mesh, in_specs=in_specs, out_specs=out_specs, check_vma=False
    )
```

```python
import functools
import math

import jax
import jax.numpy as jnp
import ml_dtypes
import numpy as np
from jax import lax
from jax.experimental import pallas as pl
from jax.experimental.pallas import tpu as pltpu
from jax.sharding import PartitionSpec as P

NLAT = 361
LMAX = 360
EPSILON = 1e-05
GROUP = 256
SPLIT = 64
REST = 16
LANES = 128
NONE = 1 << 14
VMEM = 60 * 1024 * 1024
BF = jnp.bfloat16
F32 = jnp.float32


def ceil_to(value, step):
    return -(-value // step) * step


class Plan:
    def __init__(self, space, band, fields, lon, channels, degrees):
        self.n, self.rows, self.fields, self.lon = space, band, fields, lon
        self.channels, self.degrees = channels, degrees
        self.all_rows = space * band
        self.fpad = SPLIT + REST
        self.live_t = -(-GROUP // space)
        self.tp = ceil_to(self.live_t, 8)
        self.tb = self.tp // 8
        self.rest_groups = -(-self.tb // 4)
        self.rows1 = self.tp + 8 * self.rest_groups
        self.rows2 = 2 * self.tp
        self.low = space * self.live_t
        self.high = LMAX + 1 - self.low
        self.pairs = ceil_to(-(-self.high // 2), 8)
        self.quads = self.pairs // 4
        self.quad_pad = ceil_to(self.quads, 8)
        self.span = ceil_to(self.high + 1, 16)
        self.half = ceil_to(band, 16)
        self.half_lanes = LANES // 2
        self.rb = max(k for k in range(1, 9) if band % k == 0)
        blocks = band // self.rb
        half = blocks // 2
        counts = [count for count in (1, blocks - 1 - half, half) if count > 0]
        self.chunks = []
        start = 0
        for count in counts:
            self.chunks.append((start * self.rb, count * self.rb))
            start += count

    def low_orders(self):
        device = np.arange(self.n)[:, None]
        position = np.arange(self.tp)[None, :]
        return np.where(position < self.live_t, device * self.live_t + position, NONE)

    def high_orders(self):
        pair = np.arange(self.pairs)
        first = np.where(2 * pair < self.high, self.low + pair, NONE)
        second = np.where(2 * pair < self.high - 1, LMAX - pair, NONE)
        return np.stack([first, second])


def dft_rows(plan, order, inverse):
    live = (order <= LMAX)[..., None]
    turn = (np.where(order <= LMAX, order, 0)[..., None] * np.arange(plan.lon)) % plan.lon
    angle = turn * (2.0 * math.pi / plan.lon)
    if inverse:
        scale = np.where((order == 0) | (2 * order == plan.lon), 1.0, 2.0)[..., None]
    else:
        scale = 1.0 / plan.lon
    rows = np.stack([np.cos(angle) * scale, -np.sin(angle) * scale]) * live
    return rows.astype(ml_dtypes.bfloat16)


def params(**more):
    return pltpu.CompilerParams(vmem_limit_bytes=VMEM, **more)


def call(kernel, name, operands, in_specs, out_specs, out_shape, grid, scratch=()):
    results = out_shape if isinstance(out_shape, (list, tuple)) else [out_shape]
    moved = sum(math.prod(a.shape) * a.dtype.itemsize for a in list(operands) + list(results))
    return pl.pallas_call(
        kernel,
        grid=grid,
        in_specs=in_specs,
        out_specs=out_specs,
        out_shape=out_shape,
        scratch_shapes=list(scratch),
        compiler_params=params(),
        cost_estimate=pl.CostEstimate(flops=0, transcendentals=0, bytes_accessed=4 * moved),
        name=name,
    )(*operands)


def whole(shape):
    return pl.BlockSpec(shape, lambda *_: (0,) * len(shape))


def table_kernel(m_ref, shift_ref, start_ref, cos_ref, quad_ref, live_ref, fwd_ref, inv_ref, one, two, logs, stage):
    block = pl.program_id(1)
    lanes = fwd_ref.shape[2]
    order, shift = m_ref[...], shift_ref[...]

    @pl.when(block == 0)
    def _():
        one[...] = jnp.zeros_like(one)
        two[...] = jnp.zeros_like(two)
        logs[...] = start_ref[...]

    ups, backs, pasts, onsets, keeps = [], [], [], [], []
    for p in range(16):
        deg = shift + (block * 16 + p).astype(F32)
        ups.append(
            jnp.sqrt((4.0 * deg * deg - 1.0) / jnp.maximum(deg * deg - order * order, 1.0))
        )
        less = (deg - 1.0) * (deg - 1.0)
        backs.append(
            jnp.sqrt(
                jnp.maximum(less - order * order, 0.0) / jnp.maximum(4.0 * less - 1.0, 1.0)
            )
        )
        pasts.append(order < deg)
        onsets.append(jnp.where(order == deg, 1.0, 0.0))
        keeps.append((order <= deg) & (deg <= LMAX))
    for c in range(one.shape[1] // LANES):
        at = slice(c * LANES, (c + 1) * LANES)
        first, second, log_scale = one[:, at], two[:, at], logs[:, at]
        cosine = cos_ref[:, at]
        scale = jnp.exp(log_scale)
        for p in range(16):
            current = jnp.where(
                pasts[p], ups[p] * (cosine * first - backs[p] * second), onsets[p]
            )
            stage[c, pl.ds(p, 8, stride=16), :] = jnp.where(keeps[p], current * scale, 0.0)
            second = first
            first = current
        size = jnp.maximum(jnp.abs(first), jnp.abs(second))
        factor = jnp.where(size > 1.0, size, 1.0)
        one[:, at] = first / factor
        two[:, at] = second / factor
        logs[:, at] = log_scale + jnp.log(factor)
        width = min(LANES, lanes - c * LANES)
        out = slice(c * LANES, c * LANES + width)
        for i in range(8):
            values = stage[c, i * 16 : (i + 1) * 16, :]
            fwd_ref[i, :, out] = (values * quad_ref[:, at]).astype(BF)[:, :width]
            inv_ref[i, :, out] = (values * live_ref[:, at]).astype(BF)[:, :width]


def legendre_tables(orders, shift, log_start, cosines, quad, live, degrees):
    rows = cosines.shape[0]
    wide = ceil_to(rows, LANES)
    tp = orders.shape[0]

    def spread(row):
        return jnp.pad(row, (0, wide - rows))[None]

    shape = jax.ShapeDtypeStruct((tp, degrees, rows), BF)
    row_spec = pl.BlockSpec((1, wide), lambda i, j: (0, 0))
    lane_spec = pl.BlockSpec((8, LANES), lambda i, j: (i, 0))
    out_spec = pl.BlockSpec((8, 16, rows), lambda i, j: (i, j, 0))
    return call(
        table_kernel,
        "legendre_tables",
        [
            orders.astype(F32),
            shift.astype(F32),
            jnp.pad(log_start, ((0, 0), (0, wide - rows))),
            spread(cosines),
            spread(quad),
            spread(live),
        ],
        [
            lane_spec,
            lane_spec,
            pl.BlockSpec((8, wide), lambda i, j: (i, 0)),
            row_spec,
            row_spec,
            row_spec,
        ],
        [out_spec, out_spec],
        [shape, shape],
        (tp // 8, degrees // 16),
        [
            pltpu.VMEM((8, wide), F32),
            pltpu.VMEM((8, wide), F32),
            pltpu.VMEM((8, wide), F32),
            pltpu.VMEM((wide // LANES, 128, LANES), F32),
        ],
    )


def analyse_modes(x, dft_ref):
    head, tail = x[:SPLIT], x[SPLIT:]
    right = jnp.concatenate([head, head] + [tail] * (LANES // REST), axis=0)
    return [
        lax.dot_general(
            dft_ref[k], right, (((1,), (1,)), ((), ())), preferred_element_type=F32
        )
        for k in range(2)
    ]


def analyse_low_kernel(plan, x_ref, dft_ref, *outs):
    lane = lax.broadcasted_iota(jnp.int32, (1, LANES), 1)
    part = lane // REST
    n, tp = plan.n, plan.tp
    for r in range(plan.rb):
        cosine, sine = analyse_modes(x_ref[r], dft_ref)
        main = jnp.where(lane < SPLIT, cosine[:, :LANES], sine[:, :LANES])
        for o in range(n):
            pieces = [main[o * tp : (o + 1) * tp]]
            for group in range(plan.rest_groups):
                rest = jnp.zeros((8, LANES), F32)
                for i in range(min(4, plan.tb - group * 4)):
                    first = o * tp + (group * 4 + i) * 8
                    rest = jnp.where(part == 2 * i, cosine[first : first + 8, LANES:], rest)
                    rest = jnp.where(part == 2 * i + 1, sine[first : first + 8, LANES:], rest)
                pieces.append(rest)
            outs[o][r] = jnp.concatenate(pieces, axis=0).astype(BF)


def analyse_high_kernel(plan, x_ref, dft_ref, out):
    lane = lax.broadcasted_iota(jnp.int32, (1, LANES), 1)
    even = lane // REST % 2 == 0
    for r in range(plan.rb):
        cosine, sine = analyse_modes(x_ref[r], dft_ref)
        main = jnp.where(lane < SPLIT, cosine[:, :LANES], sine[:, :LANES])
        rest = jnp.where(even, cosine[:, LANES:], sine[:, LANES:])
        out[r] = jnp.concatenate([main, rest], axis=1).astype(BF)


def analyse(plan, kernel, name, x, dft, height, lanes, count):
    shape = jax.ShapeDtypeStruct((plan.rows, height, lanes), BF)
    return call(
        functools.partial(kernel, plan),
        name,
        [x, dft],
        [pl.BlockSpec((plan.rb, plan.fpad, plan.lon), lambda i: (i, 0, 0)), whole(dft.shape)],
        [pl.BlockSpec((plan.rb, height, lanes), lambda i: (i, 0, 0))] * count,
        [shape] * count,
        (plan.rows // plan.rb,),
    )


def analyse_low(plan, x, dft):
    return analyse(plan, analyse_low_kernel, "analyse_low", x, dft, plan.rows1, LANES, plan.n)


def analyse_high(plan, x, dft):
    return analyse(
        plan, analyse_high_kernel, "analyse_high", x, dft, 2 * plan.pairs, 2 * LANES, 1
    )[0]


def unpack(plan, refs, store, height):
    start = 0
    for parts in refs:
        for o, ref in enumerate(parts):

            def step(r, unused, base=o * plan.rows + start, ref=ref):
                at = pl.multiple_of((base + r) * height, 8)
                store[pl.ds(at, height), :] = ref[r].astype(F32)
                return unused

            lax.fori_loop(0, ref.shape[0], step, 0)
        start += parts[0].shape[0]


def repack(plan, refs, store, height):
    start = 0
    for parts in refs:
        for o, ref in enumerate(parts):

            def step(r, unused, base=o * plan.rows + start, ref=ref):
                at = pl.multiple_of((base + r) * height, 8)
                ref[r] = store[pl.ds(at, height), :].astype(BF)
                return unused

            lax.fori_loop(0, ref.shape[0], step, 0)
        start += parts[0].shape[0]


def by_device(plan, refs):
    return [refs[i : i + plan.n] for i in range(0, len(refs), plan.n)]


def rest_row(plan, t):
    block = t // 8
    return plan.tp + 8 * (block // 4) + t % 8


def spectrum_forward_kernel(plan, *refs):
    recv, (fwd, inv, mix, gain) = refs[: plan.n], refs[plan.n : plan.n + 4]
    outs, zin, yout = refs[plan.n + 4 : -2], refs[-2], refs[-1]
    t = pl.program_id(0)

    @pl.when(t == 0)
    def _():
        unpack(plan, [recv], zin, plan.rows1)
        if plan.live_t < plan.tp:
            yout[...] = jnp.zeros_like(yout)

    z = jnp.concatenate(
        [
            zin[pl.ds(t, plan.all_rows, stride=plan.rows1), :],
            zin[pl.ds(rest_row(plan, t), plan.all_rows, stride=plan.rows1), :],
        ],
        axis=1,
    ).astype(BF)
    coeffs = jnp.dot(fwd[0], z, preferred_element_type=F32).astype(BF)
    filtered = (jnp.dot(coeffs, mix[0], preferred_element_type=F32) * gain[...]).astype(BF)
    y = lax.dot_general(
        inv[0], filtered, (((0,), (0,)), ((), ())), preferred_element_type=F32
    )
    for k in range(2):
        yout[pl.ds(k * plan.tp + t, plan.all_rows, stride=plan.rows2), :] = y[
            :, k * LANES : (k + 1) * LANES
        ]

    @pl.when(t == plan.live_t - 1)
    def _():
        repack(plan, by_device(plan, outs), yout, plan.rows2)


def spectrum_backward_kernel(plan, count, *refs):
    recvs = refs[:count]
    fwd, inv, mix, gain = refs[count : count + 4]
    outs, zin, yout = refs[count + 4 : -2], refs[-2], refs[-1]
    t = pl.program_id(0)

    @pl.when(t == 0)
    def _():
        unpack(plan, by_device(plan, recvs), zin, plan.rows2)
        yout[...] = jnp.zeros_like(yout)

    z = jnp.concatenate(
        [
            zin[pl.ds(k * plan.tp + t, plan.all_rows, stride=plan.rows2), :]
            for k in range(2)
        ],
        axis=1,
    ).astype(BF)
    grad = (jnp.dot(inv[0], z, preferred_element_type=F32) * gain[...]).astype(BF)
    back = jnp.dot(grad, mix[0], preferred_element_type=F32).astype(BF)
    y = lax.dot_general(fwd[0], back, (((0,), (0,)), ((), ())), preferred_element_type=F32)
    yout[pl.ds(t, plan.all_rows, stride=plan.rows1), :] = y[:, :LANES]
    where = pl.ds(rest_row(plan, t), plan.all_rows, stride=plan.rows1)
    yout[where, :] = yout[where, :] + y[:, LANES:]

    @pl.when(t == plan.live_t - 1)
    def _():
        repack(plan, [outs], yout, plan.rows1)


def spectrum_specs(plan, mix, gain):
    table = pl.BlockSpec((1, plan.degrees, plan.all_rows), lambda t: (t, 0, 0))
    return [table, table, pl.BlockSpec((1,) + mix.shape[1:], lambda t: ((t // 8) % 4, 0, 0)), whole(gain.shape)]


def spectrum_forward(plan, recv, fwd, inv, mix, gain):
    shapes = [(count, plan.rows2, LANES) for _, count in plan.chunks for _ in range(plan.n)]
    parts = call(
        functools.partial(spectrum_forward_kernel, plan),
        "spectrum_forward",
        [*recv, fwd, inv, mix, gain],
        [whole(r.shape) for r in recv] + spectrum_specs(plan, mix, gain),
        [whole(s) for s in shapes],
        [jax.ShapeDtypeStruct(s, BF) for s in shapes],
        (plan.live_t,),
        [
            pltpu.VMEM((plan.all_rows * plan.rows1, LANES), F32),
            pltpu.VMEM((plan.all_rows * plan.rows2, LANES), F32),
        ],
    )
    return by_device(plan, parts)


def spectrum_backward(plan, recvs, fwd, inv, mix, gain):
    shape = (plan.rows, plan.rows1, LANES)
    flat = [part for parts in recvs for part in parts]
    return call(
        functools.partial(spectrum_backward_kernel, plan, len(flat)),
        "spectrum_backward",
        [*flat, fwd, inv, mix, gain],
        [whole(r.shape) for r in flat] + spectrum_specs(plan, mix, gain),
        [whole(shape)] * plan.n,
        [jax.ShapeDtypeStruct(shape, BF)] * plan.n,
        (plan.live_t,),
        [
            pltpu.VMEM((plan.all_rows * plan.rows2, LANES), F32),
            pltpu.VMEM((plan.all_rows * plan.rows1, LANES), F32),
        ],
    )


def pair_gain(plan, pair, gain):
    row = lax.broadcasted_iota(jnp.int32, (plan.span, 1), 0)
    first, second = plan.low + pair, plan.low - 1
    first_at = pl.multiple_of(first // 8 * 8, 8)
    one = jnp.where(
        row < plan.high - pair,
        gain[first % 8, pl.ds(first_at, plan.span), :],
        gain[second % 8, pl.ds(second // 8 * 8, plan.span), :],
    )
    return jnp.concatenate([one, one], axis=1)


def load_rows(plan, refs, store, height, wide):
    start = 0
    for ref in refs:

        def step(r, unused, start=start, ref=ref):
            at = pl.multiple_of((start + r) * height, 8)
            for w in range(wide):
                store[w, pl.ds(at, height), :] = ref[r, :, w * LANES : (w + 1) * LANES].astype(F32)
            return unused

        lax.fori_loop(0, ref.shape[0], step, 0)
        start += ref.shape[0]

    def clear(r, unused):
        at = pl.multiple_of(r * height, 8)
        for w in range(wide):
            store[w, pl.ds(at, height), :] = jnp.zeros((height, LANES), F32)
        return unused

    lax.fori_loop(start, plan.half_lanes, clear, 0)


def high_partial_kernel(plan, zonal, fwd, out, zin):
    quad = pl.program_id(0)
    block = lax.broadcasted_iota(jnp.int32, (1, LANES), 1) // (2 * REST)

    @pl.when(quad == 0)
    def _():
        load_rows(plan, [zonal], zin, 2 * plan.pairs, 2)

    rest = jnp.zeros((plan.span, LANES), F32)
    for i in range(4):
        pair = quad * 4 + i
        z = jnp.concatenate(
            [
                jnp.concatenate(
                    [
                        zin[w, pl.ds(s * plan.pairs + pair, plan.half_lanes, stride=2 * plan.pairs), :]
                        for s in range(2)
                    ],
                    axis=0,
                )
                for w in range(2)
            ],
            axis=1,
        ).astype(BF)
        coeffs = jnp.dot(fwd[i], z, preferred_element_type=F32)
        out[0, i] = coeffs[:, :LANES].astype(BF)
        rest = rest + jnp.where(block == i, coeffs[:, LANES:], 0.0)
    out[0, 4] = rest.astype(BF)


def high_synthesis_kernel(plan, coeffs, inv, mix, gain, out, yout):
    quad = pl.program_id(0)
    height = 4 * plan.pairs
    for i in range(4):
        pair = quad * 4 + i
        both = jnp.concatenate([coeffs[0, i], coeffs[0, 4]], axis=1)
        filtered = jnp.dot(both, mix[i], preferred_element_type=F32) * pair_gain(plan, pair, gain)
        y = lax.dot_general(
            inv[i], filtered.astype(BF), (((0,), (0,)), ((), ())), preferred_element_type=F32
        )
        for k in range(2):
            for s in range(2):
                yout[pl.ds((2 * k + s) * plan.pairs + pair, plan.half_lanes, stride=height), :] = y[
                    s * plan.half_lanes : (s + 1) * plan.half_lanes, k * LANES : (k + 1) * LANES
                ]

    @pl.when(quad == plan.quads - 1)
    def _():
        def step(r, unused):
            out[r] = yout[pl.ds(pl.multiple_of(r * height, 8), height), :].astype(BF)
            return unused

        lax.fori_loop(0, plan.rows, step, 0)


def high_adjoint_kernel(plan, count, *refs):
    grads, (inv, mix, gain, out, zin) = refs[:count], refs[count:]
    quad = pl.program_id(0)
    height = 4 * plan.pairs

    @pl.when(quad == 0)
    def _():
        load_rows(plan, grads, zin, height, 1)

    rest = jnp.zeros((plan.span, LANES), F32)
    for i in range(4):
        pair = quad * 4 + i
        z = jnp.concatenate(
            [
                jnp.concatenate(
                    [
                        zin[0, pl.ds((2 * k + s) * plan.pairs + pair, plan.half_lanes, stride=height), :]
                        for s in range(2)
                    ],
                    axis=0,
                )
                for k in range(2)
            ],
            axis=1,
        ).astype(BF)
        grad = jnp.dot(inv[i], z, preferred_element_type=F32) * pair_gain(plan, pair, gain)
        back = jnp.dot(grad.astype(BF), mix[i], preferred_element_type=F32)
        out[0, i] = back[:, :LANES].astype(BF)
        rest = rest + back[:, LANES:]
    out[0, 4] = rest.astype(BF)


def high_zonal_kernel(plan, grads, fwd, out, yout):
    quad = pl.program_id(0)
    height = 2 * plan.pairs + 2 * plan.quad_pad
    block = lax.broadcasted_iota(jnp.int32, (1, LANES), 1) // (2 * REST)

    if plan.quad_pad > plan.quads:

        @pl.when(quad == 0)
        def _():
            yout[...] = jnp.zeros_like(yout)

    rest = jnp.zeros((LANES, LANES), F32)
    for i in range(4):
        pair = quad * 4 + i
        both = jnp.concatenate([grads[0, i], grads[0, 4]], axis=1)
        y = lax.dot_general(
            fwd[i], both, (((0,), (0,)), ((), ())), preferred_element_type=F32
        )
        for s in range(2):
            yout[pl.ds(s * plan.pairs + pair, plan.half_lanes, stride=height), :] = y[
                s * plan.half_lanes : (s + 1) * plan.half_lanes, :LANES
            ]
        rest = rest + jnp.where(block == i, y[:, LANES:], 0.0)
    for s in range(2):
        row = 2 * plan.pairs + s * plan.quad_pad + quad
        yout[pl.ds(row, plan.half_lanes, stride=height), :] = rest[
            s * plan.half_lanes : (s + 1) * plan.half_lanes
        ]

    @pl.when(quad == plan.quads - 1)
    def _():
        def step(r, unused):
            out[r] = yout[pl.ds(pl.multiple_of(r * height, 8), height), :].astype(BF)
            return unused

        lax.fori_loop(0, plan.rows, step, 0)


def high_call(plan, kernel, name, whole_in, blocked, fixed, out_shape, out_whole, scratch):
    def quad_spec(array):
        size = array.shape[0] // plan.quads
        rest = array.shape[1:]
        return pl.BlockSpec((size,) + rest, lambda q: (q,) + (0,) * len(rest))

    return call(
        kernel,
        name,
        [*whole_in, *blocked, *fixed],
        [whole(a.shape) for a in whole_in]
        + [quad_spec(a) for a in blocked]
        + [whole(a.shape) for a in fixed],
        whole(out_shape) if out_whole else quad_spec(jax.ShapeDtypeStruct(out_shape, BF)),
        jax.ShapeDtypeStruct(out_shape, BF),
        (plan.quads,),
        [pltpu.VMEM(scratch, F32)],
    )


def high_partial(plan, zonal, fwd):
    return high_call(
        plan, functools.partial(high_partial_kernel, plan), "high_partial", [zonal], [fwd], [],
        (plan.quads, 5, plan.span, LANES), False, (2, plan.half_lanes * 2 * plan.pairs, LANES),
    )


def high_synthesis(plan, coeffs, inv, mix, gain):
    return high_call(
        plan, functools.partial(high_synthesis_kernel, plan), "high_synthesis", [], [coeffs, inv],
        [mix, gain], (plan.rows, 4 * plan.pairs, LANES), True,
        (plan.half_lanes * 4 * plan.pairs, LANES),
    )


def high_adjoint(plan, grads, inv, mix, gain):
    return high_call(
        plan, functools.partial(high_adjoint_kernel, plan, len(grads)), "high_adjoint", grads, [inv],
        [mix, gain], (plan.quads, 5, plan.span, LANES), False,
        (1, plan.half_lanes * 4 * plan.pairs, LANES),
    )


def high_zonal(plan, grads, fwd):
    height = 2 * plan.pairs + 2 * plan.quad_pad
    return high_call(
        plan, functools.partial(high_zonal_kernel, plan), "high_zonal", [], [grads, fwd], [],
        (plan.rows, height, LANES), True, (plan.half_lanes * height, LANES),
    )


def predict_kernel(plan, first, live_ref, x_ref, idft_ref, enc_ref, dec_ref, *refs):
    recv, (high, pred_ref, slope_ref, left, field) = refs[: plan.n], refs[plan.n :]
    c = plan.channels
    wide = plan.n * plan.rows2
    for r in range(plan.rb):
        left[r * c : (r + 1) * c, :wide] = jnp.concatenate([ref[r] for ref in recv], axis=0).T
        left[r * c : (r + 1) * c, wide:] = high[r].T
    field[...] = jnp.dot(left[...], idft_ref[...], preferred_element_type=F32)
    base = first + pl.program_id(0) * plan.rb

    def step(r, unused):
        live = live_ref[base + r]
        x = x_ref[r]
        u = field[pl.ds(pl.multiple_of(r * c, 8), c), :]
        hidden = (jnp.dot(enc_ref[...], x, preferred_element_type=F32) * live).astype(BF)
        phi = 0.5 + 0.5 * lax.erf(u * (1.0 / math.sqrt(2.0)))
        slope = phi + u * jnp.exp(-0.5 * u * u) * (1.0 / math.sqrt(2.0 * math.pi))
        slope_ref[r] = slope.astype(BF)
        block = ((u * phi + hidden.astype(F32)) * live).astype(BF)
        decoded = jnp.dot(dec_ref[...], block, preferred_element_type=F32)
        pred_ref[r] = ((x.astype(F32) + decoded) * live).astype(BF)
        return unused

    lax.fori_loop(0, plan.rb, step, 0)


def predict(plan, chunk, live, x, idft, enc_t, dec_t, recv, high):
    first, count = chunk
    skip = first // plan.rb
    shape = (count, plan.fpad, plan.lon)
    slope_shape = (count, plan.channels, plan.lon)
    return call(
        functools.partial(predict_kernel, plan, first),
        "predict",
        [live, x, idft, enc_t, dec_t, *recv, high],
        [
            pl.BlockSpec(memory_space=pltpu.SMEM),
            pl.BlockSpec((plan.rb,) + shape[1:], lambda i: (i + skip, 0, 0)),
            whole(idft.shape),
            whole(enc_t.shape),
            whole(dec_t.shape),
        ]
        + [pl.BlockSpec((plan.rb, plan.rows2, LANES), lambda i: (i, 0, 0))] * plan.n
        + [pl.BlockSpec((plan.rb,) + high.shape[1:], lambda i: (i + skip, 0, 0))],
        [
            pl.BlockSpec((plan.rb,) + shape[1:], lambda i: (i, 0, 0)),
            pl.BlockSpec((plan.rb,) + slope_shape[1:], lambda i: (i, 0, 0)),
        ],
        [jax.ShapeDtypeStruct(shape, BF), jax.ShapeDtypeStruct(slope_shape, BF)],
        (count // plan.rb,),
        [
            pltpu.VMEM((plan.rb * plan.channels, idft.shape[0]), BF),
            pltpu.VMEM((plan.rb * plan.channels, plan.lon), F32),
        ],
    )


def score_kernel(plan, first, members, area_ref, own_ref, all_ref, obs_ref, slope_ref, idft_ref, dec_ref, *refs):
    grad_ref, outs, (out_high, right) = refs[0], refs[1 : 1 + plan.n], refs[1 + plan.n :]
    c = plan.channels
    base = first + pl.program_id(0) * plan.rb

    def step(r, unused):
        area = area_ref[base + r]
        own = own_ref[r].astype(F32)
        gap = own - obs_ref[r].astype(F32)
        total = gap * lax.rsqrt(jnp.sum(gap * gap, axis=0, keepdims=True) + EPSILON)
        for e in range(members):
            gap = own - all_ref[e, r].astype(F32)
            near = lax.rsqrt(jnp.sum(gap * gap, axis=0, keepdims=True) + EPSILON)
            total = total - gap * (near * (1.0 / members))
        grad = (total * area).astype(BF)
        grad_ref[r] = grad
        block = jnp.dot(dec_ref[...], grad, preferred_element_type=F32)
        right[pl.ds(pl.multiple_of(r * c, 16), c), :] = (
            block * slope_ref[r].astype(F32)
        ).astype(BF)
        return unused

    lax.fori_loop(0, plan.rb, step, 0)
    wide = plan.n * plan.rows2

    def modes(first, last):
        return lax.dot_general(
            idft_ref[first:last, :],
            right[...],
            (((1,), (1,)), ((), ())),
            preferred_element_type=F32,
        ).astype(BF)

    low, high = modes(0, wide), modes(wide, idft_ref.shape[0])
    for r in range(plan.rb):
        for o in range(plan.n):
            outs[o][r] = low[o * plan.rows2 : (o + 1) * plan.rows2, r * c : (r + 1) * c]
        out_high[r] = high[:, r * c : (r + 1) * c]


def score(plan, chunk, area, own, everyone, observed, slope, idft, dec):
    first, count = chunk
    skip = first // plan.rb
    members = everyone.shape[0]
    cell = (plan.rb, plan.fpad, plan.lon)
    out_shape = (count, plan.rows2, LANES)
    high = 4 * plan.pairs
    here = pl.BlockSpec(cell, lambda i: (i, 0, 0))
    grad, *outs = call(
        functools.partial(score_kernel, plan, first, members),
        "score",
        [area, own, everyone, observed, slope, idft, dec],
        [
            pl.BlockSpec(memory_space=pltpu.SMEM),
            here,
            pl.BlockSpec((members,) + cell, lambda i: (0, i, 0, 0)),
            pl.BlockSpec(cell, lambda i: (i + skip, 0, 0)),
            pl.BlockSpec((plan.rb, plan.channels, plan.lon), lambda i: (i, 0, 0)),
            whole(idft.shape),
            whole(dec.shape),
        ],
        [here]
        + [pl.BlockSpec((plan.rb, plan.rows2, LANES), lambda i: (i, 0, 0))] * plan.n
        + [pl.BlockSpec((plan.rb, high, LANES), lambda i: (i, 0, 0))],
        [jax.ShapeDtypeStruct((count,) + cell[1:], BF)]
        + [jax.ShapeDtypeStruct(out_shape, BF)] * plan.n
        + [jax.ShapeDtypeStruct((count, high, LANES), BF)],
        (count // plan.rb,),
        [pltpu.VMEM((plan.rb * plan.channels, plan.lon), BF)],
    )
    return grad, outs[:-1], outs[-1]


def finish_kernel(
    plan, live_ref, grad_ref, main_ref, rest_ref, through_ref, *refs
):
    n, tp, tb = plan.n, plan.tp, plan.tb
    recv, (high_ref, out_ref, left, small, field, field_small) = refs[:n], refs[n:]
    wide, tall, quads = n * tp, 2 * plan.pairs, 2 * plan.quad_pad
    for r in range(plan.rb):
        piece = [ref[r].astype(F32) for ref in recv]
        high = high_ref[r].astype(F32)
        mains = [
            (0, jnp.concatenate([p[:tp] for p in piece], axis=0).T),
            (2 * wide, high[:tall].T),
        ]
        for first, main in mains:
            size = main.shape[1]
            for k in range(2):
                at = first + k * size
                left[r * SPLIT : (r + 1) * SPLIT, at : at + size] = main[
                    k * SPLIT : (k + 1) * SPLIT
                ].astype(BF)
        at = 0
        rests = [
            (
                jnp.concatenate([p[tp + 8 * group : tp + 8 * (group + 1)] for p in piece], axis=0),
                min(4, tb - 4 * group),
            )
            for group in range(plan.rest_groups)
        ] + [(high[tall:], 4)]
        for rest, blocks in rests:
            turned = rest.T.astype(BF)
            for part in range(2 * blocks):
                small[r * REST : (r + 1) * REST, at : at + turned.shape[1]] = turned[
                    part * REST : (part + 1) * REST
                ]
                at += turned.shape[1]
    field[...] = jnp.dot(left[...], main_ref[...], preferred_element_type=F32)
    field_small[...] = jnp.dot(small[...], rest_ref[...], preferred_element_type=F32)
    base = pl.program_id(0) * plan.rb

    def step(r, unused):
        live = live_ref[base + r]
        grad = grad_ref[r]
        through = jnp.dot(through_ref[...], grad, preferred_element_type=F32)
        spectral = jnp.concatenate(
            [
                field[pl.ds(pl.multiple_of(r * SPLIT, 8), SPLIT), :],
                field_small[pl.ds(pl.multiple_of(r * REST, 8), REST), :],
            ],
            axis=0,
        )
        out_ref[r] = ((grad.astype(F32) + through + spectral) * live).astype(BF)
        return unused

    lax.fori_loop(0, plan.rb, step, 0)


def finish(plan, live, grad, main, rest, through, recv, high):
    cell = (plan.rb, plan.fpad, plan.lon)
    here = pl.BlockSpec(cell, lambda i: (i, 0, 0))
    return call(
        functools.partial(finish_kernel, plan),
        "finish",
        [live, grad, main, rest, through, *recv, high],
        [
            pl.BlockSpec(memory_space=pltpu.SMEM),
            here,
            whole(main.shape),
            whole(rest.shape),
            whole(through.shape),
        ]
        + [pl.BlockSpec((plan.rb, plan.rows1, LANES), lambda i: (i, 0, 0))] * plan.n
        + [pl.BlockSpec((plan.rb,) + high.shape[1:], lambda i: (i, 0, 0))],
        here,
        jax.ShapeDtypeStruct((plan.rows, plan.fpad, plan.lon), BF),
        (plan.rows // plan.rb,),
        [
            pltpu.VMEM((plan.rb * SPLIT, main.shape[0]), BF),
            pltpu.VMEM((plan.rb * REST, rest.shape[0]), BF),
            pltpu.VMEM((plan.rb * SPLIT, plan.lon), F32),
            pltpu.VMEM((plan.rb * REST, plan.lon), F32),
        ],
    )


def row_geometry(band_rows, band_len, lat_count):
    band_count = band_rows.shape[0]
    row_index = jnp.arange(band_count * band_len, dtype=jnp.int32)
    row_owner = row_index // band_len
    offset = row_index - row_owner * band_len
    starts = jnp.cumsum(band_rows) - band_rows
    owner_hot = (row_owner[:, None] == jnp.arange(band_count, dtype=jnp.int32)[None, :]).astype(
        jnp.int32
    )
    first_lat = jnp.sum(owner_hot * starts[None, :], axis=1)
    length = jnp.sum(owner_hot * band_rows[None, :], axis=1)
    live_rows = offset < length
    latitude = jnp.minimum(first_lat + offset, lat_count - 1)
    colatitude = latitude.astype(F32) * (math.pi / (lat_count - 1))
    return (live_rows.astype(F32), jnp.cos(colatitude), jnp.sin(colatitude))


def log_diagonal(order):
    index = np.arange(1, LMAX + 1, dtype=np.float64)
    sums = np.concatenate([[0.0], np.cumsum(0.5 * np.log((2 * index + 1) / (2 * index)))])
    return (0.5 * math.log(0.5) + sums[np.minimum(order, LMAX)]).astype(np.float32)


def field_weights(plan, weight):
    select = np.zeros((4, 2 * LANES, plan.fields), np.float32)
    side = np.zeros((4, 2 * LANES, 2), np.float32)
    for b in range(4):
        for k in range(2):
            for f in range(plan.fields):
                first = k * SPLIT + f if f < SPLIT else LANES + (2 * b + k) * REST + f - SPLIT
                select[b, first, f] = 1.0
                side[b, first, k] = 1.0
    spread = jnp.einsum("blf,fc->blc", select, weight, precision=lax.Precision.HIGHEST)
    both = jnp.concatenate([spread, spread], axis=2)
    return (both * np.repeat(side, plan.channels, axis=2)).astype(BF)


def on_device(
    states, observed, band_rows, encoder_weight, mixing_weight, degree_gain, decoder_weight
):
    space = lax.axis_size("space")
    me = lax.axis_index("space")
    fields, band, lon = observed.shape
    channels = encoder_weight.shape[1]
    plan = Plan(space, band, fields, lon, channels, degree_gain.shape[0])
    live, cosines, sines = row_geometry(band_rows, band, NLAT)
    quad = live * sines * (math.pi / (NLAT - 1))
    log_sines = jnp.log(jnp.maximum(sines, 1e-30))
    live_own = lax.dynamic_slice_in_dim(live, me * band, band)
    area = 8.0 * lax.dynamic_slice_in_dim(sines, me * band, band) * live_own

    pad = plan.fpad - fields
    rows = jnp.pad(jnp.transpose(states[0], (1, 0, 2)), ((0, 0), (0, pad), (0, 0)))
    truth = jnp.pad(jnp.transpose(observed, (1, 0, 2)), ((0, 0), (0, pad), (0, 0)))

    enc_f = encoder_weight.astype(F32)
    exact = lax.Precision.HIGHEST
    through_mix = jnp.dot(enc_f, mixing_weight.astype(F32), precision=exact)
    mix = field_weights(plan, through_mix)
    mix_back = jnp.transpose(mix, (0, 2, 1))
    gain = jnp.concatenate([degree_gain, degree_gain], axis=1)
    enc_t = jnp.pad(encoder_weight.T, ((0, 0), (0, pad)))
    dec_t = jnp.pad(decoder_weight.T, ((0, pad), (0, 0)))
    dec = jnp.pad(decoder_weight, ((0, 0), (0, pad)))
    through = jnp.pad(
        jnp.dot(enc_f, decoder_weight.astype(F32), precision=exact), ((0, pad), (0, pad))
    ).astype(BF)

    n, tp, tb = plan.n, plan.tp, plan.tb
    low, high = plan.low_orders(), plan.high_orders()
    low_f, high_f = dft_rows(plan, low, False), dft_rows(plan, high, False)
    low_i, high_i = dft_rows(plan, low, True), dft_rows(plan, high, True)

    def from_here(table):
        table = jnp.asarray(table)
        return lax.dynamic_slice_in_dim(jnp.concatenate([table, table]), me, n)

    low_sums = from_here(low_f.transpose(1, 2, 0, 3))
    low_sums = jnp.transpose(low_sums, (2, 0, 1, 3))
    dft_low = low_sums.reshape(2, n * tp, lon)
    dft_high = jnp.asarray(high_f.reshape(2, 2 * plan.pairs, lon))
    idft = jnp.concatenate(
        [
            from_here(low_i.transpose(1, 0, 2, 3)).reshape(n * 2 * tp, lon),
            jnp.asarray(high_i.reshape(4 * plan.pairs, lon)),
        ]
    )
    dft_main = jnp.concatenate(
        [low_sums.reshape(2 * n * tp, lon), jnp.asarray(high_f.reshape(4 * plan.pairs, lon))]
    )
    low_rest = jnp.transpose(low_sums.reshape(2, n, tb, 8, lon), (2, 0, 1, 3, 4))
    quads = np.zeros((2, 2, plan.quad_pad, 4, lon), low_f.dtype)
    quads[:, :, : plan.quads] = high_f.reshape(2, 2, plan.quads, 4, lon)
    dft_rest = jnp.concatenate(
        [low_rest.reshape(-1, lon), jnp.asarray(quads.transpose(3, 0, 1, 2, 4).reshape(-1, lon))]
    )

    def exchange(parts):
        got = [parts[0]] + [None] * (n - 1)
        for s in range(1, n):
            got[n - s] = lax.ppermute(parts[s], "space", [(i, (i + s) % n) for i in range(n)])
        return got

    recv = exchange(analyse_low(plan, rows, dft_low))
    zonal_high = analyse_high(plan, rows, dft_high)

    half = plan.half_lanes

    def side(value):
        value = jnp.pad(value, (0, half - band))
        return jnp.concatenate([value, value])

    def sides(pair_values):
        return jnp.asarray(np.repeat(pair_values.T, half, axis=1))

    own = [
        side(lax.dynamic_slice_in_dim(v, me * band, band)) for v in (cosines, quad, live, log_sines)
    ]
    shift = np.stack([plan.low + np.arange(plan.pairs), np.full(plan.pairs, plan.low - 1)])
    start = sides(log_diagonal(high)) + sides(high.astype(np.float32)) * own[3][None, :]
    high_fwd, high_inv = legendre_tables(
        sides(high), sides(shift), start, own[0], own[1], own[2], plan.span
    )
    high_coeffs = lax.psum(high_partial(plan, zonal_high, high_fwd), "space")

    orders = lax.dynamic_index_in_dim(jnp.asarray(low, jnp.int32), me, keepdims=False)
    diagonal = lax.dynamic_index_in_dim(jnp.asarray(log_diagonal(low)), me, keepdims=False)
    orders_wide = jnp.broadcast_to(orders[:, None], (tp, LANES))
    ordered = [from_here(v.reshape(n, band)).reshape(-1) for v in (cosines, quad, live, log_sines)]
    start = diagonal[:, None] + orders.astype(F32)[:, None] * ordered[3][None, :]
    low_fwd, low_inv = legendre_tables(
        orders_wide, jnp.zeros_like(orders_wide), start, *ordered[:3], plan.degrees
    )

    spectrum = spectrum_forward(plan, recv, low_fwd, low_inv, mix, gain)
    synth = [exchange(part) for part in spectrum]
    reach = ceil_to(plan.low + plan.pairs + plan.span, 8)
    longer = jnp.pad(degree_gain, ((0, reach + 8 - degree_gain.shape[0]), (0, 0)))
    gain_long = jnp.stack([longer[s : s + reach] for s in range(8)])
    synth_high = high_synthesis(plan, high_coeffs, high_inv, mix, gain_long)

    def after(value, other):
        return lax.optimization_barrier((value, other))

    predictions, grads, returned, returned_high = [], [], [], []
    gathered = []
    for i, chunk in enumerate(plan.chunks):
        pred, slope = predict(
            plan, chunk, live_own, rows, idft, enc_t, dec_t, synth[i], synth_high
        )
        predictions.append(pred)
        gathered.append((lax.all_gather(pred[None], "member", axis=0, tiled=True), slope))
    for i, chunk in enumerate(plan.chunks):
        pred, (everyone, slope) = predictions[i], gathered[i]
        if i:
            pred, returned[i - 1] = after(pred, returned[i - 1])
        grad, out, out_high = score(plan, chunk, area, pred, everyone, truth, slope, idft, dec)
        grads.append(grad)
        returned_high.append(out_high)
        if i == len(plan.chunks) - 1:
            high_grads = high_adjoint(plan, returned_high, high_inv, mix_back, gain_long)
            out, high_grads = after(out, high_grads)
            high_grads = lax.psum(high_grads, "space")
        returned.append(exchange(out))

    parts = spectrum_backward(plan, returned, low_fwd, low_inv, mix_back, gain)
    parts, high_grads = after(parts, high_grads)
    zonal_grad = high_zonal(plan, high_grads, high_fwd)
    last = exchange(parts)
    state_grad = finish(
        plan, live_own, jnp.concatenate(grads), dft_main, dft_rest, through, last, zonal_grad
    )

    def outward(block):
        return jnp.transpose(block[:, :fields], (1, 0, 2))[None]

    return (outward(jnp.concatenate(predictions)), outward(state_grad))


def solution(mesh):
    in_specs = (P("member", None, "space", None), P(None, "space", None), P(), P(), P(), P(), P())
    out_specs = (P("member", None, "space", None), P("member", None, "space", None))
    return jax.shard_map(
        on_device, mesh=mesh, in_specs=in_specs, out_specs=out_specs, check_vma=False
    )
```

```python
import functools
import math

import jax
import jax.numpy as jnp
import ml_dtypes
import numpy as np
from jax import lax
from jax.experimental import pallas as pl
from jax.experimental.pallas import tpu as pltpu
from jax.sharding import PartitionSpec as P

NLAT = 361
LMAX = 360
EPSILON = 1e-05
GROUP = 256
SPLIT = 64
REST = 16
LANES = 128
NONE = 1 << 14
VMEM = 60 * 1024 * 1024
BF = jnp.bfloat16
F32 = jnp.float32


def ceil_to(value, step):
    return -(-value // step) * step


class Plan:
    def __init__(self, space, band, fields, lon, channels, degrees):
        self.n, self.rows, self.fields, self.lon = space, band, fields, lon
        self.channels, self.degrees = channels, degrees
        self.all_rows = space * band
        self.fpad = SPLIT + REST
        self.live_t = -(-GROUP // space)
        self.tp = ceil_to(self.live_t, 8)
        self.tb = self.tp // 8
        self.rest_groups = -(-self.tb // 4)
        self.rows1 = self.tp + 8 * self.rest_groups
        self.rows2 = 2 * self.tp
        self.low = space * self.live_t
        self.step = max(k for k in (1, 2, 4) if self.live_t % k == 0)
        self.high = LMAX + 1 - self.low
        self.pairs = ceil_to(-(-self.high // 2), 8)
        self.quads = self.pairs // 4
        self.quad_pad = ceil_to(self.quads, 8)
        self.span = ceil_to(self.high + 1, 16)
        self.half = ceil_to(band, 16)
        self.half_lanes = LANES // 2
        self.rb = max(k for k in range(1, 9) if band % k == 0)
        blocks = band // self.rb
        half = blocks // 2
        counts = [count for count in (1, blocks - 1 - half, half) if count > 0]
        self.chunks = []
        start = 0
        for count in counts:
            self.chunks.append((start * self.rb, count * self.rb))
            start += count

    def low_orders(self):
        device = np.arange(self.n)[:, None]
        position = np.arange(self.tp)[None, :]
        return np.where(position < self.live_t, device * self.live_t + position, NONE)

    def high_orders(self):
        pair = np.arange(self.pairs)
        first = np.where(2 * pair < self.high, self.low + pair, NONE)
        second = np.where(2 * pair < self.high - 1, LMAX - pair, NONE)
        return np.stack([first, second])


def dft_rows(plan, order, inverse):
    live = (order <= LMAX)[..., None]
    turn = (np.where(order <= LMAX, order, 0)[..., None] * np.arange(plan.lon)) % plan.lon
    angle = turn * (2.0 * math.pi / plan.lon)
    if inverse:
        scale = np.where((order == 0) | (2 * order == plan.lon), 1.0, 2.0)[..., None]
    else:
        scale = 1.0 / plan.lon
    rows = np.stack([np.cos(angle) * scale, -np.sin(angle) * scale]) * live
    return rows.astype(ml_dtypes.bfloat16)


def params(**more):
    return pltpu.CompilerParams(vmem_limit_bytes=VMEM, **more)


def call(kernel, name, operands, in_specs, out_specs, out_shape, grid, scratch=()):
    results = out_shape if isinstance(out_shape, (list, tuple)) else [out_shape]
    moved = sum(math.prod(a.shape) * a.dtype.itemsize for a in list(operands) + list(results))
    return pl.pallas_call(
        kernel,
        grid=grid,
        in_specs=in_specs,
        out_specs=out_specs,
        out_shape=out_shape,
        scratch_shapes=list(scratch),
        compiler_params=params(),
        cost_estimate=pl.CostEstimate(flops=0, transcendentals=0, bytes_accessed=4 * moved),
        name=name,
    )(*operands)


def whole(shape):
    return pl.BlockSpec(shape, lambda *_: (0,) * len(shape))


def table_kernel(m_ref, shift_ref, start_ref, cos_ref, quad_ref, live_ref, fwd_ref, inv_ref, stage):
    lanes = fwd_ref.shape[2]
    order, shift = m_ref[...], shift_ref[...]
    square = order * order
    parts = [slice(c, c + LANES) for c in range(0, start_ref.shape[1], LANES)]

    def block(index, state):
        before = state[0]
        at_row = pl.multiple_of(index * 16, 16)
        ups, backs, pasts, onsets, keeps = [], [], [], [], []
        for p in range(16):
            deg = shift + (index * 16 + p).astype(F32)
            ratio = jnp.maximum((deg * deg - square) / (4.0 * deg * deg - 1.0), 0.0)
            root = lax.rsqrt(jnp.maximum(ratio, 1e-20))
            ups.append(root)
            backs.append(before)
            before = ratio * root
            pasts.append(order < deg)
            onsets.append(jnp.where(order == deg, 1.0, 0.0))
            keeps.append(deg <= LMAX)
        after = [before]
        for c, at in enumerate(parts):
            first, second, log_scale = state[1 + 3 * c : 4 + 3 * c]
            cosine = cos_ref[:, at]
            scale = jnp.exp(log_scale)
            for p in range(16):
                current = jnp.where(
                    pasts[p], ups[p] * (cosine * first - backs[p] * second), onsets[p]
                )
                stage[c, pl.ds(p, 8, stride=16), :] = jnp.where(keeps[p], current * scale, 0.0)
                second = first
                first = current
            size = jnp.maximum(jnp.abs(first), jnp.abs(second))
            factor = jnp.where(size > 1.0, size, 1.0)
            after += [first / factor, second / factor, log_scale + jnp.log(factor)]
        for c, at in enumerate(parts):
            width = min(LANES, lanes - c * LANES)
            out = slice(c * LANES, c * LANES + width)
            for i in range(8):
                values = stage[c, i * 16 : (i + 1) * 16, :]
                fwd_ref[i, pl.ds(at_row, 16), out] = (values * quad_ref[:, at]).astype(BF)[:, :width]
                inv_ref[i, pl.ds(at_row, 16), out] = (values * live_ref[:, at]).astype(BF)[:, :width]
        return tuple(after)

    zero = jnp.zeros((8, LANES), F32)
    state = [zero]
    for at in parts:
        state += [zero, zero, start_ref[:, at]]
    lax.fori_loop(0, fwd_ref.shape[1] // 16, block, tuple(state))


def legendre_tables(orders, shift, log_start, cosines, quad, live, degrees):
    rows = cosines.shape[0]
    wide = ceil_to(rows, LANES)
    tp = orders.shape[0]

    def spread(row):
        return jnp.pad(row, (0, wide - rows))[None]

    shape = jax.ShapeDtypeStruct((tp, degrees, rows), BF)
    row_spec = whole((1, wide))
    lane_spec = pl.BlockSpec((8, LANES), lambda i: (i, 0))
    out_spec = pl.BlockSpec((8, degrees, rows), lambda i: (i, 0, 0))
    return call(
        table_kernel,
        "legendre_tables",
        [
            orders.astype(F32),
            shift.astype(F32),
            jnp.pad(log_start, ((0, 0), (0, wide - rows))),
            spread(cosines),
            spread(quad),
            spread(live),
        ],
        [
            lane_spec,
            lane_spec,
            pl.BlockSpec((8, wide), lambda i: (i, 0)),
            row_spec,
            row_spec,
            row_spec,
        ],
        [out_spec, out_spec],
        [shape, shape],
        (tp // 8,),
        [pltpu.VMEM((wide // LANES, 128, LANES), F32)],
    )


def analyse_modes(x, dft_ref):
    head, tail = x[:SPLIT], x[SPLIT:]
    right = jnp.concatenate([head, head] + [tail] * (LANES // REST), axis=0)
    return [
        lax.dot_general(
            dft_ref[k], right, (((1,), (1,)), ((), ())), preferred_element_type=F32
        )
        for k in range(2)
    ]


def analyse_low_kernel(plan, x_ref, dft_ref, *outs):
    lane = lax.broadcasted_iota(jnp.int32, (1, LANES), 1)
    part = lane // REST
    n, tp = plan.n, plan.tp
    for r in range(plan.rb):
        cosine, sine = analyse_modes(x_ref[r], dft_ref)
        main = jnp.where(lane < SPLIT, cosine[:, :LANES], sine[:, :LANES])
        for o in range(n):
            pieces = [main[o * tp : (o + 1) * tp]]
            for group in range(plan.rest_groups):
                rest = jnp.zeros((8, LANES), F32)
                for i in range(min(4, plan.tb - group * 4)):
                    first = o * tp + (group * 4 + i) * 8
                    rest = jnp.where(part == 2 * i, cosine[first : first + 8, LANES:], rest)
                    rest = jnp.where(part == 2 * i + 1, sine[first : first + 8, LANES:], rest)
                pieces.append(rest)
            outs[o][r] = jnp.concatenate(pieces, axis=0).astype(BF)


def analyse_high_kernel(plan, x_ref, dft_ref, out):
    lane = lax.broadcasted_iota(jnp.int32, (1, LANES), 1)
    even = lane // REST % 2 == 0
    for r in range(plan.rb):
        cosine, sine = analyse_modes(x_ref[r], dft_ref)
        main = jnp.where(lane < SPLIT, cosine[:, :LANES], sine[:, :LANES])
        rest = jnp.where(even, cosine[:, LANES:], sine[:, LANES:])
        out[r] = jnp.concatenate([main, rest], axis=1).astype(BF)


def analyse(plan, kernel, name, x, dft, height, lanes, count):
    shape = jax.ShapeDtypeStruct((plan.rows, height, lanes), BF)
    return call(
        functools.partial(kernel, plan),
        name,
        [x, dft],
        [pl.BlockSpec((plan.rb, plan.fpad, plan.lon), lambda i: (i, 0, 0)), whole(dft.shape)],
        [pl.BlockSpec((plan.rb, height, lanes), lambda i: (i, 0, 0))] * count,
        [shape] * count,
        (plan.rows // plan.rb,),
    )


def analyse_low(plan, x, dft):
    return analyse(plan, analyse_low_kernel, "analyse_low", x, dft, plan.rows1, LANES, plan.n)


def analyse_high(plan, x, dft):
    return analyse(
        plan, analyse_high_kernel, "analyse_high", x, dft, 2 * plan.pairs, 2 * LANES, 1
    )[0]


def unpack(plan, refs, store, height):
    start = 0
    for parts in refs:
        for o, ref in enumerate(parts):

            def step(r, unused, base=o * plan.rows + start, ref=ref):
                at = pl.multiple_of((base + r) * height, 8)
                store[pl.ds(at, height), :] = ref[r].astype(F32)
                return unused

            lax.fori_loop(0, ref.shape[0], step, 0)
        start += parts[0].shape[0]


def repack(plan, refs, store, height):
    start = 0
    for parts in refs:
        for o, ref in enumerate(parts):

            def step(r, unused, base=o * plan.rows + start, ref=ref):
                at = pl.multiple_of((base + r) * height, 8)
                ref[r] = store[pl.ds(at, height), :].astype(BF)
                return unused

            lax.fori_loop(0, ref.shape[0], step, 0)
        start += parts[0].shape[0]


def by_device(plan, refs):
    return [refs[i : i + plan.n] for i in range(0, len(refs), plan.n)]


def rest_row(plan, t):
    block = t // 8
    return plan.tp + 8 * (block // 4) + t % 8


def spectrum_forward_kernel(plan, *refs):
    recv, (fwd, inv, mix, gain) = refs[: plan.n], refs[plan.n : plan.n + 4]
    outs, zin, yout = refs[plan.n + 4 : -2], refs[-2], refs[-1]
    step = pl.program_id(0)

    @pl.when(step == 0)
    def _():
        unpack(plan, [recv], zin, plan.rows1)
        if plan.live_t < plan.tp:
            yout[...] = jnp.zeros_like(yout)

    for i in range(plan.step):
        t = step * plan.step + i
        z = jnp.concatenate(
            [
                zin[pl.ds(t, plan.all_rows, stride=plan.rows1), :],
                zin[pl.ds(rest_row(plan, t), plan.all_rows, stride=plan.rows1), :],
            ],
            axis=1,
        ).astype(BF)
        coeffs = jnp.dot(fwd[i], z, preferred_element_type=F32).astype(BF)
        filtered = (jnp.dot(coeffs, mix[0], preferred_element_type=F32) * gain[...]).astype(BF)
        y = lax.dot_general(
            inv[i], filtered, (((0,), (0,)), ((), ())), preferred_element_type=F32
        )
        for k in range(2):
            yout[pl.ds(k * plan.tp + t, plan.all_rows, stride=plan.rows2), :] = y[
                :, k * LANES : (k + 1) * LANES
            ]

    @pl.when(step == plan.live_t // plan.step - 1)
    def _():
        repack(plan, by_device(plan, outs), yout, plan.rows2)


def spectrum_backward_kernel(plan, count, *refs):
    recvs = refs[:count]
    fwd, inv, mix, gain = refs[count : count + 4]
    outs, zin, yout = refs[count + 4 : -2], refs[-2], refs[-1]
    step = pl.program_id(0)

    @pl.when(step == 0)
    def _():
        unpack(plan, by_device(plan, recvs), zin, plan.rows2)
        yout[...] = jnp.zeros_like(yout)

    for i in range(plan.step):
        t = step * plan.step + i
        z = jnp.concatenate(
            [
                zin[pl.ds(k * plan.tp + t, plan.all_rows, stride=plan.rows2), :]
                for k in range(2)
            ],
            axis=1,
        ).astype(BF)
        grad = (jnp.dot(inv[i], z, preferred_element_type=F32) * gain[...]).astype(BF)
        back = jnp.dot(grad, mix[0], preferred_element_type=F32).astype(BF)
        y = lax.dot_general(fwd[i], back, (((0,), (0,)), ((), ())), preferred_element_type=F32)
        yout[pl.ds(t, plan.all_rows, stride=plan.rows1), :] = y[:, :LANES]
        where = pl.ds(rest_row(plan, t), plan.all_rows, stride=plan.rows1)
        yout[where, :] = yout[where, :] + y[:, LANES:]

    @pl.when(step == plan.live_t // plan.step - 1)
    def _():
        repack(plan, [outs], yout, plan.rows1)


def spectrum_specs(plan, mix, gain):
    table = pl.BlockSpec((plan.step, plan.degrees, plan.all_rows), lambda t: (t, 0, 0))
    return [table, table, pl.BlockSpec((1,) + mix.shape[1:], lambda t: ((t * plan.step // 8) % 4, 0, 0)), whole(gain.shape)]


def spectrum_forward(plan, recv, fwd, inv, mix, gain):
    shapes = [(count, plan.rows2, LANES) for _, count in plan.chunks for _ in range(plan.n)]
    parts = call(
        functools.partial(spectrum_forward_kernel, plan),
        "spectrum_forward",
        [*recv, fwd, inv, mix, gain],
        [whole(r.shape) for r in recv] + spectrum_specs(plan, mix, gain),
        [whole(s) for s in shapes],
        [jax.ShapeDtypeStruct(s, BF) for s in shapes],
        (plan.live_t // plan.step,),
        [
            pltpu.VMEM((plan.all_rows * plan.rows1, LANES), F32),
            pltpu.VMEM((plan.all_rows * plan.rows2, LANES), F32),
        ],
    )
    return by_device(plan, parts)


def spectrum_backward(plan, recvs, fwd, inv, mix, gain):
    shape = (plan.rows, plan.rows1, LANES)
    flat = [part for parts in recvs for part in parts]
    return call(
        functools.partial(spectrum_backward_kernel, plan, len(flat)),
        "spectrum_backward",
        [*flat, fwd, inv, mix, gain],
        [whole(r.shape) for r in flat] + spectrum_specs(plan, mix, gain),
        [whole(shape)] * plan.n,
        [jax.ShapeDtypeStruct(shape, BF)] * plan.n,
        (plan.live_t // plan.step,),
        [
            pltpu.VMEM((plan.all_rows * plan.rows2, LANES), F32),
            pltpu.VMEM((plan.all_rows * plan.rows1, LANES), F32),
        ],
    )


def pair_gain(plan, pair, gain):
    row = lax.broadcasted_iota(jnp.int32, (plan.span, 1), 0)
    first, second = plan.low + pair, plan.low - 1
    first_at = pl.multiple_of(first // 8 * 8, 8)
    one = jnp.where(
        row < plan.high - pair,
        gain[first % 8, pl.ds(first_at, plan.span), :],
        gain[second % 8, pl.ds(second // 8 * 8, plan.span), :],
    )
    return jnp.concatenate([one, one], axis=1)


def load_rows(plan, refs, store, height, wide):
    start = 0
    for ref in refs:

        def step(r, unused, start=start, ref=ref):
            at = pl.multiple_of((start + r) * height, 8)
            for w in range(wide):
                store[w, pl.ds(at, height), :] = ref[r, :, w * LANES : (w + 1) * LANES].astype(F32)
            return unused

        lax.fori_loop(0, ref.shape[0], step, 0)
        start += ref.shape[0]

    def clear(r, unused):
        at = pl.multiple_of(r * height, 8)
        for w in range(wide):
            store[w, pl.ds(at, height), :] = jnp.zeros((height, LANES), F32)
        return unused

    lax.fori_loop(start, plan.half_lanes, clear, 0)


def high_partial_kernel(plan, zonal, fwd, out, zin):
    quad = pl.program_id(0)
    block = lax.broadcasted_iota(jnp.int32, (1, LANES), 1) // (2 * REST)

    @pl.when(quad == 0)
    def _():
        load_rows(plan, [zonal], zin, 2 * plan.pairs, 2)

    rest = jnp.zeros((plan.span, LANES), F32)
    for i in range(4):
        pair = quad * 4 + i
        z = jnp.concatenate(
            [
                jnp.concatenate(
                    [
                        zin[w, pl.ds(s * plan.pairs + pair, plan.half_lanes, stride=2 * plan.pairs), :]
                        for s in range(2)
                    ],
                    axis=0,
                )
                for w in range(2)
            ],
            axis=1,
        ).astype(BF)
        coeffs = jnp.dot(fwd[i], z, preferred_element_type=F32)
        out[0, i] = coeffs[:, :LANES].astype(BF)
        rest = rest + jnp.where(block == i, coeffs[:, LANES:], 0.0)
    out[0, 4] = rest.astype(BF)


def high_synthesis_kernel(plan, coeffs, inv, mix, gain, out, yout):
    quad = pl.program_id(0)
    height = 4 * plan.pairs
    for i in range(4):
        pair = quad * 4 + i
        both = jnp.concatenate([coeffs[0, i], coeffs[0, 4]], axis=1)
        filtered = jnp.dot(both, mix[i], preferred_element_type=F32) * pair_gain(plan, pair, gain)
        y = lax.dot_general(
            inv[i], filtered.astype(BF), (((0,), (0,)), ((), ())), preferred_element_type=F32
        )
        for k in range(2):
            for s in range(2):
                yout[pl.ds((2 * k + s) * plan.pairs + pair, plan.half_lanes, stride=height), :] = y[
                    s * plan.half_lanes : (s + 1) * plan.half_lanes, k * LANES : (k + 1) * LANES
                ]

    @pl.when(quad == plan.quads - 1)
    def _():
        def step(r, unused):
            out[r] = yout[pl.ds(pl.multiple_of(r * height, 8), height), :].astype(BF)
            return unused

        lax.fori_loop(0, plan.rows, step, 0)


def high_adjoint_kernel(plan, count, *refs):
    grads, (inv, mix, gain, out, zin) = refs[:count], refs[count:]
    quad = pl.program_id(0)
    height = 4 * plan.pairs

    @pl.when(quad == 0)
    def _():
        load_rows(plan, grads, zin, height, 1)

    rest = jnp.zeros((plan.span, LANES), F32)
    for i in range(4):
        pair = quad * 4 + i
        z = jnp.concatenate(
            [
                jnp.concatenate(
                    [
                        zin[0, pl.ds((2 * k + s) * plan.pairs + pair, plan.half_lanes, stride=height), :]
                        for s in range(2)
                    ],
                    axis=0,
                )
                for k in range(2)
            ],
            axis=1,
        ).astype(BF)
        grad = jnp.dot(inv[i], z, preferred_element_type=F32) * pair_gain(plan, pair, gain)
        back = jnp.dot(grad.astype(BF), mix[i], preferred_element_type=F32)
        out[0, i] = back[:, :LANES].astype(BF)
        rest = rest + back[:, LANES:]
    out[0, 4] = rest.astype(BF)


def high_zonal_kernel(plan, grads, fwd, out, yout):
    quad = pl.program_id(0)
    height = 2 * plan.pairs + 2 * plan.quad_pad
    block = lax.broadcasted_iota(jnp.int32, (1, LANES), 1) // (2 * REST)

    if plan.quad_pad > plan.quads:

        @pl.when(quad == 0)
        def _():
            yout[...] = jnp.zeros_like(yout)

    rest = jnp.zeros((LANES, LANES), F32)
    for i in range(4):
        pair = quad * 4 + i
        both = jnp.concatenate([grads[0, i], grads[0, 4]], axis=1)
        y = lax.dot_general(
            fwd[i], both, (((0,), (0,)), ((), ())), preferred_element_type=F32
        )
        for s in range(2):
            yout[pl.ds(s * plan.pairs + pair, plan.half_lanes, stride=height), :] = y[
                s * plan.half_lanes : (s + 1) * plan.half_lanes, :LANES
            ]
        rest = rest + jnp.where(block == i, y[:, LANES:], 0.0)
    for s in range(2):
        row = 2 * plan.pairs + s * plan.quad_pad + quad
        yout[pl.ds(row, plan.half_lanes, stride=height), :] = rest[
            s * plan.half_lanes : (s + 1) * plan.half_lanes
        ]

    @pl.when(quad == plan.quads - 1)
    def _():
        def step(r, unused):
            out[r] = yout[pl.ds(pl.multiple_of(r * height, 8), height), :].astype(BF)
            return unused

        lax.fori_loop(0, plan.rows, step, 0)


def high_call(plan, kernel, name, whole_in, blocked, fixed, out_shape, out_whole, scratch):
    def quad_spec(array):
        size = array.shape[0] // plan.quads
        rest = array.shape[1:]
        return pl.BlockSpec((size,) + rest, lambda q: (q,) + (0,) * len(rest))

    return call(
        kernel,
        name,
        [*whole_in, *blocked, *fixed],
        [whole(a.shape) for a in whole_in]
        + [quad_spec(a) for a in blocked]
        + [whole(a.shape) for a in fixed],
        whole(out_shape) if out_whole else quad_spec(jax.ShapeDtypeStruct(out_shape, BF)),
        jax.ShapeDtypeStruct(out_shape, BF),
        (plan.quads,),
        [pltpu.VMEM(scratch, F32)],
    )


def high_partial(plan, zonal, fwd):
    return high_call(
        plan, functools.partial(high_partial_kernel, plan), "high_partial", [zonal], [fwd], [],
        (plan.quads, 5, plan.span, LANES), False, (2, plan.half_lanes * 2 * plan.pairs, LANES),
    )


def high_synthesis(plan, coeffs, inv, mix, gain):
    return high_call(
        plan, functools.partial(high_synthesis_kernel, plan), "high_synthesis", [], [coeffs, inv],
        [mix, gain], (plan.rows, 4 * plan.pairs, LANES), True,
        (plan.half_lanes * 4 * plan.pairs, LANES),
    )


def high_adjoint(plan, grads, inv, mix, gain):
    return high_call(
        plan, functools.partial(high_adjoint_kernel, plan, len(grads)), "high_adjoint", grads, [inv],
        [mix, gain], (plan.quads, 5, plan.span, LANES), False,
        (1, plan.half_lanes * 4 * plan.pairs, LANES),
    )


def high_zonal(plan, grads, fwd):
    height = 2 * plan.pairs + 2 * plan.quad_pad
    return high_call(
        plan, functools.partial(high_zonal_kernel, plan), "high_zonal", [], [grads, fwd], [],
        (plan.rows, height, LANES), True, (plan.half_lanes * height, LANES),
    )


def predict_kernel(plan, first, live_ref, x_ref, idft_ref, enc_ref, dec_ref, *refs):
    recv, (high, pred_ref, slope_ref, left, field) = refs[: plan.n], refs[plan.n :]
    c = plan.channels
    wide = plan.n * plan.rows2
    for r in range(plan.rb):
        left[r * c : (r + 1) * c, :wide] = jnp.concatenate([ref[r] for ref in recv], axis=0).T
        left[r * c : (r + 1) * c, wide:] = high[r].T
    field[...] = jnp.dot(left[...], idft_ref[...], preferred_element_type=F32)
    base = first + pl.program_id(0) * plan.rb

    def step(r, unused):
        live = live_ref[base + r]
        x = x_ref[r]
        u = field[pl.ds(pl.multiple_of(r * c, 8), c), :]
        hidden = (jnp.dot(enc_ref[...], x, preferred_element_type=F32) * live).astype(BF)
        phi = 0.5 + 0.5 * lax.erf(u * (1.0 / math.sqrt(2.0)))
        slope = phi + u * jnp.exp(-0.5 * u * u) * (1.0 / math.sqrt(2.0 * math.pi))
        slope_ref[r] = slope.astype(BF)
        block = ((u * phi + hidden.astype(F32)) * live).astype(BF)
        decoded = jnp.dot(dec_ref[...], block, preferred_element_type=F32)
        pred_ref[r] = ((x.astype(F32) + decoded) * live).astype(BF)
        return unused

    lax.fori_loop(0, plan.rb, step, 0)


def predict(plan, chunk, live, x, idft, enc_t, dec_t, recv, high):
    first, count = chunk
    skip = first // plan.rb
    shape = (count, plan.fpad, plan.lon)
    slope_shape = (count, plan.channels, plan.lon)
    return call(
        functools.partial(predict_kernel, plan, first),
        "predict",
        [live, x, idft, enc_t, dec_t, *recv, high],
        [
            pl.BlockSpec(memory_space=pltpu.SMEM),
            pl.BlockSpec((plan.rb,) + shape[1:], lambda i: (i + skip, 0, 0)),
            whole(idft.shape),
            whole(enc_t.shape),
            whole(dec_t.shape),
        ]
        + [pl.BlockSpec((plan.rb, plan.rows2, LANES), lambda i: (i, 0, 0))] * plan.n
        + [pl.BlockSpec((plan.rb,) + high.shape[1:], lambda i: (i + skip, 0, 0))],
        [
            pl.BlockSpec((plan.rb,) + shape[1:], lambda i: (i, 0, 0)),
            pl.BlockSpec((plan.rb,) + slope_shape[1:], lambda i: (i, 0, 0)),
        ],
        [jax.ShapeDtypeStruct(shape, BF), jax.ShapeDtypeStruct(slope_shape, BF)],
        (count // plan.rb,),
        [
            pltpu.VMEM((plan.rb * plan.channels, idft.shape[0]), BF),
            pltpu.VMEM((plan.rb * plan.channels, plan.lon), F32),
        ],
    )


def score_kernel(plan, first, members, area_ref, own_ref, all_ref, obs_ref, slope_ref, idft_ref, dec_ref, *refs):
    grad_ref, outs, (out_high, right) = refs[0], refs[1 : 1 + plan.n], refs[1 + plan.n :]
    c = plan.channels
    base = first + pl.program_id(0) * plan.rb

    def step(r, unused):
        area = area_ref[base + r]
        own = own_ref[r].astype(F32)
        gap = own - obs_ref[r].astype(F32)
        total = gap * lax.rsqrt(jnp.sum(gap * gap, axis=0, keepdims=True) + EPSILON)
        for e in range(members):
            gap = own - all_ref[e, r].astype(F32)
            near = lax.rsqrt(jnp.sum(gap * gap, axis=0, keepdims=True) + EPSILON)
            total = total - gap * (near * (1.0 / members))
        grad = (total * area).astype(BF)
        grad_ref[r] = grad
        block = jnp.dot(dec_ref[...], grad, preferred_element_type=F32)
        right[pl.ds(pl.multiple_of(r * c, 16), c), :] = (
            block * slope_ref[r].astype(F32)
        ).astype(BF)
        return unused

    lax.fori_loop(0, plan.rb, step, 0)
    wide = plan.n * plan.rows2

    def modes(first, last):
        return lax.dot_general(
            idft_ref[first:last, :],
            right[...],
            (((1,), (1,)), ((), ())),
            preferred_element_type=F32,
        ).astype(BF)

    low, high = modes(0, wide), modes(wide, idft_ref.shape[0])
    for r in range(plan.rb):
        for o in range(plan.n):
            outs[o][r] = low[o * plan.rows2 : (o + 1) * plan.rows2, r * c : (r + 1) * c]
        out_high[r] = high[:, r * c : (r + 1) * c]


def score(plan, chunk, area, own, everyone, observed, slope, idft, dec):
    first, count = chunk
    skip = first // plan.rb
    members = everyone.shape[0]
    cell = (plan.rb, plan.fpad, plan.lon)
    out_shape = (count, plan.rows2, LANES)
    high = 4 * plan.pairs
    here = pl.BlockSpec(cell, lambda i: (i, 0, 0))
    grad, *outs = call(
        functools.partial(score_kernel, plan, first, members),
        "score",
        [area, own, everyone, observed, slope, idft, dec],
        [
            pl.BlockSpec(memory_space=pltpu.SMEM),
            here,
            pl.BlockSpec((members,) + cell, lambda i: (0, i, 0, 0)),
            pl.BlockSpec(cell, lambda i: (i + skip, 0, 0)),
            pl.BlockSpec((plan.rb, plan.channels, plan.lon), lambda i: (i, 0, 0)),
            whole(idft.shape),
            whole(dec.shape),
        ],
        [here]
        + [pl.BlockSpec((plan.rb, plan.rows2, LANES), lambda i: (i, 0, 0))] * plan.n
        + [pl.BlockSpec((plan.rb, high, LANES), lambda i: (i, 0, 0))],
        [jax.ShapeDtypeStruct((count,) + cell[1:], BF)]
        + [jax.ShapeDtypeStruct(out_shape, BF)] * plan.n
        + [jax.ShapeDtypeStruct((count, high, LANES), BF)],
        (count // plan.rb,),
        [pltpu.VMEM((plan.rb * plan.channels, plan.lon), BF)],
    )
    return grad, outs[:-1], outs[-1]


def finish_kernel(
    plan, live_ref, grad_ref, main_ref, rest_ref, through_ref, *refs
):
    n, tp, tb = plan.n, plan.tp, plan.tb
    recv, (high_ref, out_ref, left, small, field, field_small) = refs[:n], refs[n:]
    wide, tall, quads = n * tp, 2 * plan.pairs, 2 * plan.quad_pad
    for r in range(plan.rb):
        piece = [ref[r].astype(F32) for ref in recv]
        high = high_ref[r].astype(F32)
        mains = [
            (0, jnp.concatenate([p[:tp] for p in piece], axis=0).T),
            (2 * wide, high[:tall].T),
        ]
        for first, main in mains:
            size = main.shape[1]
            for k in range(2):
                at = first + k * size
                left[r * SPLIT : (r + 1) * SPLIT, at : at + size] = main[
                    k * SPLIT : (k + 1) * SPLIT
                ].astype(BF)
        at = 0
        rests = [
            (
                jnp.concatenate([p[tp + 8 * group : tp + 8 * (group + 1)] for p in piece], axis=0),
                min(4, tb - 4 * group),
            )
            for group in range(plan.rest_groups)
        ] + [(high[tall:], 4)]
        for rest, blocks in rests:
            turned = rest.T.astype(BF)
            for part in range(2 * blocks):
                small[r * REST : (r + 1) * REST, at : at + turned.shape[1]] = turned[
                    part * REST : (part + 1) * REST
                ]
                at += turned.shape[1]
    field[...] = jnp.dot(left[...], main_ref[...], preferred_element_type=F32)
    field_small[...] = jnp.dot(small[...], rest_ref[...], preferred_element_type=F32)
    base = pl.program_id(0) * plan.rb

    def step(r, unused):
        live = live_ref[base + r]
        grad = grad_ref[r]
        through = jnp.dot(through_ref[...], grad, preferred_element_type=F32)
        spectral = jnp.concatenate(
            [
                field[pl.ds(pl.multiple_of(r * SPLIT, 8), SPLIT), :],
                field_small[pl.ds(pl.multiple_of(r * REST, 8), REST), :],
            ],
            axis=0,
        )
        out_ref[r] = ((grad.astype(F32) + through + spectral) * live).astype(BF)
        return unused

    lax.fori_loop(0, plan.rb, step, 0)


def finish(plan, live, grad, main, rest, through, recv, high):
    cell = (plan.rb, plan.fpad, plan.lon)
    here = pl.BlockSpec(cell, lambda i: (i, 0, 0))
    return call(
        functools.partial(finish_kernel, plan),
        "finish",
        [live, grad, main, rest, through, *recv, high],
        [
            pl.BlockSpec(memory_space=pltpu.SMEM),
            here,
            whole(main.shape),
            whole(rest.shape),
            whole(through.shape),
        ]
        + [pl.BlockSpec((plan.rb, plan.rows1, LANES), lambda i: (i, 0, 0))] * plan.n
        + [pl.BlockSpec((plan.rb,) + high.shape[1:], lambda i: (i, 0, 0))],
        here,
        jax.ShapeDtypeStruct((plan.rows, plan.fpad, plan.lon), BF),
        (plan.rows // plan.rb,),
        [
            pltpu.VMEM((plan.rb * SPLIT, main.shape[0]), BF),
            pltpu.VMEM((plan.rb * REST, rest.shape[0]), BF),
            pltpu.VMEM((plan.rb * SPLIT, plan.lon), F32),
            pltpu.VMEM((plan.rb * REST, plan.lon), F32),
        ],
    )


def row_geometry(band_rows, band_len, lat_count):
    band_count = band_rows.shape[0]
    row_index = jnp.arange(band_count * band_len, dtype=jnp.int32)
    row_owner = row_index // band_len
    offset = row_index - row_owner * band_len
    starts = jnp.cumsum(band_rows) - band_rows
    owner_hot = (row_owner[:, None] == jnp.arange(band_count, dtype=jnp.int32)[None, :]).astype(
        jnp.int32
    )
    first_lat = jnp.sum(owner_hot * starts[None, :], axis=1)
    length = jnp.sum(owner_hot * band_rows[None, :], axis=1)
    live_rows = offset < length
    latitude = jnp.minimum(first_lat + offset, lat_count - 1)
    colatitude = latitude.astype(F32) * (math.pi / (lat_count - 1))
    return (live_rows.astype(F32), jnp.cos(colatitude), jnp.sin(colatitude))


def log_diagonal(order):
    index = np.arange(1, LMAX + 1, dtype=np.float64)
    sums = np.concatenate([[0.0], np.cumsum(0.5 * np.log((2 * index + 1) / (2 * index)))])
    return (0.5 * math.log(0.5) + sums[np.minimum(order, LMAX)]).astype(np.float32)


def field_weights(plan, weight):
    select = np.zeros((4, 2 * LANES, plan.fields), np.float32)
    side = np.zeros((4, 2 * LANES, 2), np.float32)
    for b in range(4):
        for k in range(2):
            for f in range(plan.fields):
                first = k * SPLIT + f if f < SPLIT else LANES + (2 * b + k) * REST + f - SPLIT
                select[b, first, f] = 1.0
                side[b, first, k] = 1.0
    spread = jnp.einsum("blf,fc->blc", select, weight, precision=lax.Precision.HIGHEST)
    both = jnp.concatenate([spread, spread], axis=2)
    return (both * np.repeat(side, plan.channels, axis=2)).astype(BF)


def on_device(
    states, observed, band_rows, encoder_weight, mixing_weight, degree_gain, decoder_weight
):
    space = lax.axis_size("space")
    me = lax.axis_index("space")
    fields, band, lon = observed.shape
    channels = encoder_weight.shape[1]
    plan = Plan(space, band, fields, lon, channels, degree_gain.shape[0])
    live, cosines, sines = row_geometry(band_rows, band, NLAT)
    quad = live * sines * (math.pi / (NLAT - 1))
    log_sines = jnp.log(jnp.maximum(sines, 1e-30))
    live_own = lax.dynamic_slice_in_dim(live, me * band, band)
    area = 8.0 * lax.dynamic_slice_in_dim(sines, me * band, band) * live_own

    pad = plan.fpad - fields
    rows = jnp.pad(jnp.transpose(states[0], (1, 0, 2)), ((0, 0), (0, pad), (0, 0)))
    truth = jnp.pad(jnp.transpose(observed, (1, 0, 2)), ((0, 0), (0, pad), (0, 0)))

    enc_f = encoder_weight.astype(F32)
    exact = lax.Precision.HIGHEST
    through_mix = jnp.dot(enc_f, mixing_weight.astype(F32), precision=exact)
    mix = field_weights(plan, through_mix)
    mix_back = jnp.transpose(mix, (0, 2, 1))
    gain = jnp.concatenate([degree_gain, degree_gain], axis=1)
    enc_t = jnp.pad(encoder_weight.T, ((0, 0), (0, pad)))
    dec_t = jnp.pad(decoder_weight.T, ((0, pad), (0, 0)))
    dec = jnp.pad(decoder_weight, ((0, 0), (0, pad)))
    through = jnp.pad(
        jnp.dot(enc_f, decoder_weight.astype(F32), precision=exact), ((0, pad), (0, pad))
    ).astype(BF)

    n, tp, tb = plan.n, plan.tp, plan.tb
    low, high = plan.low_orders(), plan.high_orders()
    low_f, high_f = dft_rows(plan, low, False), dft_rows(plan, high, False)
    low_i, high_i = dft_rows(plan, low, True), dft_rows(plan, high, True)

    def from_here(table):
        table = jnp.asarray(table)
        return lax.dynamic_slice_in_dim(jnp.concatenate([table, table]), me, n)

    low_sums = from_here(low_f.transpose(1, 2, 0, 3))
    low_sums = jnp.transpose(low_sums, (2, 0, 1, 3))
    dft_low = low_sums.reshape(2, n * tp, lon)
    dft_high = jnp.asarray(high_f.reshape(2, 2 * plan.pairs, lon))
    idft = jnp.concatenate(
        [
            from_here(low_i.transpose(1, 0, 2, 3)).reshape(n * 2 * tp, lon),
            jnp.asarray(high_i.reshape(4 * plan.pairs, lon)),
        ]
    )
    dft_main = jnp.concatenate(
        [low_sums.reshape(2 * n * tp, lon), jnp.asarray(high_f.reshape(4 * plan.pairs, lon))]
    )
    low_rest = jnp.transpose(low_sums.reshape(2, n, tb, 8, lon), (2, 0, 1, 3, 4))
    quads = np.zeros((2, 2, plan.quad_pad, 4, lon), low_f.dtype)
    quads[:, :, : plan.quads] = high_f.reshape(2, 2, plan.quads, 4, lon)
    dft_rest = jnp.concatenate(
        [low_rest.reshape(-1, lon), jnp.asarray(quads.transpose(3, 0, 1, 2, 4).reshape(-1, lon))]
    )

    def exchange(parts):
        got = [parts[0]] + [None] * (n - 1)
        for s in sorted(range(1, n), key=lambda s: abs(2 * s - n)):
            got[n - s] = lax.ppermute(parts[s], "space", [(i, (i + s) % n) for i in range(n)])
        return got

    recv = exchange(analyse_low(plan, rows, dft_low))
    zonal_high = analyse_high(plan, rows, dft_high)

    half = plan.half_lanes

    def side(value):
        value = jnp.pad(value, (0, half - band))
        return jnp.concatenate([value, value])

    def sides(pair_values):
        return jnp.asarray(np.repeat(pair_values.T, half, axis=1))

    own = [
        side(lax.dynamic_slice_in_dim(v, me * band, band)) for v in (cosines, quad, live, log_sines)
    ]
    shift = np.stack([plan.low + np.arange(plan.pairs), np.full(plan.pairs, plan.low - 1)])
    start = sides(log_diagonal(high)) + sides(high.astype(np.float32)) * own[3][None, :]
    high_fwd, high_inv = legendre_tables(
        sides(high), sides(shift), start, own[0], own[1], own[2], plan.span
    )
    high_coeffs = lax.psum(high_partial(plan, zonal_high, high_fwd), "space")

    orders = lax.dynamic_index_in_dim(jnp.asarray(low, jnp.int32), me, keepdims=False)
    diagonal = lax.dynamic_index_in_dim(jnp.asarray(log_diagonal(low)), me, keepdims=False)
    orders_wide = jnp.broadcast_to(orders[:, None], (tp, LANES))
    ordered = [from_here(v.reshape(n, band)).reshape(-1) for v in (cosines, quad, live, log_sines)]
    start = diagonal[:, None] + orders.astype(F32)[:, None] * ordered[3][None, :]
    low_fwd, low_inv = legendre_tables(
        orders_wide, jnp.zeros_like(orders_wide), start, *ordered[:3], plan.degrees
    )

    spectrum = spectrum_forward(plan, recv, low_fwd, low_inv, mix, gain)
    synth = [exchange(part) for part in spectrum]
    reach = ceil_to(plan.low + plan.pairs + plan.span, 8)
    longer = jnp.pad(degree_gain, ((0, reach + 8 - degree_gain.shape[0]), (0, 0)))
    gain_long = jnp.stack([longer[s : s + reach] for s in range(8)])
    synth_high = high_synthesis(plan, high_coeffs, high_inv, mix, gain_long)

    def after(value, other):
        return lax.optimization_barrier((value, other))

    predictions, grads, returned, returned_high = [], [], [], []
    gathered = []
    for i, chunk in enumerate(plan.chunks):
        live_now = live_own
        if i == 1:
            live_now, truth = after(live_own, truth)
        pred, slope = predict(
            plan, chunk, live_now, rows, idft, enc_t, dec_t, synth[i], synth_high
        )
        predictions.append(pred)
        gathered.append((lax.all_gather(pred[None], "member", axis=0, tiled=True), slope))
    for i, chunk in enumerate(plan.chunks):
        pred, (everyone, slope) = predictions[i], gathered[i]
        if i:
            pred, returned[i - 1] = after(pred, returned[i - 1])
        grad, out, out_high = score(plan, chunk, area, pred, everyone, truth, slope, idft, dec)
        grads.append(grad)
        returned_high.append(out_high)
        if i == len(plan.chunks) - 1:
            high_grads = high_adjoint(plan, returned_high, high_inv, mix_back, gain_long)
            out, high_grads = after(out, high_grads)
            high_grads = lax.psum(high_grads, "space")
        returned.append(exchange(out))

    parts = spectrum_backward(plan, returned, low_fwd, low_inv, mix_back, gain)
    ends, high_grads = after([parts[1], parts[n - 1]], high_grads)
    parts = [parts[0], ends[0], *parts[2 : n - 1], ends[1]]
    zonal_grad = high_zonal(plan, high_grads, high_fwd)
    last = exchange(parts)
    state_grad = finish(
        plan, live_own, jnp.concatenate(grads), dft_main, dft_rest, through, last, zonal_grad
    )

    def outward(block):
        return jnp.transpose(block[:, :fields], (1, 0, 2))[None]

    return (outward(jnp.concatenate(predictions)), outward(state_grad))


def solution(mesh):
    in_specs = (P("member", None, "space", None), P(None, "space", None), P(), P(), P(), P(), P())
    out_specs = (P("member", None, "space", None), P("member", None, "space", None))
    return jax.shard_map(
        on_device, mesh=mesh, in_specs=in_specs, out_specs=out_specs, check_vma=False
    )
```

```python
import functools
import math

import jax
import jax.numpy as jnp
import ml_dtypes
import numpy as np
from jax import lax
from jax.experimental import pallas as pl
from jax.experimental.pallas import tpu as pltpu
from jax.sharding import PartitionSpec as P

NLAT = 361
LMAX = 360
EPSILON = 1e-05
GROUP = 256
SPLIT = 64
REST = 16
LANES = 128
NONE = 1 << 14
VMEM = 60 * 1024 * 1024
BF = jnp.bfloat16
F32 = jnp.float32


def ceil_to(value, step):
    return -(-value // step) * step


class Plan:
    def __init__(self, space, band, fields, lon, channels, degrees):
        self.n, self.rows, self.fields, self.lon = space, band, fields, lon
        self.channels, self.degrees = channels, degrees
        self.all_rows = space * band
        self.fpad = SPLIT + REST
        self.live_t = -(-GROUP // space)
        self.tp = ceil_to(self.live_t, 8)
        self.tb = self.tp // 8
        self.rest_groups = -(-self.tb // 4)
        self.rows1 = self.tp + 8 * self.rest_groups
        self.rows2 = 2 * self.tp
        self.low = space * self.live_t
        self.step = max(k for k in (1, 2, 4) if self.live_t % k == 0)
        self.high = LMAX + 1 - self.low
        self.pairs = ceil_to(-(-self.high // 2), 8)
        self.quads = self.pairs // 4
        self.quad_pad = ceil_to(self.quads, 8)
        self.span = ceil_to(self.high + 1, 16)
        self.half = ceil_to(band, 16)
        self.half_lanes = LANES // 2
        self.rb = max(k for k in range(1, 9) if band % k == 0)
        blocks = band // self.rb
        half = blocks // 2
        counts = [count for count in (1, blocks - 1 - half, half) if count > 0]
        self.chunks = []
        start = 0
        for count in counts:
            self.chunks.append((start * self.rb, count * self.rb))
            start += count

    def low_orders(self):
        device = np.arange(self.n)[:, None]
        position = np.arange(self.tp)[None, :]
        return np.where(position < self.live_t, device * self.live_t + position, NONE)

    def high_orders(self):
        pair = np.arange(self.pairs)
        first = np.where(2 * pair < self.high, self.low + pair, NONE)
        second = np.where(2 * pair < self.high - 1, LMAX - pair, NONE)
        return np.stack([first, second])


def dft_rows(plan, order, inverse):
    live = (order <= LMAX)[..., None]
    turn = (np.where(order <= LMAX, order, 0)[..., None] * np.arange(plan.lon)) % plan.lon
    angle = turn * (2.0 * math.pi / plan.lon)
    if inverse:
        scale = np.where((order == 0) | (2 * order == plan.lon), 1.0, 2.0)[..., None]
    else:
        scale = 1.0 / plan.lon
    rows = np.stack([np.cos(angle) * scale, -np.sin(angle) * scale]) * live
    return rows.astype(ml_dtypes.bfloat16)


def params(**more):
    return pltpu.CompilerParams(vmem_limit_bytes=VMEM, **more)


def call(kernel, name, operands, in_specs, out_specs, out_shape, grid, scratch=()):
    results = out_shape if isinstance(out_shape, (list, tuple)) else [out_shape]
    moved = sum(math.prod(a.shape) * a.dtype.itemsize for a in list(operands) + list(results))
    return pl.pallas_call(
        kernel,
        grid=grid,
        in_specs=in_specs,
        out_specs=out_specs,
        out_shape=out_shape,
        scratch_shapes=list(scratch),
        compiler_params=params(),
        cost_estimate=pl.CostEstimate(flops=0, transcendentals=0, bytes_accessed=4 * moved),
        name=name,
    )(*operands)


def whole(shape):
    return pl.BlockSpec(shape, lambda *_: (0,) * len(shape))


def table_kernel(m_ref, shift_ref, start_ref, cos_ref, quad_ref, live_ref, fwd_ref, inv_ref, stage):
    lanes = fwd_ref.shape[2]
    order, shift = m_ref[...], shift_ref[...]
    square = order * order
    parts = [slice(c, c + LANES) for c in range(0, start_ref.shape[1], LANES)]

    def block(index, state):
        before = state[0]
        at_row = pl.multiple_of(index * 16, 16)
        ups, backs, pasts, onsets, keeps = [], [], [], [], []
        for p in range(16):
            deg = shift + (index * 16 + p).astype(F32)
            ratio = jnp.maximum((deg * deg - square) / (4.0 * deg * deg - 1.0), 0.0)
            root = lax.rsqrt(jnp.maximum(ratio, 1e-20))
            ups.append(root)
            backs.append(before)
            before = ratio * root
            pasts.append(order < deg)
            onsets.append(jnp.where(order == deg, 1.0, 0.0))
            keeps.append(deg <= LMAX)
        after = [before]
        for c, at in enumerate(parts):
            first, second, log_scale = state[1 + 3 * c : 4 + 3 * c]
            cosine = cos_ref[:, at]
            scale = jnp.exp(log_scale)
            for p in range(16):
                current = jnp.where(
                    pasts[p], ups[p] * (cosine * first - backs[p] * second), onsets[p]
                )
                stage[c, pl.ds(p, 8, stride=16), :] = jnp.where(keeps[p], current * scale, 0.0)
                second = first
                first = current
            size = jnp.maximum(jnp.abs(first), jnp.abs(second))
            factor = jnp.where(size > 1.0, size, 1.0)
            after += [first / factor, second / factor, log_scale + jnp.log(factor)]
        for c, at in enumerate(parts):
            width = min(LANES, lanes - c * LANES)
            out = slice(c * LANES, c * LANES + width)
            for i in range(8):
                values = stage[c, i * 16 : (i + 1) * 16, :]
                fwd_ref[i, pl.ds(at_row, 16), out] = (values * quad_ref[:, at]).astype(BF)[:, :width]
                inv_ref[i, pl.ds(at_row, 16), out] = (values * live_ref[:, at]).astype(BF)[:, :width]
        return tuple(after)

    zero = jnp.zeros((8, LANES), F32)
    state = [zero]
    for at in parts:
        state += [zero, zero, start_ref[:, at]]
    lax.fori_loop(0, fwd_ref.shape[1] // 16, block, tuple(state))


def legendre_tables(orders, shift, log_start, cosines, quad, live, degrees):
    rows = cosines.shape[0]
    wide = ceil_to(rows, LANES)
    tp = orders.shape[0]

    def spread(row):
        return jnp.pad(row, (0, wide - rows))[None]

    shape = jax.ShapeDtypeStruct((tp, degrees, rows), BF)
    row_spec = whole((1, wide))
    lane_spec = pl.BlockSpec((8, LANES), lambda i: (i, 0))
    out_spec = pl.BlockSpec((8, degrees, rows), lambda i: (i, 0, 0))
    return call(
        table_kernel,
        "legendre_tables",
        [
            orders.astype(F32),
            shift.astype(F32),
            jnp.pad(log_start, ((0, 0), (0, wide - rows))),
            spread(cosines),
            spread(quad),
            spread(live),
        ],
        [
            lane_spec,
            lane_spec,
            pl.BlockSpec((8, wide), lambda i: (i, 0)),
            row_spec,
            row_spec,
            row_spec,
        ],
        [out_spec, out_spec],
        [shape, shape],
        (tp // 8,),
        [pltpu.VMEM((wide // LANES, 128, LANES), F32)],
    )


def analyse_modes(x, dft_ref):
    head, tail = x[:SPLIT], x[SPLIT:]
    right = jnp.concatenate([head, head] + [tail] * (LANES // REST), axis=0)
    return [
        lax.dot_general(
            dft_ref[k], right, (((1,), (1,)), ((), ())), preferred_element_type=F32
        )
        for k in range(2)
    ]


def analyse_low_kernel(plan, x_ref, dft_ref, *outs):
    lane = lax.broadcasted_iota(jnp.int32, (1, LANES), 1)
    part = lane // REST
    n, tp = plan.n, plan.tp
    for r in range(plan.rb):
        cosine, sine = analyse_modes(x_ref[r], dft_ref)
        main = jnp.where(lane < SPLIT, cosine[:, :LANES], sine[:, :LANES])
        for o in range(n):
            pieces = [main[o * tp : (o + 1) * tp]]
            for group in range(plan.rest_groups):
                rest = jnp.zeros((8, LANES), F32)
                for i in range(min(4, plan.tb - group * 4)):
                    first = o * tp + (group * 4 + i) * 8
                    rest = jnp.where(part == 2 * i, cosine[first : first + 8, LANES:], rest)
                    rest = jnp.where(part == 2 * i + 1, sine[first : first + 8, LANES:], rest)
                pieces.append(rest)
            outs[o][r] = jnp.concatenate(pieces, axis=0).astype(BF)


def analyse_high_kernel(plan, x_ref, dft_ref, out):
    lane = lax.broadcasted_iota(jnp.int32, (1, LANES), 1)
    even = lane // REST % 2 == 0
    for r in range(plan.rb):
        cosine, sine = analyse_modes(x_ref[r], dft_ref)
        main = jnp.where(lane < SPLIT, cosine[:, :LANES], sine[:, :LANES])
        rest = jnp.where(even, cosine[:, LANES:], sine[:, LANES:])
        out[r] = jnp.concatenate([main, rest], axis=1).astype(BF)


def analyse(plan, kernel, name, x, dft, height, lanes, count):
    shape = jax.ShapeDtypeStruct((plan.rows, height, lanes), BF)
    return call(
        functools.partial(kernel, plan),
        name,
        [x, dft],
        [pl.BlockSpec((plan.rb, plan.fpad, plan.lon), lambda i: (i, 0, 0)), whole(dft.shape)],
        [pl.BlockSpec((plan.rb, height, lanes), lambda i: (i, 0, 0))] * count,
        [shape] * count,
        (plan.rows // plan.rb,),
    )


def analyse_low(plan, x, dft):
    return list(analyse(plan, analyse_low_kernel, "analyse_low", x, dft, plan.rows1, LANES, plan.n))


def analyse_high(plan, x, dft):
    return analyse(
        plan, analyse_high_kernel, "analyse_high", x, dft, 2 * plan.pairs, 2 * LANES, 1
    )[0]


def unpack(plan, refs, store, height):
    start = 0
    for parts in refs:
        for o, ref in enumerate(parts):

            def step(r, unused, base=o * plan.rows + start, ref=ref):
                at = pl.multiple_of((base + r) * height, 8)
                store[pl.ds(at, height), :] = ref[r].astype(F32)
                return unused

            lax.fori_loop(0, ref.shape[0], step, 0)
        start += parts[0].shape[0]


def repack(plan, refs, store, height):
    start = 0
    for parts in refs:
        for o, ref in enumerate(parts):

            def step(r, unused, base=o * plan.rows + start, ref=ref):
                at = pl.multiple_of((base + r) * height, 8)
                ref[r] = store[pl.ds(at, height), :].astype(BF)
                return unused

            lax.fori_loop(0, ref.shape[0], step, 0)
        start += parts[0].shape[0]


def by_device(plan, refs):
    return [refs[i : i + plan.n] for i in range(0, len(refs), plan.n)]


def rest_row(plan, t):
    block = t // 8
    return plan.tp + 8 * (block // 4) + t % 8


def spectrum_forward_kernel(plan, *refs):
    recv, (fwd, inv, mix, gain) = refs[: plan.n], refs[plan.n : plan.n + 4]
    outs, zin, yout = refs[plan.n + 4 : -2], refs[-2], refs[-1]
    step = pl.program_id(0)

    @pl.when(step == 0)
    def _():
        unpack(plan, [recv], zin, plan.rows1)
        if plan.live_t < plan.tp:
            yout[...] = jnp.zeros_like(yout)

    for i in range(plan.step):
        t = step * plan.step + i
        z = jnp.concatenate(
            [
                zin[pl.ds(t, plan.all_rows, stride=plan.rows1), :],
                zin[pl.ds(rest_row(plan, t), plan.all_rows, stride=plan.rows1), :],
            ],
            axis=1,
        ).astype(BF)
        coeffs = jnp.dot(fwd[i], z, preferred_element_type=F32).astype(BF)
        filtered = (jnp.dot(coeffs, mix[0], preferred_element_type=F32) * gain[...]).astype(BF)
        y = lax.dot_general(
            inv[i], filtered, (((0,), (0,)), ((), ())), preferred_element_type=F32
        )
        for k in range(2):
            yout[pl.ds(k * plan.tp + t, plan.all_rows, stride=plan.rows2), :] = y[
                :, k * LANES : (k + 1) * LANES
            ]

    @pl.when(step == plan.live_t // plan.step - 1)
    def _():
        repack(plan, by_device(plan, outs), yout, plan.rows2)


def spectrum_backward_kernel(plan, count, *refs):
    recvs = refs[:count]
    fwd, inv, mix, gain = refs[count : count + 4]
    outs, zin, yout = refs[count + 4 : -2], refs[-2], refs[-1]
    step = pl.program_id(0)

    @pl.when(step == 0)
    def _():
        unpack(plan, by_device(plan, recvs), zin, plan.rows2)
        yout[...] = jnp.zeros_like(yout)

    for i in range(plan.step):
        t = step * plan.step + i
        z = jnp.concatenate(
            [
                zin[pl.ds(k * plan.tp + t, plan.all_rows, stride=plan.rows2), :]
                for k in range(2)
            ],
            axis=1,
        ).astype(BF)
        grad = (jnp.dot(inv[i], z, preferred_element_type=F32) * gain[...]).astype(BF)
        back = jnp.dot(grad, mix[0], preferred_element_type=F32).astype(BF)
        y = lax.dot_general(fwd[i], back, (((0,), (0,)), ((), ())), preferred_element_type=F32)
        yout[pl.ds(t, plan.all_rows, stride=plan.rows1), :] = y[:, :LANES]
        where = pl.ds(rest_row(plan, t), plan.all_rows, stride=plan.rows1)
        yout[where, :] = yout[where, :] + y[:, LANES:]

    @pl.when(step == plan.live_t // plan.step - 1)
    def _():
        repack(plan, [outs], yout, plan.rows1)


def spectrum_specs(plan, mix, gain):
    table = pl.BlockSpec((plan.step, plan.degrees, plan.all_rows), lambda t: (t, 0, 0))
    return [table, table, pl.BlockSpec((1,) + mix.shape[1:], lambda t: ((t * plan.step // 8) % 4, 0, 0)), whole(gain.shape)]


def spectrum_forward(plan, recv, fwd, inv, mix, gain):
    shapes = [(count, plan.rows2, LANES) for _, count in plan.chunks for _ in range(plan.n)]
    parts = call(
        functools.partial(spectrum_forward_kernel, plan),
        "spectrum_forward",
        [*recv, fwd, inv, mix, gain],
        [whole(r.shape) for r in recv] + spectrum_specs(plan, mix, gain),
        [whole(s) for s in shapes],
        [jax.ShapeDtypeStruct(s, BF) for s in shapes],
        (plan.live_t // plan.step,),
        [
            pltpu.VMEM((plan.all_rows * plan.rows1, LANES), F32),
            pltpu.VMEM((plan.all_rows * plan.rows2, LANES), F32),
        ],
    )
    return by_device(plan, parts)


def spectrum_backward(plan, recvs, fwd, inv, mix, gain):
    shape = (plan.rows, plan.rows1, LANES)
    flat = [part for parts in recvs for part in parts]
    return call(
        functools.partial(spectrum_backward_kernel, plan, len(flat)),
        "spectrum_backward",
        [*flat, fwd, inv, mix, gain],
        [whole(r.shape) for r in flat] + spectrum_specs(plan, mix, gain),
        [whole(shape)] * plan.n,
        [jax.ShapeDtypeStruct(shape, BF)] * plan.n,
        (plan.live_t // plan.step,),
        [
            pltpu.VMEM((plan.all_rows * plan.rows2, LANES), F32),
            pltpu.VMEM((plan.all_rows * plan.rows1, LANES), F32),
        ],
    )


def pair_gain(plan, pair, gain):
    row = lax.broadcasted_iota(jnp.int32, (plan.span, 1), 0)
    first, second = plan.low + pair, plan.low - 1
    first_at = pl.multiple_of(first // 8 * 8, 8)
    one = jnp.where(
        row < plan.high - pair,
        gain[first % 8, pl.ds(first_at, plan.span), :],
        gain[second % 8, pl.ds(second // 8 * 8, plan.span), :],
    )
    return jnp.concatenate([one, one], axis=1)


def load_rows(plan, refs, store, height, wide):
    start = 0
    for ref in refs:

        def step(r, unused, start=start, ref=ref):
            at = pl.multiple_of((start + r) * height, 8)
            for w in range(wide):
                store[w, pl.ds(at, height), :] = ref[r, :, w * LANES : (w + 1) * LANES].astype(F32)
            return unused

        lax.fori_loop(0, ref.shape[0], step, 0)
        start += ref.shape[0]

    def clear(r, unused):
        at = pl.multiple_of(r * height, 8)
        for w in range(wide):
            store[w, pl.ds(at, height), :] = jnp.zeros((height, LANES), F32)
        return unused

    lax.fori_loop(start, plan.half_lanes, clear, 0)


def high_partial_kernel(plan, zonal, fwd, out, zin):
    quad = pl.program_id(0)
    block = lax.broadcasted_iota(jnp.int32, (1, LANES), 1) // (2 * REST)

    @pl.when(quad == 0)
    def _():
        load_rows(plan, [zonal], zin, 2 * plan.pairs, 2)

    rest = jnp.zeros((plan.span, LANES), F32)
    for i in range(4):
        pair = quad * 4 + i
        z = jnp.concatenate(
            [
                jnp.concatenate(
                    [
                        zin[w, pl.ds(s * plan.pairs + pair, plan.half_lanes, stride=2 * plan.pairs), :]
                        for s in range(2)
                    ],
                    axis=0,
                )
                for w in range(2)
            ],
            axis=1,
        ).astype(BF)
        coeffs = jnp.dot(fwd[i], z, preferred_element_type=F32)
        out[0, i] = coeffs[:, :LANES].astype(BF)
        rest = rest + jnp.where(block == i, coeffs[:, LANES:], 0.0)
    out[0, 4] = rest.astype(BF)


def high_synthesis_kernel(plan, coeffs, inv, mix, gain, out, yout):
    quad = pl.program_id(0)
    height = 4 * plan.pairs
    for i in range(4):
        pair = quad * 4 + i
        both = jnp.concatenate([coeffs[0, i], coeffs[0, 4]], axis=1)
        filtered = jnp.dot(both, mix[i], preferred_element_type=F32) * pair_gain(plan, pair, gain)
        y = lax.dot_general(
            inv[i], filtered.astype(BF), (((0,), (0,)), ((), ())), preferred_element_type=F32
        )
        for k in range(2):
            for s in range(2):
                yout[pl.ds((2 * k + s) * plan.pairs + pair, plan.half_lanes, stride=height), :] = y[
                    s * plan.half_lanes : (s + 1) * plan.half_lanes, k * LANES : (k + 1) * LANES
                ]

    @pl.when(quad == plan.quads - 1)
    def _():
        def step(r, unused):
            out[r] = yout[pl.ds(pl.multiple_of(r * height, 8), height), :].astype(BF)
            return unused

        lax.fori_loop(0, plan.rows, step, 0)


def high_adjoint_kernel(plan, count, *refs):
    grads, (inv, mix, gain, out, zin) = refs[:count], refs[count:]
    quad = pl.program_id(0)
    height = 4 * plan.pairs

    @pl.when(quad == 0)
    def _():
        load_rows(plan, grads, zin, height, 1)

    rest = jnp.zeros((plan.span, LANES), F32)
    for i in range(4):
        pair = quad * 4 + i
        z = jnp.concatenate(
            [
                jnp.concatenate(
                    [
                        zin[0, pl.ds((2 * k + s) * plan.pairs + pair, plan.half_lanes, stride=height), :]
                        for s in range(2)
                    ],
                    axis=0,
                )
                for k in range(2)
            ],
            axis=1,
        ).astype(BF)
        grad = jnp.dot(inv[i], z, preferred_element_type=F32) * pair_gain(plan, pair, gain)
        back = jnp.dot(grad.astype(BF), mix[i], preferred_element_type=F32)
        out[0, i] = back[:, :LANES].astype(BF)
        rest = rest + back[:, LANES:]
    out[0, 4] = rest.astype(BF)


def high_zonal_kernel(plan, grads, fwd, out, yout):
    quad = pl.program_id(0)
    height = 2 * plan.pairs + 2 * plan.quad_pad
    block = lax.broadcasted_iota(jnp.int32, (1, LANES), 1) // (2 * REST)

    if plan.quad_pad > plan.quads:

        @pl.when(quad == 0)
        def _():
            yout[...] = jnp.zeros_like(yout)

    rest = jnp.zeros((LANES, LANES), F32)
    for i in range(4):
        pair = quad * 4 + i
        both = jnp.concatenate([grads[0, i], grads[0, 4]], axis=1)
        y = lax.dot_general(
            fwd[i], both, (((0,), (0,)), ((), ())), preferred_element_type=F32
        )
        for s in range(2):
            yout[pl.ds(s * plan.pairs + pair, plan.half_lanes, stride=height), :] = y[
                s * plan.half_lanes : (s + 1) * plan.half_lanes, :LANES
            ]
        rest = rest + jnp.where(block == i, y[:, LANES:], 0.0)
    for s in range(2):
        row = 2 * plan.pairs + s * plan.quad_pad + quad
        yout[pl.ds(row, plan.half_lanes, stride=height), :] = rest[
            s * plan.half_lanes : (s + 1) * plan.half_lanes
        ]

    @pl.when(quad == plan.quads - 1)
    def _():
        def step(r, unused):
            out[r] = yout[pl.ds(pl.multiple_of(r * height, 8), height), :].astype(BF)
            return unused

        lax.fori_loop(0, plan.rows, step, 0)


def high_call(plan, kernel, name, whole_in, blocked, fixed, out_shape, out_whole, scratch):
    def quad_spec(array):
        size = array.shape[0] // plan.quads
        rest = array.shape[1:]
        return pl.BlockSpec((size,) + rest, lambda q: (q,) + (0,) * len(rest))

    return call(
        kernel,
        name,
        [*whole_in, *blocked, *fixed],
        [whole(a.shape) for a in whole_in]
        + [quad_spec(a) for a in blocked]
        + [whole(a.shape) for a in fixed],
        whole(out_shape) if out_whole else quad_spec(jax.ShapeDtypeStruct(out_shape, BF)),
        jax.ShapeDtypeStruct(out_shape, BF),
        (plan.quads,),
        [pltpu.VMEM(scratch, F32)],
    )


def high_partial(plan, zonal, fwd):
    return high_call(
        plan, functools.partial(high_partial_kernel, plan), "high_partial", [zonal], [fwd], [],
        (plan.quads, 5, plan.span, LANES), False, (2, plan.half_lanes * 2 * plan.pairs, LANES),
    )


def high_synthesis(plan, coeffs, inv, mix, gain):
    return high_call(
        plan, functools.partial(high_synthesis_kernel, plan), "high_synthesis", [], [coeffs, inv],
        [mix, gain], (plan.rows, 4 * plan.pairs, LANES), True,
        (plan.half_lanes * 4 * plan.pairs, LANES),
    )


def high_adjoint(plan, grads, inv, mix, gain):
    return high_call(
        plan, functools.partial(high_adjoint_kernel, plan, len(grads)), "high_adjoint", grads, [inv],
        [mix, gain], (plan.quads, 5, plan.span, LANES), False,
        (1, plan.half_lanes * 4 * plan.pairs, LANES),
    )


def high_zonal(plan, grads, fwd):
    height = 2 * plan.pairs + 2 * plan.quad_pad
    return high_call(
        plan, functools.partial(high_zonal_kernel, plan), "high_zonal", [], [grads, fwd], [],
        (plan.rows, height, LANES), True, (plan.half_lanes * height, LANES),
    )


def predict_kernel(plan, first, live_ref, x_ref, idft_ref, enc_ref, dec_ref, *refs):
    recv, (high, pred_ref, slope_ref, left, field) = refs[: plan.n], refs[plan.n :]
    c = plan.channels
    wide = plan.n * plan.rows2
    for r in range(plan.rb):
        left[r * c : (r + 1) * c, :wide] = jnp.concatenate([ref[r] for ref in recv], axis=0).T
        left[r * c : (r + 1) * c, wide:] = high[r].T
    field[...] = jnp.dot(left[...], idft_ref[...], preferred_element_type=F32)
    base = first + pl.program_id(0) * plan.rb

    def step(r, unused):
        live = live_ref[base + r]
        x = x_ref[r]
        u = field[pl.ds(pl.multiple_of(r * c, 8), c), :]
        hidden = (jnp.dot(enc_ref[...], x, preferred_element_type=F32) * live).astype(BF)
        phi = 0.5 + 0.5 * lax.erf(u * (1.0 / math.sqrt(2.0)))
        slope = phi + u * jnp.exp(-0.5 * u * u) * (1.0 / math.sqrt(2.0 * math.pi))
        slope_ref[r] = slope.astype(BF)
        block = ((u * phi + hidden.astype(F32)) * live).astype(BF)
        decoded = jnp.dot(dec_ref[...], block, preferred_element_type=F32)
        pred_ref[r] = ((x.astype(F32) + decoded) * live).astype(BF)
        return unused

    lax.fori_loop(0, plan.rb, step, 0)


def predict(plan, chunk, live, x, idft, enc_t, dec_t, recv, high):
    first, count = chunk
    skip = first // plan.rb
    shape = (count, plan.fpad, plan.lon)
    slope_shape = (count, plan.channels, plan.lon)
    return call(
        functools.partial(predict_kernel, plan, first),
        "predict",
        [live, x, idft, enc_t, dec_t, *recv, high],
        [
            pl.BlockSpec(memory_space=pltpu.SMEM),
            pl.BlockSpec((plan.rb,) + shape[1:], lambda i: (i + skip, 0, 0)),
            whole(idft.shape),
            whole(enc_t.shape),
            whole(dec_t.shape),
        ]
        + [pl.BlockSpec((plan.rb, plan.rows2, LANES), lambda i: (i, 0, 0))] * plan.n
        + [pl.BlockSpec((plan.rb,) + high.shape[1:], lambda i: (i + skip, 0, 0))],
        [
            pl.BlockSpec((plan.rb,) + shape[1:], lambda i: (i, 0, 0)),
            pl.BlockSpec((plan.rb,) + slope_shape[1:], lambda i: (i, 0, 0)),
        ],
        [jax.ShapeDtypeStruct(shape, BF), jax.ShapeDtypeStruct(slope_shape, BF)],
        (count // plan.rb,),
        [
            pltpu.VMEM((plan.rb * plan.channels, idft.shape[0]), BF),
            pltpu.VMEM((plan.rb * plan.channels, plan.lon), F32),
        ],
    )


def score_kernel(plan, first, others, area_ref, own_ref, obs_ref, slope_ref, idft_ref, dec_ref, *refs):
    other_refs, refs = refs[:others], refs[others:]
    grad_ref, outs, (out_high, right) = refs[0], refs[1 : 1 + plan.n], refs[1 + plan.n :]
    c = plan.channels
    base = first + pl.program_id(0) * plan.rb

    def step(r, unused):
        area = area_ref[base + r]
        own = own_ref[r].astype(F32)
        gap = own - obs_ref[r].astype(F32)
        total = gap * lax.rsqrt(jnp.sum(gap * gap, axis=0, keepdims=True) + EPSILON)
        for ref in other_refs:
            gap = own - ref[r].astype(F32)
            near = lax.rsqrt(jnp.sum(gap * gap, axis=0, keepdims=True) + EPSILON)
            total = total - gap * (near * (1.0 / (others + 1)))
        grad = (total * area).astype(BF)
        grad_ref[r] = grad
        block = jnp.dot(dec_ref[...], grad, preferred_element_type=F32)
        right[pl.ds(pl.multiple_of(r * c, 16), c), :] = (
            block * slope_ref[r].astype(F32)
        ).astype(BF)
        return unused

    lax.fori_loop(0, plan.rb, step, 0)
    wide = plan.n * plan.rows2

    def modes(first, last):
        return lax.dot_general(
            idft_ref[first:last, :],
            right[...],
            (((1,), (1,)), ((), ())),
            preferred_element_type=F32,
        ).astype(BF)

    low, high = modes(0, wide), modes(wide, idft_ref.shape[0])
    for r in range(plan.rb):
        for o in range(plan.n):
            outs[o][r] = low[o * plan.rows2 : (o + 1) * plan.rows2, r * c : (r + 1) * c]
        out_high[r] = high[:, r * c : (r + 1) * c]


def score(plan, chunk, area, own, others, observed, slope, idft, dec):
    first, count = chunk
    skip = first // plan.rb
    cell = (plan.rb, plan.fpad, plan.lon)
    out_shape = (count, plan.rows2, LANES)
    high = 4 * plan.pairs
    here = pl.BlockSpec(cell, lambda i: (i, 0, 0))
    grad, *outs = call(
        functools.partial(score_kernel, plan, first, len(others)),
        "score",
        [area, own, observed, slope, idft, dec, *others],
        [
            pl.BlockSpec(memory_space=pltpu.SMEM),
            here,
            pl.BlockSpec(cell, lambda i: (i + skip, 0, 0)),
            pl.BlockSpec((plan.rb, plan.channels, plan.lon), lambda i: (i, 0, 0)),
            whole(idft.shape),
            whole(dec.shape),
        ]
        + [here] * len(others),
        [here]
        + [pl.BlockSpec((plan.rb, plan.rows2, LANES), lambda i: (i, 0, 0))] * plan.n
        + [pl.BlockSpec((plan.rb, high, LANES), lambda i: (i, 0, 0))],
        [jax.ShapeDtypeStruct((count,) + cell[1:], BF)]
        + [jax.ShapeDtypeStruct(out_shape, BF)] * plan.n
        + [jax.ShapeDtypeStruct((count, high, LANES), BF)],
        (count // plan.rb,),
        [pltpu.VMEM((plan.rb * plan.channels, plan.lon), BF)],
    )
    return grad, outs[:-1], outs[-1]


def finish_kernel(
    plan, live_ref, grad_ref, main_ref, rest_ref, through_ref, *refs
):
    n, tp, tb = plan.n, plan.tp, plan.tb
    recv, (high_ref, out_ref, left, small, field, field_small) = refs[:n], refs[n:]
    wide, tall, quads = n * tp, 2 * plan.pairs, 2 * plan.quad_pad
    for r in range(plan.rb):
        piece = [ref[r].astype(F32) for ref in recv]
        high = high_ref[r].astype(F32)
        mains = [
            (0, jnp.concatenate([p[:tp] for p in piece], axis=0).T),
            (2 * wide, high[:tall].T),
        ]
        for first, main in mains:
            size = main.shape[1]
            for k in range(2):
                at = first + k * size
                left[r * SPLIT : (r + 1) * SPLIT, at : at + size] = main[
                    k * SPLIT : (k + 1) * SPLIT
                ].astype(BF)
        at = 0
        rests = [
            (
                jnp.concatenate([p[tp + 8 * group : tp + 8 * (group + 1)] for p in piece], axis=0),
                min(4, tb - 4 * group),
            )
            for group in range(plan.rest_groups)
        ] + [(high[tall:], 4)]
        for rest, blocks in rests:
            turned = rest.T.astype(BF)
            for part in range(2 * blocks):
                small[r * REST : (r + 1) * REST, at : at + turned.shape[1]] = turned[
                    part * REST : (part + 1) * REST
                ]
                at += turned.shape[1]
    field[...] = jnp.dot(left[...], main_ref[...], preferred_element_type=F32)
    field_small[...] = jnp.dot(small[...], rest_ref[...], preferred_element_type=F32)
    base = pl.program_id(0) * plan.rb

    def step(r, unused):
        live = live_ref[base + r]
        grad = grad_ref[r]
        through = jnp.dot(through_ref[...], grad, preferred_element_type=F32)
        spectral = jnp.concatenate(
            [
                field[pl.ds(pl.multiple_of(r * SPLIT, 8), SPLIT), :],
                field_small[pl.ds(pl.multiple_of(r * REST, 8), REST), :],
            ],
            axis=0,
        )
        out_ref[r] = ((grad.astype(F32) + through + spectral) * live).astype(BF)
        return unused

    lax.fori_loop(0, plan.rb, step, 0)


def finish(plan, live, grad, main, rest, through, recv, high):
    cell = (plan.rb, plan.fpad, plan.lon)
    here = pl.BlockSpec(cell, lambda i: (i, 0, 0))
    return call(
        functools.partial(finish_kernel, plan),
        "finish",
        [live, grad, main, rest, through, *recv, high],
        [
            pl.BlockSpec(memory_space=pltpu.SMEM),
            here,
            whole(main.shape),
            whole(rest.shape),
            whole(through.shape),
        ]
        + [pl.BlockSpec((plan.rb, plan.rows1, LANES), lambda i: (i, 0, 0))] * plan.n
        + [pl.BlockSpec((plan.rb,) + high.shape[1:], lambda i: (i, 0, 0))],
        here,
        jax.ShapeDtypeStruct((plan.rows, plan.fpad, plan.lon), BF),
        (plan.rows // plan.rb,),
        [
            pltpu.VMEM((plan.rb * SPLIT, main.shape[0]), BF),
            pltpu.VMEM((plan.rb * REST, rest.shape[0]), BF),
            pltpu.VMEM((plan.rb * SPLIT, plan.lon), F32),
            pltpu.VMEM((plan.rb * REST, plan.lon), F32),
        ],
    )


def row_geometry(band_rows, band_len, lat_count):
    band_count = band_rows.shape[0]
    row_index = jnp.arange(band_count * band_len, dtype=jnp.int32)
    row_owner = row_index // band_len
    offset = row_index - row_owner * band_len
    starts = jnp.cumsum(band_rows) - band_rows
    owner_hot = (row_owner[:, None] == jnp.arange(band_count, dtype=jnp.int32)[None, :]).astype(
        jnp.int32
    )
    first_lat = jnp.sum(owner_hot * starts[None, :], axis=1)
    length = jnp.sum(owner_hot * band_rows[None, :], axis=1)
    live_rows = offset < length
    latitude = jnp.minimum(first_lat + offset, lat_count - 1)
    colatitude = latitude.astype(F32) * (math.pi / (lat_count - 1))
    return (live_rows.astype(F32), jnp.cos(colatitude), jnp.sin(colatitude))


def log_diagonal(order):
    index = np.arange(1, LMAX + 1, dtype=np.float64)
    sums = np.concatenate([[0.0], np.cumsum(0.5 * np.log((2 * index + 1) / (2 * index)))])
    return (0.5 * math.log(0.5) + sums[np.minimum(order, LMAX)]).astype(np.float32)


def field_weights(plan, weight):
    select = np.zeros((4, 2 * LANES, plan.fields), np.float32)
    side = np.zeros((4, 2 * LANES, 2), np.float32)
    for b in range(4):
        for k in range(2):
            for f in range(plan.fields):
                first = k * SPLIT + f if f < SPLIT else LANES + (2 * b + k) * REST + f - SPLIT
                select[b, first, f] = 1.0
                side[b, first, k] = 1.0
    spread = jnp.einsum("blf,fc->blc", select, weight, precision=lax.Precision.HIGHEST)
    both = jnp.concatenate([spread, spread], axis=2)
    return (both * np.repeat(side, plan.channels, axis=2)).astype(BF)


def on_device(
    states, observed, band_rows, encoder_weight, mixing_weight, degree_gain, decoder_weight
):
    space = lax.axis_size("space")
    me = lax.axis_index("space")
    fields, band, lon = observed.shape
    channels = encoder_weight.shape[1]
    plan = Plan(space, band, fields, lon, channels, degree_gain.shape[0])
    live, cosines, sines = row_geometry(band_rows, band, NLAT)
    quad = live * sines * (math.pi / (NLAT - 1))
    log_sines = jnp.log(jnp.maximum(sines, 1e-30))
    live_own = lax.dynamic_slice_in_dim(live, me * band, band)
    area = 8.0 * lax.dynamic_slice_in_dim(sines, me * band, band) * live_own

    pad = plan.fpad - fields
    rows = jnp.pad(jnp.transpose(states[0], (1, 0, 2)), ((0, 0), (0, pad), (0, 0)))
    truth = jnp.pad(jnp.transpose(observed, (1, 0, 2)), ((0, 0), (0, pad), (0, 0)))

    enc_f = encoder_weight.astype(F32)
    exact = lax.Precision.HIGHEST
    through_mix = jnp.dot(enc_f, mixing_weight.astype(F32), precision=exact)
    mix = field_weights(plan, through_mix)
    mix_back = jnp.transpose(mix, (0, 2, 1))
    gain = jnp.concatenate([degree_gain, degree_gain], axis=1)
    enc_t = jnp.pad(encoder_weight.T, ((0, 0), (0, pad)))
    dec_t = jnp.pad(decoder_weight.T, ((0, pad), (0, 0)))
    dec = jnp.pad(decoder_weight, ((0, 0), (0, pad)))
    through = jnp.pad(
        jnp.dot(enc_f, decoder_weight.astype(F32), precision=exact), ((0, pad), (0, pad))
    ).astype(BF)

    n, tp, tb = plan.n, plan.tp, plan.tb
    low, high = plan.low_orders(), plan.high_orders()
    low_f, high_f = dft_rows(plan, low, False), dft_rows(plan, high, False)
    low_i, high_i = dft_rows(plan, low, True), dft_rows(plan, high, True)

    def from_here(table):
        table = jnp.asarray(table)
        return lax.dynamic_slice_in_dim(jnp.concatenate([table, table]), me, n)

    low_sums = from_here(low_f.transpose(1, 2, 0, 3))
    low_sums = jnp.transpose(low_sums, (2, 0, 1, 3))
    dft_low = low_sums.reshape(2, n * tp, lon)
    dft_high = jnp.asarray(high_f.reshape(2, 2 * plan.pairs, lon))
    idft = jnp.concatenate(
        [
            from_here(low_i.transpose(1, 0, 2, 3)).reshape(n * 2 * tp, lon),
            jnp.asarray(high_i.reshape(4 * plan.pairs, lon)),
        ]
    )
    dft_main = jnp.concatenate(
        [low_sums.reshape(2 * n * tp, lon), jnp.asarray(high_f.reshape(4 * plan.pairs, lon))]
    )
    low_rest = jnp.transpose(low_sums.reshape(2, n, tb, 8, lon), (2, 0, 1, 3, 4))
    quads = np.zeros((2, 2, plan.quad_pad, 4, lon), low_f.dtype)
    quads[:, :, : plan.quads] = high_f.reshape(2, 2, plan.quads, 4, lon)
    dft_rest = jnp.concatenate(
        [low_rest.reshape(-1, lon), jnp.asarray(quads.transpose(3, 0, 1, 2, 4).reshape(-1, lon))]
    )

    def other_members(block):
        size = lax.axis_size("member")
        chips = size // 2
        if size % 2:
            ring = range(1, size)
            return [lax.ppermute(block, "member", [(i, (i + d) % size) for i in range(size)]) for d in ring]
        blocks = [block]
        for d in range(1, chips):
            to = [(i, (i // 2 + d) % chips * 2 + i % 2) for i in range(size)]
            blocks.append(lax.ppermute(block, "member", to))
        swap = [(i, i + 1 - 2 * (i % 2)) for i in range(size)]
        return blocks[1:] + [lax.ppermute(b, "member", swap) for b in blocks]

    def outward(block):
        return jnp.transpose(block[:, :fields], (1, 0, 2))[None]

    def exchange(parts):
        got = [parts[0]] + [None] * (n - 1)
        for s in sorted(range(1, n), key=lambda s: abs(2 * s - n)):
            got[n - s] = lax.ppermute(parts[s], "space", [(i, (i + s) % n) for i in range(n)])
        return got

    sent = analyse_low(plan, rows, dft_low)
    rows_next, sent[0] = lax.optimization_barrier((rows, sent[0]))
    recv = exchange(sent)
    zonal_high = analyse_high(plan, rows_next, dft_high)

    half = plan.half_lanes

    def side(value):
        value = jnp.pad(value, (0, half - band))
        return jnp.concatenate([value, value])

    def sides(pair_values):
        return jnp.asarray(np.repeat(pair_values.T, half, axis=1))

    own = [
        side(lax.dynamic_slice_in_dim(v, me * band, band)) for v in (cosines, quad, live, log_sines)
    ]
    shift = np.stack([plan.low + np.arange(plan.pairs), np.full(plan.pairs, plan.low - 1)])
    start = sides(log_diagonal(high)) + sides(high.astype(np.float32)) * own[3][None, :]
    high_fwd, high_inv = legendre_tables(
        sides(high), sides(shift), start, own[0], own[1], own[2], plan.span
    )
    high_coeffs = lax.psum(high_partial(plan, zonal_high, high_fwd), "space")

    orders = lax.dynamic_index_in_dim(jnp.asarray(low, jnp.int32), me, keepdims=False)
    diagonal = lax.dynamic_index_in_dim(jnp.asarray(log_diagonal(low)), me, keepdims=False)
    orders_wide = jnp.broadcast_to(orders[:, None], (tp, LANES))
    ordered = [from_here(v.reshape(n, band)).reshape(-1) for v in (cosines, quad, live, log_sines)]
    start = diagonal[:, None] + orders.astype(F32)[:, None] * ordered[3][None, :]
    low_fwd, low_inv = legendre_tables(
        orders_wide, jnp.zeros_like(orders_wide), start, *ordered[:3], plan.degrees
    )

    spectrum = spectrum_forward(plan, recv, low_fwd, low_inv, mix, gain)
    synth = [exchange(part) for part in spectrum]
    reach = ceil_to(plan.low + plan.pairs + plan.span, 8)
    longer = jnp.pad(degree_gain, ((0, reach + 8 - degree_gain.shape[0]), (0, 0)))
    gain_long = jnp.stack([longer[s : s + reach] for s in range(8)])

    def after(value, other):
        return lax.optimization_barrier((value, other))

    synth_high = high_synthesis(plan, high_coeffs, high_inv, mix, gain_long)

    predictions, grads, returned, returned_high = [], [], [], []
    gathered = []
    for i, chunk in enumerate(plan.chunks):
        live_now = live_own
        if i == 1:
            live_now, truth = after(live_own, truth)
        pred, slope = predict(
            plan, chunk, live_now, rows, idft, enc_t, dec_t, synth[i], synth_high
        )
        predictions.append(pred)
        gathered.append((other_members(pred), slope))
    for i, chunk in enumerate(plan.chunks):
        pred, (others, slope) = predictions[i], gathered[i]
        if i:
            pred, returned[i - 1] = after(pred, returned[i - 1])
        grad, out, out_high = score(plan, chunk, area, pred, others, truth, slope, idft, dec)
        grads.append(grad)
        returned_high.append(out_high)
        if i == len(plan.chunks) - 1:
            high_grads = high_adjoint(plan, returned_high, high_inv, mix_back, gain_long)
            out, high_grads = after(out, high_grads)
            high_grads = lax.psum(high_grads, "space")
        returned.append(exchange(out))

    parts = spectrum_backward(plan, returned, low_fwd, low_inv, mix_back, gain)
    zonal_grad = high_zonal(plan, high_grads, high_fwd)
    grads = jnp.concatenate(grads)
    predictions = outward(jnp.concatenate(predictions))
    ends, (zonal_grad, grads, predictions) = after(
        [parts[1], parts[n - 1]], (zonal_grad, grads, predictions)
    )
    parts = [parts[0], ends[0], *parts[2 : n - 1], ends[1]]
    last = exchange(parts)
    state_grad = finish(
        plan, live_own, grads, dft_main, dft_rest, through, last, zonal_grad
    )

    return (predictions, outward(state_grad))


def solution(mesh):
    in_specs = (P("member", None, "space", None), P(None, "space", None), P(), P(), P(), P(), P())
    out_specs = (P("member", None, "space", None), P("member", None, "space", None))
    return jax.shard_map(
        on_device, mesh=mesh, in_specs=in_specs, out_specs=out_specs, check_vma=False
    )
```

```python
import functools
import math

import jax
import jax.numpy as jnp
import ml_dtypes
import numpy as np
from jax import lax
from jax.experimental import pallas as pl
from jax.experimental.pallas import tpu as pltpu
from jax.sharding import PartitionSpec as P

NLAT = 361
LMAX = 360
EPSILON = 1e-05
GROUP = 256
SPLIT = 64
REST = 16
LANES = 128
NONE = 1 << 14
VMEM = 60 * 1024 * 1024
BF = jnp.bfloat16
F32 = jnp.float32


def ceil_to(value, step):
    return -(-value // step) * step


class Plan:
    def __init__(self, space, band, fields, lon, channels, degrees):
        self.n, self.rows, self.fields, self.lon = space, band, fields, lon
        self.channels, self.degrees = channels, degrees
        self.all_rows = space * band
        self.fpad = SPLIT + REST
        self.live_t = -(-GROUP // space)
        self.tp = ceil_to(self.live_t, 8)
        self.tb = self.tp // 8
        self.rest_groups = -(-self.tb // 4)
        self.rows1 = self.tp + 8 * self.rest_groups
        self.rows2 = 2 * self.tp
        self.low = space * self.live_t
        self.step = max(k for k in (1, 2, 4) if self.live_t % k == 0)
        self.high = LMAX + 1 - self.low
        self.pairs = ceil_to(-(-self.high // 2), 8)
        self.quads = self.pairs // 4
        self.quad_pad = ceil_to(self.quads, 8)
        self.span = ceil_to(self.high + 1, 16)
        self.half = ceil_to(band, 16)
        self.half_lanes = LANES // 2
        self.rb = max(k for k in range(1, 9) if band % k == 0)
        blocks = band // self.rb
        half = blocks // 2
        rest = (blocks - half) // 2
        counts = [count for count in (rest, blocks - half - rest, half) if count > 0]
        self.chunks = []
        start = 0
        for count in counts:
            self.chunks.append((start * self.rb, count * self.rb))
            start += count

    def low_orders(self):
        device = np.arange(self.n)[:, None]
        position = np.arange(self.tp)[None, :]
        return np.where(position < self.live_t, device * self.live_t + position, NONE)

    def high_orders(self):
        pair = np.arange(self.pairs)
        first = np.where(2 * pair < self.high, self.low + pair, NONE)
        second = np.where(2 * pair < self.high - 1, LMAX - pair, NONE)
        return np.stack([first, second])


def dft_rows(plan, order, inverse):
    live = (order <= LMAX)[..., None]
    turn = (np.where(order <= LMAX, order, 0)[..., None] * np.arange(plan.lon)) % plan.lon
    angle = turn * (2.0 * math.pi / plan.lon)
    if inverse:
        scale = np.where((order == 0) | (2 * order == plan.lon), 1.0, 2.0)[..., None]
    else:
        scale = 1.0 / plan.lon
    rows = np.stack([np.cos(angle) * scale, -np.sin(angle) * scale]) * live
    return rows.astype(ml_dtypes.bfloat16)


def params(**more):
    return pltpu.CompilerParams(vmem_limit_bytes=VMEM, **more)


def call(kernel, name, operands, in_specs, out_specs, out_shape, grid, scratch=()):
    results = out_shape if isinstance(out_shape, (list, tuple)) else [out_shape]
    moved = sum(math.prod(a.shape) * a.dtype.itemsize for a in list(operands) + list(results))
    return pl.pallas_call(
        kernel,
        grid=grid,
        in_specs=in_specs,
        out_specs=out_specs,
        out_shape=out_shape,
        scratch_shapes=list(scratch),
        compiler_params=params(),
        cost_estimate=pl.CostEstimate(flops=0, transcendentals=0, bytes_accessed=4 * moved),
        name=name,
    )(*operands)


def whole(shape):
    return pl.BlockSpec(shape, lambda *_: (0,) * len(shape))


def table_kernel(m_ref, shift_ref, start_ref, cos_ref, quad_ref, live_ref, fwd_ref, inv_ref, stage):
    lanes = fwd_ref.shape[2]
    order, shift = m_ref[...], shift_ref[...]
    square = order * order
    parts = [slice(c, c + LANES) for c in range(0, start_ref.shape[1], LANES)]

    def block(index, state):
        before = state[0]
        at_row = pl.multiple_of(index * 16, 16)
        ups, backs, pasts, onsets, keeps = [], [], [], [], []
        for p in range(16):
            deg = shift + (index * 16 + p).astype(F32)
            ratio = jnp.maximum((deg * deg - square) / (4.0 * deg * deg - 1.0), 0.0)
            root = lax.rsqrt(jnp.maximum(ratio, 1e-20))
            ups.append(root)
            backs.append(before)
            before = ratio * root
            pasts.append(order < deg)
            onsets.append(jnp.where(order == deg, 1.0, 0.0))
            keeps.append(deg <= LMAX)
        after = [before]
        for c, at in enumerate(parts):
            first, second, log_scale = state[1 + 3 * c : 4 + 3 * c]
            cosine = cos_ref[:, at]
            scale = jnp.exp(log_scale)
            for p in range(16):
                current = jnp.where(
                    pasts[p], ups[p] * (cosine * first - backs[p] * second), onsets[p]
                )
                stage[c, pl.ds(p, 8, stride=16), :] = jnp.where(keeps[p], current * scale, 0.0)
                second = first
                first = current
            size = jnp.maximum(jnp.abs(first), jnp.abs(second))
            factor = jnp.where(size > 1.0, size, 1.0)
            after += [first / factor, second / factor, log_scale + jnp.log(factor)]
        for c, at in enumerate(parts):
            width = min(LANES, lanes - c * LANES)
            out = slice(c * LANES, c * LANES + width)
            for i in range(8):
                values = stage[c, i * 16 : (i + 1) * 16, :]
                fwd_ref[i, pl.ds(at_row, 16), out] = (values * quad_ref[:, at]).astype(BF)[:, :width]
                inv_ref[i, pl.ds(at_row, 16), out] = (values * live_ref[:, at]).astype(BF)[:, :width]
        return tuple(after)

    zero = jnp.zeros((8, LANES), F32)
    state = [zero]
    for at in parts:
        state += [zero, zero, start_ref[:, at]]
    lax.fori_loop(0, fwd_ref.shape[1] // 16, block, tuple(state))


def legendre_tables(orders, shift, log_start, cosines, quad, live, degrees):
    rows = cosines.shape[0]
    wide = ceil_to(rows, LANES)
    tp = orders.shape[0]

    def spread(row):
        return jnp.pad(row, (0, wide - rows))[None]

    shape = jax.ShapeDtypeStruct((tp, degrees, rows), BF)
    row_spec = whole((1, wide))
    lane_spec = pl.BlockSpec((8, LANES), lambda i: (i, 0))
    out_spec = pl.BlockSpec((8, degrees, rows), lambda i: (i, 0, 0))
    return call(
        table_kernel,
        "legendre_tables",
        [
            orders.astype(F32),
            shift.astype(F32),
            jnp.pad(log_start, ((0, 0), (0, wide - rows))),
            spread(cosines),
            spread(quad),
            spread(live),
        ],
        [
            lane_spec,
            lane_spec,
            pl.BlockSpec((8, wide), lambda i: (i, 0)),
            row_spec,
            row_spec,
            row_spec,
        ],
        [out_spec, out_spec],
        [shape, shape],
        (tp // 8,),
        [pltpu.VMEM((wide // LANES, 128, LANES), F32)],
    )


def analyse_modes(x, dft_ref):
    head, tail = x[:SPLIT], x[SPLIT:]
    right = jnp.concatenate([head, head] + [tail] * (LANES // REST), axis=0)
    return [
        lax.dot_general(
            dft_ref[k], right, (((1,), (1,)), ((), ())), preferred_element_type=F32
        )
        for k in range(2)
    ]


def analyse_low_kernel(plan, x_ref, dft_ref, *outs):
    lane = lax.broadcasted_iota(jnp.int32, (1, LANES), 1)
    part = lane // REST
    n, tp = plan.n, plan.tp
    for r in range(plan.rb):
        cosine, sine = analyse_modes(x_ref[r], dft_ref)
        main = jnp.where(lane < SPLIT, cosine[:, :LANES], sine[:, :LANES])
        for o in range(n):
            pieces = [main[o * tp : (o + 1) * tp]]
            for group in range(plan.rest_groups):
                rest = jnp.zeros((8, LANES), F32)
                for i in range(min(4, plan.tb - group * 4)):
                    first = o * tp + (group * 4 + i) * 8
                    rest = jnp.where(part == 2 * i, cosine[first : first + 8, LANES:], rest)
                    rest = jnp.where(part == 2 * i + 1, sine[first : first + 8, LANES:], rest)
                pieces.append(rest)
            outs[o][r] = jnp.concatenate(pieces, axis=0).astype(BF)


def analyse_high_kernel(plan, x_ref, dft_ref, out):
    lane = lax.broadcasted_iota(jnp.int32, (1, LANES), 1)
    even = lane // REST % 2 == 0
    for r in range(plan.rb):
        cosine, sine = analyse_modes(x_ref[r], dft_ref)
        main = jnp.where(lane < SPLIT, cosine[:, :LANES], sine[:, :LANES])
        rest = jnp.where(even, cosine[:, LANES:], sine[:, LANES:])
        out[r] = jnp.concatenate([main, rest], axis=1).astype(BF)


def analyse(plan, kernel, name, x, dft, height, lanes, count):
    shape = jax.ShapeDtypeStruct((plan.rows, height, lanes), BF)
    return call(
        functools.partial(kernel, plan),
        name,
        [x, dft],
        [pl.BlockSpec((plan.rb, plan.fpad, plan.lon), lambda i: (i, 0, 0)), whole(dft.shape)],
        [pl.BlockSpec((plan.rb, height, lanes), lambda i: (i, 0, 0))] * count,
        [shape] * count,
        (plan.rows // plan.rb,),
    )


def analyse_low(plan, x, dft):
    return list(analyse(plan, analyse_low_kernel, "analyse_low", x, dft, plan.rows1, LANES, plan.n))


def analyse_high(plan, x, dft):
    return analyse(
        plan, analyse_high_kernel, "analyse_high", x, dft, 2 * plan.pairs, 2 * LANES, 1
    )[0]


def unpack(plan, refs, store, height):
    start = 0
    for parts in refs:
        for o, ref in enumerate(parts):

            def step(r, unused, base=o * plan.rows + start, ref=ref):
                at = pl.multiple_of((base + r) * height, 8)
                store[pl.ds(at, height), :] = ref[r].astype(F32)
                return unused

            lax.fori_loop(0, ref.shape[0], step, 0)
        start += parts[0].shape[0]


def repack(plan, refs, store, height):
    start = 0
    for parts in refs:
        for o, ref in enumerate(parts):

            def step(r, unused, base=o * plan.rows + start, ref=ref):
                at = pl.multiple_of((base + r) * height, 8)
                ref[r] = store[pl.ds(at, height), :].astype(BF)
                return unused

            lax.fori_loop(0, ref.shape[0], step, 0)
        start += parts[0].shape[0]


def by_device(plan, refs):
    return [refs[i : i + plan.n] for i in range(0, len(refs), plan.n)]


def rest_row(plan, t):
    block = t // 8
    return plan.tp + 8 * (block // 4) + t % 8


def spectrum_forward_kernel(plan, *refs):
    recv, (fwd, inv, mix, gain) = refs[: plan.n], refs[plan.n : plan.n + 4]
    outs, zin, yout = refs[plan.n + 4 : -2], refs[-2], refs[-1]
    step = pl.program_id(0)

    @pl.when(step == 0)
    def _():
        unpack(plan, [recv], zin, plan.rows1)
        if plan.live_t < plan.tp:
            yout[...] = jnp.zeros_like(yout)

    for i in range(plan.step):
        t = step * plan.step + i
        z = jnp.concatenate(
            [
                zin[pl.ds(t, plan.all_rows, stride=plan.rows1), :],
                zin[pl.ds(rest_row(plan, t), plan.all_rows, stride=plan.rows1), :],
            ],
            axis=1,
        ).astype(BF)
        coeffs = jnp.dot(fwd[i], z, preferred_element_type=F32).astype(BF)
        filtered = (jnp.dot(coeffs, mix[0], preferred_element_type=F32) * gain[...]).astype(BF)
        y = lax.dot_general(
            inv[i], filtered, (((0,), (0,)), ((), ())), preferred_element_type=F32
        )
        for k in range(2):
            yout[pl.ds(k * plan.tp + t, plan.all_rows, stride=plan.rows2), :] = y[
                :, k * LANES : (k + 1) * LANES
            ]

    @pl.when(step == plan.live_t // plan.step - 1)
    def _():
        repack(plan, by_device(plan, outs), yout, plan.rows2)


def spectrum_backward_kernel(plan, count, *refs):
    recvs = refs[:count]
    fwd, inv, mix, gain = refs[count : count + 4]
    outs, zin, yout = refs[count + 4 : -2], refs[-2], refs[-1]
    step = pl.program_id(0)

    @pl.when(step == 0)
    def _():
        unpack(plan, by_device(plan, recvs), zin, plan.rows2)
        yout[...] = jnp.zeros_like(yout)

    for i in range(plan.step):
        t = step * plan.step + i
        z = jnp.concatenate(
            [
                zin[pl.ds(k * plan.tp + t, plan.all_rows, stride=plan.rows2), :]
                for k in range(2)
            ],
            axis=1,
        ).astype(BF)
        grad = (jnp.dot(inv[i], z, preferred_element_type=F32) * gain[...]).astype(BF)
        back = jnp.dot(grad, mix[0], preferred_element_type=F32).astype(BF)
        y = lax.dot_general(fwd[i], back, (((0,), (0,)), ((), ())), preferred_element_type=F32)
        yout[pl.ds(t, plan.all_rows, stride=plan.rows1), :] = y[:, :LANES]
        where = pl.ds(rest_row(plan, t), plan.all_rows, stride=plan.rows1)
        yout[where, :] = yout[where, :] + y[:, LANES:]

    @pl.when(step == plan.live_t // plan.step - 1)
    def _():
        repack(plan, [outs], yout, plan.rows1)


def spectrum_specs(plan, mix, gain):
    table = pl.BlockSpec((plan.step, plan.degrees, plan.all_rows), lambda t: (t, 0, 0))
    return [table, table, pl.BlockSpec((1,) + mix.shape[1:], lambda t: ((t * plan.step // 8) % 4, 0, 0)), whole(gain.shape)]


def spectrum_forward(plan, recv, fwd, inv, mix, gain):
    shapes = [(count, plan.rows2, LANES) for _, count in plan.chunks for _ in range(plan.n)]
    parts = call(
        functools.partial(spectrum_forward_kernel, plan),
        "spectrum_forward",
        [*recv, fwd, inv, mix, gain],
        [whole(r.shape) for r in recv] + spectrum_specs(plan, mix, gain),
        [whole(s) for s in shapes],
        [jax.ShapeDtypeStruct(s, BF) for s in shapes],
        (plan.live_t // plan.step,),
        [
            pltpu.VMEM((plan.all_rows * plan.rows1, LANES), F32),
            pltpu.VMEM((plan.all_rows * plan.rows2, LANES), F32),
        ],
    )
    return by_device(plan, parts)


def spectrum_backward(plan, recvs, fwd, inv, mix, gain):
    shape = (plan.rows, plan.rows1, LANES)
    flat = [part for parts in recvs for part in parts]
    return call(
        functools.partial(spectrum_backward_kernel, plan, len(flat)),
        "spectrum_backward",
        [*flat, fwd, inv, mix, gain],
        [whole(r.shape) for r in flat] + spectrum_specs(plan, mix, gain),
        [whole(shape)] * plan.n,
        [jax.ShapeDtypeStruct(shape, BF)] * plan.n,
        (plan.live_t // plan.step,),
        [
            pltpu.VMEM((plan.all_rows * plan.rows2, LANES), F32),
            pltpu.VMEM((plan.all_rows * plan.rows1, LANES), F32),
        ],
    )


def pair_gain(plan, pair, gain):
    row = lax.broadcasted_iota(jnp.int32, (plan.span, 1), 0)
    first, second = plan.low + pair, plan.low - 1
    first_at = pl.multiple_of(first // 8 * 8, 8)
    one = jnp.where(
        row < plan.high - pair,
        gain[first % 8, pl.ds(first_at, plan.span), :],
        gain[second % 8, pl.ds(second // 8 * 8, plan.span), :],
    )
    return jnp.concatenate([one, one], axis=1)


def load_rows(plan, refs, store, height, wide):
    start = 0
    for ref in refs:

        def step(r, unused, start=start, ref=ref):
            at = pl.multiple_of((start + r) * height, 8)
            for w in range(wide):
                store[w, pl.ds(at, height), :] = ref[r, :, w * LANES : (w + 1) * LANES].astype(F32)
            return unused

        lax.fori_loop(0, ref.shape[0], step, 0)
        start += ref.shape[0]

    def clear(r, unused):
        at = pl.multiple_of(r * height, 8)
        for w in range(wide):
            store[w, pl.ds(at, height), :] = jnp.zeros((height, LANES), F32)
        return unused

    lax.fori_loop(start, plan.half_lanes, clear, 0)


def high_partial_kernel(plan, zonal, fwd, out, zin):
    quad = pl.program_id(0)
    block = lax.broadcasted_iota(jnp.int32, (1, LANES), 1) // (2 * REST)

    @pl.when(quad == 0)
    def _():
        load_rows(plan, [zonal], zin, 2 * plan.pairs, 2)

    rest = jnp.zeros((plan.span, LANES), F32)
    for i in range(4):
        pair = quad * 4 + i
        z = jnp.concatenate(
            [
                jnp.concatenate(
                    [
                        zin[w, pl.ds(s * plan.pairs + pair, plan.half_lanes, stride=2 * plan.pairs), :]
                        for s in range(2)
                    ],
                    axis=0,
                )
                for w in range(2)
            ],
            axis=1,
        ).astype(BF)
        coeffs = jnp.dot(fwd[i], z, preferred_element_type=F32)
        out[0, i] = coeffs[:, :LANES].astype(BF)
        rest = rest + jnp.where(block == i, coeffs[:, LANES:], 0.0)
    out[0, 4] = rest.astype(BF)


def high_synthesis_kernel(plan, coeffs, inv, mix, gain, out, yout):
    quad = pl.program_id(0)
    height = 4 * plan.pairs
    for i in range(4):
        pair = quad * 4 + i
        both = jnp.concatenate([coeffs[0, i], coeffs[0, 4]], axis=1)
        filtered = jnp.dot(both, mix[i], preferred_element_type=F32) * pair_gain(plan, pair, gain)
        y = lax.dot_general(
            inv[i], filtered.astype(BF), (((0,), (0,)), ((), ())), preferred_element_type=F32
        )
        for k in range(2):
            for s in range(2):
                yout[pl.ds((2 * k + s) * plan.pairs + pair, plan.half_lanes, stride=height), :] = y[
                    s * plan.half_lanes : (s + 1) * plan.half_lanes, k * LANES : (k + 1) * LANES
                ]

    @pl.when(quad == plan.quads - 1)
    def _():
        def step(r, unused):
            out[r] = yout[pl.ds(pl.multiple_of(r * height, 8), height), :].astype(BF)
            return unused

        lax.fori_loop(0, plan.rows, step, 0)


def high_adjoint_kernel(plan, count, *refs):
    grads, (inv, mix, gain, out, zin) = refs[:count], refs[count:]
    quad = pl.program_id(0)
    height = 4 * plan.pairs

    @pl.when(quad == 0)
    def _():
        load_rows(plan, grads, zin, height, 1)

    rest = jnp.zeros((plan.span, LANES), F32)
    for i in range(4):
        pair = quad * 4 + i
        z = jnp.concatenate(
            [
                jnp.concatenate(
                    [
                        zin[0, pl.ds((2 * k + s) * plan.pairs + pair, plan.half_lanes, stride=height), :]
                        for s in range(2)
                    ],
                    axis=0,
                )
                for k in range(2)
            ],
            axis=1,
        ).astype(BF)
        grad = jnp.dot(inv[i], z, preferred_element_type=F32) * pair_gain(plan, pair, gain)
        back = jnp.dot(grad.astype(BF), mix[i], preferred_element_type=F32)
        out[0, i] = back[:, :LANES].astype(BF)
        rest = rest + back[:, LANES:]
    out[0, 4] = rest.astype(BF)


def high_zonal_kernel(plan, grads, fwd, out, yout):
    quad = pl.program_id(0)
    height = 2 * plan.pairs + 2 * plan.quad_pad
    block = lax.broadcasted_iota(jnp.int32, (1, LANES), 1) // (2 * REST)

    if plan.quad_pad > plan.quads:

        @pl.when(quad == 0)
        def _():
            yout[...] = jnp.zeros_like(yout)

    rest = jnp.zeros((LANES, LANES), F32)
    for i in range(4):
        pair = quad * 4 + i
        both = jnp.concatenate([grads[0, i], grads[0, 4]], axis=1)
        y = lax.dot_general(
            fwd[i], both, (((0,), (0,)), ((), ())), preferred_element_type=F32
        )
        for s in range(2):
            yout[pl.ds(s * plan.pairs + pair, plan.half_lanes, stride=height), :] = y[
                s * plan.half_lanes : (s + 1) * plan.half_lanes, :LANES
            ]
        rest = rest + jnp.where(block == i, y[:, LANES:], 0.0)
    for s in range(2):
        row = 2 * plan.pairs + s * plan.quad_pad + quad
        yout[pl.ds(row, plan.half_lanes, stride=height), :] = rest[
            s * plan.half_lanes : (s + 1) * plan.half_lanes
        ]

    @pl.when(quad == plan.quads - 1)
    def _():
        def step(r, unused):
            out[r] = yout[pl.ds(pl.multiple_of(r * height, 8), height), :].astype(BF)
            return unused

        lax.fori_loop(0, plan.rows, step, 0)


def high_call(plan, kernel, name, whole_in, blocked, fixed, out_shape, out_whole, scratch):
    def quad_spec(array):
        size = array.shape[0] // plan.quads
        rest = array.shape[1:]
        return pl.BlockSpec((size,) + rest, lambda q: (q,) + (0,) * len(rest))

    return call(
        kernel,
        name,
        [*whole_in, *blocked, *fixed],
        [whole(a.shape) for a in whole_in]
        + [quad_spec(a) for a in blocked]
        + [whole(a.shape) for a in fixed],
        whole(out_shape) if out_whole else quad_spec(jax.ShapeDtypeStruct(out_shape, BF)),
        jax.ShapeDtypeStruct(out_shape, BF),
        (plan.quads,),
        [pltpu.VMEM(scratch, F32)],
    )


def high_partial(plan, zonal, fwd):
    return high_call(
        plan, functools.partial(high_partial_kernel, plan), "high_partial", [zonal], [fwd], [],
        (plan.quads, 5, plan.span, LANES), False, (2, plan.half_lanes * 2 * plan.pairs, LANES),
    )


def high_synthesis(plan, coeffs, inv, mix, gain):
    return high_call(
        plan, functools.partial(high_synthesis_kernel, plan), "high_synthesis", [], [coeffs, inv],
        [mix, gain], (plan.rows, 4 * plan.pairs, LANES), True,
        (plan.half_lanes * 4 * plan.pairs, LANES),
    )


def high_adjoint(plan, grads, inv, mix, gain):
    return high_call(
        plan, functools.partial(high_adjoint_kernel, plan, len(grads)), "high_adjoint", grads, [inv],
        [mix, gain], (plan.quads, 5, plan.span, LANES), False,
        (1, plan.half_lanes * 4 * plan.pairs, LANES),
    )


def high_zonal(plan, grads, fwd):
    height = 2 * plan.pairs + 2 * plan.quad_pad
    return high_call(
        plan, functools.partial(high_zonal_kernel, plan), "high_zonal", [], [grads, fwd], [],
        (plan.rows, height, LANES), True, (plan.half_lanes * height, LANES),
    )


def predict_kernel(plan, first, live_ref, x_ref, idft_ref, enc_ref, dec_ref, *refs):
    recv, (high, pred_ref, slope_ref, left, field) = refs[: plan.n], refs[plan.n :]
    c = plan.channels
    wide = plan.n * plan.rows2
    for r in range(plan.rb):
        left[r * c : (r + 1) * c, :wide] = jnp.concatenate([ref[r] for ref in recv], axis=0).T
        left[r * c : (r + 1) * c, wide:] = high[r].T
    field[...] = jnp.dot(left[...], idft_ref[...], preferred_element_type=F32)
    base = first + pl.program_id(0) * plan.rb

    def step(r, unused):
        live = live_ref[base + r]
        x = x_ref[r]
        u = field[pl.ds(pl.multiple_of(r * c, 8), c), :]
        hidden = (jnp.dot(enc_ref[...], x, preferred_element_type=F32) * live).astype(BF)
        phi = 0.5 + 0.5 * lax.erf(u * (1.0 / math.sqrt(2.0)))
        slope = phi + u * jnp.exp(-0.5 * u * u) * (1.0 / math.sqrt(2.0 * math.pi))
        slope_ref[r] = slope.astype(BF)
        block = ((u * phi + hidden.astype(F32)) * live).astype(BF)
        decoded = jnp.dot(dec_ref[...], block, preferred_element_type=F32)
        pred_ref[r] = ((x.astype(F32) + decoded) * live).astype(BF)
        return unused

    lax.fori_loop(0, plan.rb, step, 0)


def predict(plan, chunk, live, x, idft, enc_t, dec_t, recv, high):
    first, count = chunk
    skip = first // plan.rb
    shape = (count, plan.fpad, plan.lon)
    slope_shape = (count, plan.channels, plan.lon)
    return call(
        functools.partial(predict_kernel, plan, first),
        "predict",
        [live, x, idft, enc_t, dec_t, *recv, high],
        [
            pl.BlockSpec(memory_space=pltpu.SMEM),
            pl.BlockSpec((plan.rb,) + shape[1:], lambda i: (i + skip, 0, 0)),
            whole(idft.shape),
            whole(enc_t.shape),
            whole(dec_t.shape),
        ]
        + [pl.BlockSpec((plan.rb, plan.rows2, LANES), lambda i: (i, 0, 0))] * plan.n
        + [pl.BlockSpec((plan.rb,) + high.shape[1:], lambda i: (i + skip, 0, 0))],
        [
            pl.BlockSpec((plan.rb,) + shape[1:], lambda i: (i, 0, 0)),
            pl.BlockSpec((plan.rb,) + slope_shape[1:], lambda i: (i, 0, 0)),
        ],
        [jax.ShapeDtypeStruct(shape, BF), jax.ShapeDtypeStruct(slope_shape, BF)],
        (count // plan.rb,),
        [
            pltpu.VMEM((plan.rb * plan.channels, idft.shape[0]), BF),
            pltpu.VMEM((plan.rb * plan.channels, plan.lon), F32),
        ],
    )


def score_kernel(plan, first, members, area_ref, own_ref, all_ref, obs_ref, slope_ref, idft_ref, dec_ref, *refs):
    grad_ref, outs, (out_high, right) = refs[0], refs[1 : 1 + plan.n], refs[1 + plan.n :]
    c = plan.channels
    base = first + pl.program_id(0) * plan.rb

    def step(r, unused):
        area = area_ref[base + r]
        own = own_ref[r].astype(F32)
        gap = own - obs_ref[r].astype(F32)
        total = gap * lax.rsqrt(jnp.sum(gap * gap, axis=0, keepdims=True) + EPSILON)
        for e in range(members):
            gap = own - all_ref[e, r].astype(F32)
            near = lax.rsqrt(jnp.sum(gap * gap, axis=0, keepdims=True) + EPSILON)
            total = total - gap * (near * (1.0 / members))
        grad = (total * area).astype(BF)
        grad_ref[r] = grad
        block = jnp.dot(dec_ref[...], grad, preferred_element_type=F32)
        right[pl.ds(pl.multiple_of(r * c, 16), c), :] = (
            block * slope_ref[r].astype(F32)
        ).astype(BF)
        return unused

    lax.fori_loop(0, plan.rb, step, 0)
    wide = plan.n * plan.rows2

    def modes(first, last):
        return lax.dot_general(
            idft_ref[first:last, :],
            right[...],
            (((1,), (1,)), ((), ())),
            preferred_element_type=F32,
        ).astype(BF)

    low, high = modes(0, wide), modes(wide, idft_ref.shape[0])
    for r in range(plan.rb):
        for o in range(plan.n):
            outs[o][r] = low[o * plan.rows2 : (o + 1) * plan.rows2, r * c : (r + 1) * c]
        out_high[r] = high[:, r * c : (r + 1) * c]


def score(plan, chunk, area, own, everyone, observed, slope, idft, dec):
    first, count = chunk
    skip = first // plan.rb
    members = everyone.shape[0]
    cell = (plan.rb, plan.fpad, plan.lon)
    out_shape = (count, plan.rows2, LANES)
    high = 4 * plan.pairs
    here = pl.BlockSpec(cell, lambda i: (i, 0, 0))
    grad, *outs = call(
        functools.partial(score_kernel, plan, first, members),
        "score",
        [area, own, everyone, observed, slope, idft, dec],
        [
            pl.BlockSpec(memory_space=pltpu.SMEM),
            here,
            pl.BlockSpec((members,) + cell, lambda i: (0, i, 0, 0)),
            pl.BlockSpec(cell, lambda i: (i + skip, 0, 0)),
            pl.BlockSpec((plan.rb, plan.channels, plan.lon), lambda i: (i, 0, 0)),
            whole(idft.shape),
            whole(dec.shape),
        ],
        [here]
        + [pl.BlockSpec((plan.rb, plan.rows2, LANES), lambda i: (i, 0, 0))] * plan.n
        + [pl.BlockSpec((plan.rb, high, LANES), lambda i: (i, 0, 0))],
        [jax.ShapeDtypeStruct((count,) + cell[1:], BF)]
        + [jax.ShapeDtypeStruct(out_shape, BF)] * plan.n
        + [jax.ShapeDtypeStruct((count, high, LANES), BF)],
        (count // plan.rb,),
        [pltpu.VMEM((plan.rb * plan.channels, plan.lon), BF)],
    )
    return grad, outs[:-1], outs[-1]


def finish_kernel(
    plan, live_ref, grad_ref, main_ref, rest_ref, through_ref, *refs
):
    n, tp, tb = plan.n, plan.tp, plan.tb
    recv, (high_ref, out_ref, left, small, field, field_small) = refs[:n], refs[n:]
    wide, tall, quads = n * tp, 2 * plan.pairs, 2 * plan.quad_pad
    for r in range(plan.rb):
        piece = [ref[r].astype(F32) for ref in recv]
        high = high_ref[r].astype(F32)
        mains = [
            (0, jnp.concatenate([p[:tp] for p in piece], axis=0).T),
            (2 * wide, high[:tall].T),
        ]
        for first, main in mains:
            size = main.shape[1]
            for k in range(2):
                at = first + k * size
                left[r * SPLIT : (r + 1) * SPLIT, at : at + size] = main[
                    k * SPLIT : (k + 1) * SPLIT
                ].astype(BF)
        at = 0
        rests = [
            (
                jnp.concatenate([p[tp + 8 * group : tp + 8 * (group + 1)] for p in piece], axis=0),
                min(4, tb - 4 * group),
            )
            for group in range(plan.rest_groups)
        ] + [(high[tall:], 4)]
        for rest, blocks in rests:
            turned = rest.T.astype(BF)
            for part in range(2 * blocks):
                small[r * REST : (r + 1) * REST, at : at + turned.shape[1]] = turned[
                    part * REST : (part + 1) * REST
                ]
                at += turned.shape[1]
    field[...] = jnp.dot(left[...], main_ref[...], preferred_element_type=F32)
    field_small[...] = jnp.dot(small[...], rest_ref[...], preferred_element_type=F32)
    base = pl.program_id(0) * plan.rb

    def step(r, unused):
        live = live_ref[base + r]
        grad = grad_ref[r]
        through = jnp.dot(through_ref[...], grad, preferred_element_type=F32)
        spectral = jnp.concatenate(
            [
                field[pl.ds(pl.multiple_of(r * SPLIT, 8), SPLIT), :],
                field_small[pl.ds(pl.multiple_of(r * REST, 8), REST), :],
            ],
            axis=0,
        )
        out_ref[r] = ((grad.astype(F32) + through + spectral) * live).astype(BF)
        return unused

    lax.fori_loop(0, plan.rb, step, 0)


def finish(plan, live, grad, main, rest, through, recv, high):
    cell = (plan.rb, plan.fpad, plan.lon)
    here = pl.BlockSpec(cell, lambda i: (i, 0, 0))
    return call(
        functools.partial(finish_kernel, plan),
        "finish",
        [live, grad, main, rest, through, *recv, high],
        [
            pl.BlockSpec(memory_space=pltpu.SMEM),
            here,
            whole(main.shape),
            whole(rest.shape),
            whole(through.shape),
        ]
        + [pl.BlockSpec((plan.rb, plan.rows1, LANES), lambda i: (i, 0, 0))] * plan.n
        + [pl.BlockSpec((plan.rb,) + high.shape[1:], lambda i: (i, 0, 0))],
        here,
        jax.ShapeDtypeStruct((plan.rows, plan.fpad, plan.lon), BF),
        (plan.rows // plan.rb,),
        [
            pltpu.VMEM((plan.rb * SPLIT, main.shape[0]), BF),
            pltpu.VMEM((plan.rb * REST, rest.shape[0]), BF),
            pltpu.VMEM((plan.rb * SPLIT, plan.lon), F32),
            pltpu.VMEM((plan.rb * REST, plan.lon), F32),
        ],
    )


def row_geometry(band_rows, band_len, lat_count):
    band_count = band_rows.shape[0]
    row_index = jnp.arange(band_count * band_len, dtype=jnp.int32)
    row_owner = row_index // band_len
    offset = row_index - row_owner * band_len
    starts = jnp.cumsum(band_rows) - band_rows
    owner_hot = (row_owner[:, None] == jnp.arange(band_count, dtype=jnp.int32)[None, :]).astype(
        jnp.int32
    )
    first_lat = jnp.sum(owner_hot * starts[None, :], axis=1)
    length = jnp.sum(owner_hot * band_rows[None, :], axis=1)
    live_rows = offset < length
    latitude = jnp.minimum(first_lat + offset, lat_count - 1)
    colatitude = latitude.astype(F32) * (math.pi / (lat_count - 1))
    return (live_rows.astype(F32), jnp.cos(colatitude), jnp.sin(colatitude))


def log_diagonal(order):
    index = np.arange(1, LMAX + 1, dtype=np.float64)
    sums = np.concatenate([[0.0], np.cumsum(0.5 * np.log((2 * index + 1) / (2 * index)))])
    return (0.5 * math.log(0.5) + sums[np.minimum(order, LMAX)]).astype(np.float32)


def field_weights(plan, weight):
    select = np.zeros((4, 2 * LANES, plan.fields), np.float32)
    side = np.zeros((4, 2 * LANES, 2), np.float32)
    for b in range(4):
        for k in range(2):
            for f in range(plan.fields):
                first = k * SPLIT + f if f < SPLIT else LANES + (2 * b + k) * REST + f - SPLIT
                select[b, first, f] = 1.0
                side[b, first, k] = 1.0
    spread = jnp.einsum("blf,fc->blc", select, weight, precision=lax.Precision.HIGHEST)
    both = jnp.concatenate([spread, spread], axis=2)
    return (both * np.repeat(side, plan.channels, axis=2)).astype(BF)


def on_device(
    states, observed, band_rows, encoder_weight, mixing_weight, degree_gain, decoder_weight
):
    space = lax.axis_size("space")
    me = lax.axis_index("space")
    fields, band, lon = observed.shape
    channels = encoder_weight.shape[1]
    plan = Plan(space, band, fields, lon, channels, degree_gain.shape[0])
    live, cosines, sines = row_geometry(band_rows, band, NLAT)
    quad = live * sines * (math.pi / (NLAT - 1))
    log_sines = jnp.log(jnp.maximum(sines, 1e-30))
    live_own = lax.dynamic_slice_in_dim(live, me * band, band)
    area = 8.0 * lax.dynamic_slice_in_dim(sines, me * band, band) * live_own

    pad = plan.fpad - fields
    rows = jnp.pad(jnp.transpose(states[0], (1, 0, 2)), ((0, 0), (0, pad), (0, 0)))
    truth = jnp.pad(jnp.transpose(observed, (1, 0, 2)), ((0, 0), (0, pad), (0, 0)))

    enc_f = encoder_weight.astype(F32)
    exact = lax.Precision.HIGHEST
    through_mix = jnp.dot(enc_f, mixing_weight.astype(F32), precision=exact)
    mix = field_weights(plan, through_mix)
    mix_back = jnp.transpose(mix, (0, 2, 1))
    gain = jnp.concatenate([degree_gain, degree_gain], axis=1)
    enc_t = jnp.pad(encoder_weight.T, ((0, 0), (0, pad)))
    dec_t = jnp.pad(decoder_weight.T, ((0, pad), (0, 0)))
    dec = jnp.pad(decoder_weight, ((0, 0), (0, pad)))
    through = jnp.pad(
        jnp.dot(enc_f, decoder_weight.astype(F32), precision=exact), ((0, pad), (0, pad))
    ).astype(BF)

    n, tp, tb = plan.n, plan.tp, plan.tb
    low, high = plan.low_orders(), plan.high_orders()
    low_f, high_f = dft_rows(plan, low, False), dft_rows(plan, high, False)
    low_i, high_i = dft_rows(plan, low, True), dft_rows(plan, high, True)

    def from_here(table):
        table = jnp.asarray(table)
        return lax.dynamic_slice_in_dim(jnp.concatenate([table, table]), me, n)

    low_sums = from_here(low_f.transpose(1, 2, 0, 3))
    low_sums = jnp.transpose(low_sums, (2, 0, 1, 3))
    dft_low = low_sums.reshape(2, n * tp, lon)
    dft_high = jnp.asarray(high_f.reshape(2, 2 * plan.pairs, lon))
    idft = jnp.concatenate(
        [
            from_here(low_i.transpose(1, 0, 2, 3)).reshape(n * 2 * tp, lon),
            jnp.asarray(high_i.reshape(4 * plan.pairs, lon)),
        ]
    )
    dft_main = jnp.concatenate(
        [low_sums.reshape(2 * n * tp, lon), jnp.asarray(high_f.reshape(4 * plan.pairs, lon))]
    )
    low_rest = jnp.transpose(low_sums.reshape(2, n, tb, 8, lon), (2, 0, 1, 3, 4))
    quads = np.zeros((2, 2, plan.quad_pad, 4, lon), low_f.dtype)
    quads[:, :, : plan.quads] = high_f.reshape(2, 2, plan.quads, 4, lon)
    dft_rest = jnp.concatenate(
        [low_rest.reshape(-1, lon), jnp.asarray(quads.transpose(3, 0, 1, 2, 4).reshape(-1, lon))]
    )

    def outward(block):
        return jnp.transpose(block[:, :fields], (1, 0, 2))[None]

    def exchange(parts):
        got = [parts[0]] + [None] * (n - 1)
        for s in sorted(range(1, n), key=lambda s: abs(2 * s - n)):
            got[n - s] = lax.ppermute(parts[s], "space", [(i, (i + s) % n) for i in range(n)])
        return got

    sent = analyse_low(plan, rows, dft_low)
    rows_next, sent[0] = lax.optimization_barrier((rows, sent[0]))
    recv = exchange(sent)
    zonal_high = analyse_high(plan, rows_next, dft_high)

    half = plan.half_lanes

    def side(value):
        value = jnp.pad(value, (0, half - band))
        return jnp.concatenate([value, value])

    def sides(pair_values):
        return jnp.asarray(np.repeat(pair_values.T, half, axis=1))

    own = [
        side(lax.dynamic_slice_in_dim(v, me * band, band)) for v in (cosines, quad, live, log_sines)
    ]
    shift = np.stack([plan.low + np.arange(plan.pairs), np.full(plan.pairs, plan.low - 1)])
    start = sides(log_diagonal(high)) + sides(high.astype(np.float32)) * own[3][None, :]
    high_fwd, high_inv = legendre_tables(
        sides(high), sides(shift), start, own[0], own[1], own[2], plan.span
    )
    high_coeffs = lax.psum(high_partial(plan, zonal_high, high_fwd), "space")

    orders = lax.dynamic_index_in_dim(jnp.asarray(low, jnp.int32), me, keepdims=False)
    diagonal = lax.dynamic_index_in_dim(jnp.asarray(log_diagonal(low)), me, keepdims=False)
    orders_wide = jnp.broadcast_to(orders[:, None], (tp, LANES))
    ordered = [from_here(v.reshape(n, band)).reshape(-1) for v in (cosines, quad, live, log_sines)]
    start = diagonal[:, None] + orders.astype(F32)[:, None] * ordered[3][None, :]
    low_fwd, low_inv = legendre_tables(
        orders_wide, jnp.zeros_like(orders_wide), start, *ordered[:3], plan.degrees
    )

    spectrum = spectrum_forward(plan, recv, low_fwd, low_inv, mix, gain)
    synth = [exchange(part) for part in spectrum]
    reach = ceil_to(plan.low + plan.pairs + plan.span, 8)
    longer = jnp.pad(degree_gain, ((0, reach + 8 - degree_gain.shape[0]), (0, 0)))
    gain_long = jnp.stack([longer[s : s + reach] for s in range(8)])

    def after(value, other):
        return lax.optimization_barrier((value, other))

    synth_high = high_synthesis(plan, high_coeffs, high_inv, mix, gain_long)

    predictions, grads, returned, returned_high = [], [], [], []
    gathered = []
    for i, chunk in enumerate(plan.chunks):
        live_now = live_own
        if i == 1:
            live_now, truth = after(live_own, truth)
        pred, slope = predict(
            plan, chunk, live_now, rows, idft, enc_t, dec_t, synth[i], synth_high
        )
        predictions.append(pred)
        gathered.append((lax.all_gather(pred[None], "member", axis=0, tiled=True), slope))
    for i, chunk in enumerate(plan.chunks):
        pred, (everyone, slope) = predictions[i], gathered[i]
        if i:
            pred, returned[i - 1] = after(pred, returned[i - 1])
        grad, out, out_high = score(plan, chunk, area, pred, everyone, truth, slope, idft, dec)
        grads.append(grad)
        returned_high.append(out_high)
        if i == len(plan.chunks) - 1:
            high_grads = high_adjoint(plan, returned_high, high_inv, mix_back, gain_long)
            out, high_grads = after(out, high_grads)
            high_grads = lax.psum(high_grads, "space")
        returned.append(exchange(out))

    parts = spectrum_backward(plan, returned, low_fwd, low_inv, mix_back, gain)
    zonal_grad = high_zonal(plan, high_grads, high_fwd)
    grads = jnp.concatenate(grads)
    predictions = outward(jnp.concatenate(predictions))
    ends, (zonal_grad, grads, predictions) = after(
        [parts[1], parts[n - 1]], (zonal_grad, grads, predictions)
    )
    parts = [parts[0], ends[0], *parts[2 : n - 1], ends[1]]
    last = exchange(parts)
    state_grad = finish(
        plan, live_own, grads, dft_main, dft_rest, through, last, zonal_grad
    )

    return (predictions, outward(state_grad))


def solution(mesh):
    in_specs = (P("member", None, "space", None), P(None, "space", None), P(), P(), P(), P(), P())
    out_specs = (P("member", None, "space", None), P("member", None, "space", None))
    return jax.shard_map(
        on_device, mesh=mesh, in_specs=in_specs, out_specs=out_specs, check_vma=False
    )
```
